128 devices in a mesh: dom: 32 (over z, y, core), node: 4 (over x).
Axes of the slice: x: 4, y: 4, z: 4, core: 2. Of those that a mesh axis runs over, the one named last changes fastest.
Arguments:
- features: bfloat16 [65536, 256], P(('dom', 'node')), may hold values from -14 to 14
- w_query: bfloat16 [256, 256], replicated, may hold values from -0.375 to 0.375
- w_key: bfloat16 [256, 256], replicated, may hold values from -0.375 to 0.375
- w_value: bfloat16 [256, 256], replicated, may hold values from -0.375 to 0.375
- w_out: bfloat16 [256, 256], replicated, may hold values from -0.375 to 0.375
- w_expand: bfloat16 [256, 1024], replicated, may hold values from -0.375 to 0.375
- w_reduce: bfloat16 [1024, 256], replicated, may hold values from -0.1875 to 0.1875
- gain_attn: float32 [256], replicated, may hold values from 0.25 to 1.75
- gain_ffn: float32 [256], replicated, may hold values from 0.25 to 1.75
- tile_mask: int32 [65536, 7, 128], P(('dom', 'node')), may hold values 0 or 1
- local_block: int32 [512, 2], P(('dom', 'node')), may hold values from 0 to 15
- remote_slot: int32 [512, 4], P(('dom', 'node')), may hold values from 0 to 63, as said below
- remote_block: int32 [32, 4, 64], P('dom', 'node'), may hold values from 0 to 15
- d_out: bfloat16 [65536, 256], P(('dom', 'node')), may hold values from -6 to 6
Outputs:
- output: bfloat16 [65536, 256], P(('dom', 'node'))
- d_x: bfloat16 [65536, 256], P(('dom', 'node'))
- grad_query: float32 [256, 256], replicated
- grad_key: float32 [256, 256], replicated
- grad_value: float32 [256, 256], replicated
- grad_out: float32 [256, 256], replicated
- grad_expand: float32 [256, 1024], replicated
- grad_reduce: float32 [1024, 256], replicated
The draws below stay inside these ranges and needn't reach their ends.
Inputs may be any that keep to these rules, and one draw needn't show every extreme that they name: `remote_slot`: within the rows of one device the slots are distinct; slot s asks partition s // 2; on every device some partition is asked for exactly 2 blocks.
All inputs are finite; a program needn't handle non-finite values. No bound on the sum of `tile_mask` on one device may be relied on, other than what follows from the above.
Results may differ from the reference program's by a relative error of at most 0.013.
The reference program's roundings to bfloat16 on the way count: a program that leaves them out, or rounds other values in their place, can miss the bound.
Values may be sent and summed in bfloat16 or wider, within the bound.
A program may use at most 192 MiB of HBM per device.

```python
import math
import jax
import jax.numpy as jnp
from jax import lax

D = 256
HEADS = 8
FF = 1024
BLK = 128
LOCAL_TILES = 2
REMOTE_TILES = 4
TILES = 7
ROWS_DEV = 4
PART_BLOCKS = 16
CAP = 2
NODES = 65536
NBLK = 512
N_DOM = 32
N_NODE = 4


def draw_features(key, part):
    key = jax.random.fold_in(key, 5)
    return jnp.clip(jax.random.normal(key, (NODES, D), jnp.float32), -4.0, 4.0).astype(jnp.bfloat16)


def draw_remote_slot(key, part):
    key = jax.random.fold_in(key, 11)
    slot_total = N_DOM * CAP
    wanted_count = ROWS_DEV * REMOTE_TILES

    def one_device(device_key):
        perm_key, first_key, order_key = jax.random.split(device_key, 3)
        slots = jax.random.permutation(perm_key, slot_total).astype(jnp.int32)
        first_peer = jax.random.randint(first_key, (), 0, N_DOM)
        ranking = jnp.where(slots // CAP == first_peer, 0, slot_total) + jnp.arange(slot_total, dtype=jnp.int32)
        chosen = slots[jnp.argsort(ranking, stable=True)][:wanted_count]
        chosen = chosen[jax.random.permutation(order_key, wanted_count)]
        return chosen.reshape(ROWS_DEV, REMOTE_TILES)
    device_keys = jax.random.split(key, N_DOM * N_NODE)
    return jax.vmap(one_device)(device_keys).reshape(NBLK, REMOTE_TILES).astype(jnp.int32)


def plant(entries, own_key, least, top_value):
    index_at = [jax.random.randint(jax.random.fold_in(own_key, axis), (), 0, length) for axis, length in enumerate(entries.shape)]
    longest = entries.shape.index(max(entries.shape))
    neighbour = index_at[:longest] + [(index_at[longest] + 1) % entries.shape[longest]] + index_at[longest + 1:]
    return entries.at[tuple(index_at)].set(least).at[tuple(neighbour)].set(top_value)


def level_of(key, shape, cuts, low, top_value):
    level, own = 1.0, jax.random.fold_in(key, 6)
    for position, parts in cuts:
        heights = jnp.exp(jax.random.uniform(jax.random.fold_in(own, position), (parts,), jnp.float32, low / len(cuts), top_value / len(cuts)))
        level = level * jnp.repeat(heights, shape[position] // parts).reshape([-1 if axis == position else 1 for axis in range(len(shape))])
    return level


def normal_values(key, shape, scale, most, cuts=(), kind=jnp.bfloat16):
    drawn = scale * jax.random.normal(key, shape, jnp.float32)
    if cuts:
        drawn = drawn * level_of(key, shape, cuts, -0.22, 0.18)
    return jnp.clip(drawn, -most, most).astype(kind)


def setup_inputs(seed: int = 0) -> dict:
    arg_keys = jax.random.split(jax.random.key(seed), 15)
    features = draw_features(jax.random.fold_in(arg_keys[14], 71), 0)
    w_query = normal_values(arg_keys[1], (D, D), D ** -0.5, 0.375)
    w_key = normal_values(arg_keys[2], (D, D), D ** -0.5, 0.375)
    w_value = normal_values(arg_keys[3], (D, D), D ** -0.5, 0.375)
    w_out = normal_values(arg_keys[4], (D, D), D ** -0.5, 0.375)
    w_expand = normal_values(arg_keys[5], (D, FF), D ** -0.5, 0.375)
    w_reduce = normal_values(arg_keys[6], (FF, D), FF ** -0.5, 0.1875)
    gain_attn = jnp.clip(1.0 + 0.15 * jax.random.normal(arg_keys[7], (D,), jnp.float32), 0.25, 1.75)
    gain_ffn = jnp.clip(1.0 + 0.15 * jax.random.normal(arg_keys[8], (D,), jnp.float32), 0.25, 1.75)
    tile_mask = plant((jax.random.randint(arg_keys[9], (NODES, TILES, BLK), 0, 2) < 1).astype(jnp.int32), jax.random.fold_in(arg_keys[9], 1), 0, 1)
    local_block = plant(jax.random.randint(arg_keys[10], (NBLK, LOCAL_TILES), 0, PART_BLOCKS), jax.random.fold_in(arg_keys[10], 1), 0, PART_BLOCKS - 1).astype(jnp.int32)
    remote_slot = draw_remote_slot(jax.random.fold_in(arg_keys[14], 71), 0)
    remote_block = plant(jax.random.randint(arg_keys[12], (N_DOM, N_NODE, N_DOM * CAP), 0, PART_BLOCKS), jax.random.fold_in(arg_keys[12], 1), 0, PART_BLOCKS - 1).astype(jnp.int32)
    d_out = normal_values(arg_keys[13], (NODES, D), 1.0, 6.0, ((0, 128),))
    return {"features": features, "w_query": w_query, "w_key": w_key, "w_value": w_value, "w_out": w_out, "w_expand": w_expand, "w_reduce": w_reduce, "gain_attn": gain_attn, "gain_ffn": gain_ffn, "tile_mask": tile_mask, "local_block": local_block, "remote_slot": remote_slot, "remote_block": remote_block, "d_out": d_out}


EPSILON = 1e-05

def layer_norm(values, gain):
    center = values - lax.optimization_barrier(jnp.mean(values, -1, keepdims=True))
    spread = lax.optimization_barrier(jnp.mean(center * center, -1, keepdims=True))
    return center * lax.rsqrt(spread + EPSILON) * gain

def gelu_tanh(values):
    return jax.nn.gelu(values, approximate=True)

def split_heads(query_rows, pair_rows):
    groups, block_len, width = query_rows.shape
    head_dim = width // HEADS
    query_heads = query_rows.reshape(groups, block_len, HEADS, head_dim).astype(jnp.float32)
    key_heads = pair_rows[..., :width].reshape(groups, -1, HEADS, head_dim).astype(jnp.float32)
    value_heads = pair_rows[..., width:].reshape(groups, -1, HEADS, head_dim).astype(jnp.float32)
    return (query_heads, key_heads, value_heads, 1.0 / math.sqrt(head_dim))

def attend(query_rows, pair_rows, allowed):
    groups, block_len, width = query_rows.shape
    query_heads, key_heads, value_heads, score_scale = split_heads(query_rows, pair_rows)
    scores = jnp.einsum('gqhd,gkhd->ghqk', query_heads, key_heads) * score_scale
    visible = allowed[:, None]
    row_max = lax.optimization_barrier(jnp.max(jnp.where(visible, scores, -jnp.inf), -1, keepdims=True))
    weights_raw = jnp.where(visible, jnp.exp(scores - row_max), 0.0)
    row_total = lax.optimization_barrier(jnp.sum(weights_raw, -1, keepdims=True))
    probs = weights_raw / row_total
    probs_low = probs.astype(jnp.bfloat16)
    mixed = jnp.einsum('ghqk,gkhd->gqhd', probs_low.astype(jnp.float32), value_heads)
    return (mixed.astype(jnp.bfloat16).reshape(groups, block_len, width), probs, probs_low)

def attend_back(query_rows, pair_rows, probs, probs_low, d_mixed):
    groups, block_len, width = query_rows.shape
    query_heads, key_heads, value_heads, score_scale = split_heads(query_rows, pair_rows)
    d_heads = d_mixed.reshape(groups, block_len, HEADS, -1).astype(jnp.float32)
    d_probs = jnp.einsum('gqhd,gkhd->ghqk', d_heads, value_heads)
    d_values = jnp.einsum('ghqk,gqhd->gkhd', probs_low.astype(jnp.float32), d_heads)
    inner = lax.optimization_barrier(jnp.sum(probs * d_probs, -1, keepdims=True))
    d_scores = (probs * (d_probs - inner) * score_scale).astype(jnp.bfloat16).astype(jnp.float32)
    d_query = jnp.einsum('ghqk,gkhd->gqhd', d_scores, key_heads).reshape(groups, block_len, width)
    d_keys = jnp.einsum('ghqk,gqhd->gkhd', d_scores, query_heads)
    d_pairs = jnp.concatenate([d_keys.reshape(groups, -1, width), d_values.reshape(groups, -1, width)], -1)
    return (d_query, d_pairs)

def feed_tail(features, mixed_rows, w_out, w_expand, w_reduce, gain_attn, gain_ffn, d_out):
    residual = features.astype(jnp.float32) + jnp.dot(mixed_rows, w_out, preferred_element_type=jnp.float32)
    first_norm, first_back = jax.vjp(lambda values: layer_norm(values, gain_attn), residual)
    first_low = first_norm.astype(jnp.bfloat16)
    pre_act = jnp.dot(first_low, w_expand, preferred_element_type=jnp.float32)
    activation, gelu_back = jax.vjp(gelu_tanh, pre_act)
    act_low = activation.astype(jnp.bfloat16)
    second_in = first_low.astype(jnp.float32) + jnp.dot(act_low, w_reduce, preferred_element_type=jnp.float32)
    result, second_back = jax.vjp(lambda values: layer_norm(values, gain_ffn), second_in)
    output = result.astype(jnp.bfloat16)
    d_second = second_back(d_out.astype(jnp.float32))[0]
    d_second_low = d_second.astype(jnp.bfloat16)
    reduce_sum = jnp.dot(act_low.T, d_second_low, preferred_element_type=jnp.float32)
    d_pre = gelu_back(jnp.dot(d_second_low, w_reduce.T, preferred_element_type=jnp.float32))[0]
    d_pre_low = d_pre.astype(jnp.bfloat16)
    expand_sum = jnp.dot(first_low.T, d_pre_low, preferred_element_type=jnp.float32)
    d_first = d_second + jnp.dot(d_pre_low, w_expand.T, preferred_element_type=jnp.float32)
    d_resid = first_back(d_first)[0]
    d_resid_low = d_resid.astype(jnp.bfloat16)
    out_sum = jnp.dot(mixed_rows.T, d_resid_low, preferred_element_type=jnp.float32)
    d_mixed = jnp.dot(d_resid_low, w_out.T, preferred_element_type=jnp.float32).astype(jnp.bfloat16)
    return (output, d_resid, d_mixed, out_sum, expand_sum, reduce_sum)

def reference(features, w_query, w_key, w_value, w_out, w_expand, w_reduce, gain_attn, gain_ffn, tile_mask, local_block, remote_slot, remote_block, d_out):
    w_pair = jnp.concatenate([w_key, w_value], 1)
    queries = jnp.dot(features, w_query, preferred_element_type=jnp.float32).astype(jnp.bfloat16)
    pair_blocks = jnp.dot(features, w_pair, preferred_element_type=jnp.float32).astype(jnp.bfloat16).reshape(NBLK, BLK, 2 * D)
    block_ids = jnp.arange(NBLK, dtype=jnp.int32)
    device_ids = block_ids // ROWS_DEV
    part_ids = device_ids // N_NODE
    local_ids = part_ids[:, None] * PART_BLOCKS + local_block
    slot_table = remote_block.reshape(N_DOM * N_NODE, N_DOM * CAP)
    asked = slot_table[device_ids[:, None], remote_slot]
    remote_ids = remote_slot // CAP * PART_BLOCKS + asked
    key_blocks = jnp.concatenate([block_ids[:, None], local_ids, remote_ids], 1).astype(jnp.int32)
    diagonal = (jnp.arange(BLK)[:, None] == jnp.arange(BLK)[None, :]).astype(jnp.int32)
    mask_blocks = tile_mask.reshape(NBLK, BLK, TILES, BLK)
    own_part = jnp.maximum(mask_blocks[:, :, 0:1, :], diagonal[None, :, None, :])
    mask_blocks = jnp.concatenate([own_part, mask_blocks[:, :, 1:, :]], 2)
    group_size = 4 if NBLK % 4 == 0 else 1
    group_count = NBLK // group_size
    query_groups = queries.reshape(group_count, group_size, BLK, D)
    block_groups = key_blocks.reshape(group_count, group_size, TILES)
    keep_groups = (mask_blocks > 0).reshape(group_count, group_size, BLK, TILES * BLK)

    def forward_group(items):
        query_part, chosen, keep_part = items
        pair_rows = pair_blocks[chosen].reshape(group_size, TILES * BLK, 2 * D)
        return attend(query_part, pair_rows, keep_part)[0]
    mixed_rows = lax.map(forward_group, (query_groups, block_groups, keep_groups)).reshape(NODES, D)
    output, d_resid, d_mixed, out_sum, expand_sum, reduce_sum = feed_tail(features, mixed_rows, w_out, w_expand, w_reduce, gain_attn, gain_ffn, d_out)
    device_count = N_DOM * N_NODE
    slot_total = N_DOM * CAP
    near_local = jnp.concatenate([(block_ids % PART_BLOCKS)[:, None], local_block], 1).astype(jnp.int32)
    slot_part = jnp.arange(slot_total, dtype=jnp.int32) // CAP * PART_BLOCKS
    slot_global = (slot_part[None, :] + slot_table).astype(jnp.int32)
    part_base = (jnp.arange(device_count, dtype=jnp.int32) // N_NODE * PART_BLOCKS).astype(jnp.int32)
    dev_queries = queries.reshape(device_count, ROWS_DEV, BLK, D)
    dev_blocks = key_blocks.reshape(device_count, ROWS_DEV, TILES)
    dev_keep = (mask_blocks > 0).reshape(device_count, ROWS_DEV, BLK, TILES * BLK)
    dev_grads = d_mixed.reshape(device_count, ROWS_DEV, BLK, D)
    dev_near = near_local.reshape(device_count, ROWS_DEV, 1 + LOCAL_TILES)
    dev_far = remote_slot.reshape(device_count, ROWS_DEV, REMOTE_TILES).astype(jnp.int32)
    near_span = jnp.arange(PART_BLOCKS, dtype=jnp.int32)

    def backward_device(accum, items):
        query_part, chosen, keep_part, grad_part, near_sel, far_sel, base, slot_ids = items
        pair_rows = pair_blocks[chosen].reshape(ROWS_DEV, TILES * BLK, 2 * D)
        unused, probs, probs_low = attend(query_part, pair_rows, keep_part)
        d_query, d_pairs = attend_back(query_part, pair_rows, probs, probs_low, grad_part)
        d_pairs = d_pairs.reshape(ROWS_DEV, TILES, BLK, 2 * D)
        near_acc = jnp.zeros((PART_BLOCKS, BLK, 2 * D), jnp.float32).at[near_sel.reshape(-1)].add(d_pairs[:, :1 + LOCAL_TILES].reshape(-1, BLK, 2 * D))
        far_acc = jnp.zeros((slot_total, BLK, 2 * D), jnp.float32).at[far_sel.reshape(-1)].add(d_pairs[:, 1 + LOCAL_TILES:].reshape(-1, BLK, 2 * D))
        near_low = lax.optimization_barrier(near_acc.astype(jnp.bfloat16))
        far_low = lax.optimization_barrier(far_acc.astype(jnp.bfloat16))
        accum = accum.at[base + near_span].add(near_low.astype(jnp.float32))
        accum = accum.at[slot_ids].add(far_low.astype(jnp.float32))
        return (accum, d_query)
    start = jnp.zeros((NBLK, BLK, 2 * D), jnp.float32)
    pair_grads, query_grads = lax.scan(backward_device, start, (dev_queries, dev_blocks, dev_keep, dev_grads, dev_near, dev_far, part_base, slot_global))
    d_pairs = pair_grads.reshape(NODES, 2 * D)
    d_query = query_grads.reshape(NODES, D).astype(jnp.bfloat16)
    query_sum = jnp.dot(features.T, d_query, preferred_element_type=jnp.float32)
    pair_sum = jnp.dot(features.astype(jnp.float32).T, d_pairs, precision=lax.Precision.HIGHEST)
    d_rows = d_resid + jnp.dot(d_query, w_query.T, preferred_element_type=jnp.float32)
    d_rows = d_rows + jnp.dot(d_pairs, w_pair.astype(jnp.float32).T, precision=lax.Precision.HIGHEST)
    factor = 1.0 / math.sqrt(NODES)
    return (output, d_rows.astype(jnp.bfloat16), query_sum * factor, pair_sum[:, :D] * factor, pair_sum[:, D:] * factor, out_sum * factor, expand_sum * factor, reduce_sum * factor)
```

```python
import functools
import math

import jax
import jax.numpy as jnp
from jax import lax
from jax.experimental import pallas as pl
from jax.experimental.pallas import tpu as pltpu
from jax.sharding import PartitionSpec as P

HEADS = 8
EPSILON = 1e-05
MESH = pl.DeviceIdType.MESH
F32 = jnp.float32
BF16 = jnp.bfloat16
NEG = -1e30
VMEM_LIMIT = 56 << 20

D = 256
BLK = 128
TILES = 7
NEAR = 3
ROWS = 4
PART = 16
KEYS = TILES * BLK
N_DOM = 32
N_NODE = 4

_GROUPS = [
    [(2, 2)],
    [(2, 1), (2, 3)],
    [(1, 2), (3, 2)],
    [(1, 1), (3, 3)],
    [(1, 3), (3, 1)],
    [(2, 0), (0, 2)],
    [(1, 0), (3, 0), (0, 1), (0, 3)],
]
OFFSETS = [(a, b, c) for group in _GROUPS for c in range(2) for a, b in group] + [(0, 0, 1)]


def dom_peer(dom, offset, sign=1):
    core = lax.rem(dom, 2)
    y = lax.rem(dom // 2, 4)
    z = dom // 8
    dz, dy, dc = offset
    return (
        lax.rem(z + (dz if sign > 0 else 4 - dz), 4) * 8
        + lax.rem(y + (dy if sign > 0 else 4 - dy), 4) * 2
        + lax.rem(core + dc, 2)
    )


def nt(a, b):
    return lax.dot_general(a, b, (((1,), (1,)), ((), ())), preferred_element_type=F32)


def tn(a, b):
    return lax.dot_general(a, b, (((0,), (0,)), ((), ())), preferred_element_type=F32)


def nn(a, b):
    return jnp.dot(a, b, preferred_element_type=F32)


def exchange_kernel(
    feat_ref, ids_ref, mask_ref, part_ref, far_ref, wanted_ref, bias_ref,
    send_buf, own_buf, ids_smem, near_send, near_recv, id_send, id_recv, far_send, far_recv, local_sem,
):
    dom = lax.axis_index("dom")
    node = lax.axis_index("node")
    barrier = pltpu.get_barrier_semaphore()
    for offset in OFFSETS:
        pl.semaphore_signal(barrier, inc=1, device_id=(dom_peer(dom, offset), node), device_id_type=MESH)
    for step in range(1, N_NODE):
        pl.semaphore_signal(
            barrier, inc=1, device_id=(dom, lax.rem(node + step, N_NODE)), device_id_type=MESH
        )
    pl.semaphore_wait(barrier, len(OFFSETS) + N_NODE - 1)

    near_copies = []
    for step in range(1, N_NODE):
        copy = pltpu.make_async_remote_copy(
            src_ref=feat_ref, dst_ref=part_ref.at[pl.ds(node * ROWS, ROWS)],
            send_sem=near_send.at[step - 1], recv_sem=near_recv.at[step - 1],
            device_id=(dom, lax.rem(node + step, N_NODE)), device_id_type=MESH,
        )
        copy.start()
        near_copies.append(copy)
    id_copies = []
    for index, offset in enumerate(OFFSETS):
        peer = dom_peer(dom, offset)
        copy = pltpu.make_async_remote_copy(
            src_ref=ids_ref.at[peer], dst_ref=wanted_ref.at[dom],
            send_sem=id_send.at[index], recv_sem=id_recv.at[index],
            device_id=(peer, node), device_id_type=MESH,
        )
        copy.start()
        id_copies.append(copy)
    part_ref[pl.ds(node * ROWS, ROWS)] = feat_ref[...]
    wanted_ref[dom] = ids_ref[dom]
    for copy in id_copies:
        copy.wait()
    to_smem = pltpu.make_async_copy(wanted_ref, ids_smem, local_sem.at[0])
    to_smem.start()
    to_smem.wait()
    for copy in near_copies:
        copy.wait()

    far_copies = []
    for index, offset in enumerate(OFFSETS):
        peer = dom_peer(dom, offset)
        for slot in range(2):
            send_buf[index, slot] = part_ref[ids_smem[peer, 0, slot]]
        copy = pltpu.make_async_remote_copy(
            src_ref=send_buf.at[index], dst_ref=far_ref.at[dom],
            send_sem=far_send.at[index], recv_sem=far_recv.at[index],
            device_id=(peer, node), device_id_type=MESH,
        )
        copy.start()
        far_copies.append(copy)
    for slot in range(2):
        own_buf[slot] = part_ref[ids_smem[dom, 0, slot]]
    own_copy = pltpu.make_async_copy(own_buf, far_ref.at[dom], local_sem.at[1])
    own_copy.start()

    def to_bias(row, carry):
        start = pl.multiple_of(row * BLK, BLK)
        diagonal = lax.broadcasted_iota(jnp.int32, (BLK, BLK), 0) == lax.broadcasted_iota(
            jnp.int32, (BLK, BLK), 1
        )
        for tile in range(TILES):
            allowed = mask_ref[pl.ds(start, BLK), tile, :] > 0
            if tile == 0:
                allowed = jnp.logical_or(allowed, diagonal)
            bias_ref[pl.ds(start, BLK), tile * BLK : (tile + 1) * BLK] = jnp.where(
                allowed, 0.0, NEG
            ).astype(BF16)
        return carry

    lax.fori_loop(0, ROWS, to_bias, 0)
    own_copy.wait()
    for copy in far_copies:
        copy.wait()


def layer_kernel(
    local_ref, slot_ref, feat_ref, part_ref, far_ref, bias_ref, d_out_ref,
    wq_ref, wk_ref, wv_ref, wo_ref, we_ref, wr_ref, gain_a_ref, gain_f_ref, hm_ref,
    out_ref, back_ref, near_ref, rows_ref, grads_ref,
    fs, ks, vs, qs, ps, mixed, d_mixed, resid_grad, pair_acc, query_acc, expand_acc, reduce_acc, out_acc, sems,
):
    node = lax.axis_index("node")
    scale = 1.0 / math.sqrt(D // HEADS)
    log2e = math.log2(math.e)
    copies = []
    for row in range(ROWS):
        for tile in range(TILES - NEAR):
            copy = pltpu.make_async_copy(
                far_ref.at[slot_ref[row, tile]],
                fs.at[row, pl.ds((NEAR + tile) * BLK, BLK)],
                sems.at[row * (TILES - NEAR) + tile],
            )
            copy.start()
            copies.append(copy)
    for row in range(ROWS):
        fs[row, 0:BLK] = feat_ref[row * BLK : (row + 1) * BLK]
        for tile in range(NEAR - 1):
            fs[row, (tile + 1) * BLK : (tile + 2) * BLK] = part_ref[local_ref[row, tile]]
    back_ref[...] = jnp.zeros(back_ref.shape, BF16)
    near_ref[...] = jnp.zeros(near_ref.shape, F32)
    pair_acc[...] = jnp.zeros(pair_acc.shape, F32)
    query_acc[...] = jnp.zeros(query_acc.shape, F32)
    expand_acc[...] = jnp.zeros(expand_acc.shape, F32)
    reduce_acc[...] = jnp.zeros(reduce_acc.shape, F32)
    out_acc[...] = jnp.zeros(out_acc.shape, F32)
    qs[...] = nn(feat_ref[...], wq_ref[...]).astype(BF16)
    for copy in copies:
        copy.wait()

    head_low = [hm_ref[h : h + 1, :].astype(BF16) for h in range(HEADS)]
    head_f32 = [hm_ref[h : h + 1, :] for h in range(HEADS)]

    def forward(row, carry):
        start = pl.multiple_of(row * BLK, BLK)
        tile_rows = fs[row]
        keys = nn(tile_rows, wk_ref[...]).astype(BF16)
        ks[row] = keys
        values = nn(tile_rows, wv_ref[...]).astype(BF16)
        vs[row] = values
        query = qs[pl.ds(start, BLK), :]
        bias = bias_ref[pl.ds(start, BLK), :].astype(F32)
        total = jnp.zeros((BLK, D), F32)
        for pair in range(HEADS // 2):
            both = jnp.concatenate([query * head_low[2 * pair], query * head_low[2 * pair + 1]], 0)
            scores = nt(both, keys) * (scale * log2e)
            for half in range(2):
                mine = scores[half * BLK : (half + 1) * BLK] + bias
                top = jnp.max(mine, -1, keepdims=True)
                weight = jnp.exp2(mine - top)
                norm = 1.0 / jnp.sum(weight, -1, keepdims=True)
                ps[row, (2 * pair + half) * BLK : (2 * pair + half + 1) * BLK, :] = (weight * norm).astype(BF16)
            got = nn(ps[row, 2 * pair * BLK : (2 * pair + 2) * BLK, :], values)
            total = total + got[:BLK] * head_f32[2 * pair] + got[BLK:] * head_f32[2 * pair + 1]
        mixed[pl.ds(start, BLK), :] = total
        return carry

    lax.fori_loop(0, ROWS, forward, 0)

    chunk = 256

    def feed(step, carry):
        start = pl.multiple_of(step * chunk, chunk)
        sel = pl.ds(start, chunk)
        mixed_low = mixed[sel, :].astype(BF16)
        gain_a = gain_a_ref[...]
        gain_f = gain_f_ref[...]
        residual = feat_ref[sel, :].astype(F32) + nn(mixed_low, wo_ref[...])
        center = residual - jnp.mean(residual, -1, keepdims=True)
        rstd_a = lax.rsqrt(jnp.mean(center * center, -1, keepdims=True) + EPSILON)
        hat_a = center * rstd_a
        first_low = (hat_a * gain_a).astype(BF16)
        pre = nn(first_low, we_ref[...])
        root = math.sqrt(2.0 / math.pi)
        square = pre * pre
        tanh = jnp.tanh(root * (pre + 0.044715 * (square * pre)))
        half = 0.5 * (1.0 + tanh)
        act_low = (pre * half).astype(BF16)
        slope = half + 0.5 * pre * (1.0 - tanh * tanh) * (root * (1.0 + 3.0 * 0.044715 * square))
        second = first_low.astype(F32) + nn(act_low, wr_ref[...])
        center = second - jnp.mean(second, -1, keepdims=True)
        rstd_f = lax.rsqrt(jnp.mean(center * center, -1, keepdims=True) + EPSILON)
        hat_f = center * rstd_f
        out_ref[sel, :] = (hat_f * gain_f).astype(BF16)
        d_hat = d_out_ref[sel, :].astype(F32) * gain_f
        d_second = rstd_f * (
            d_hat - jnp.mean(d_hat, -1, keepdims=True) - hat_f * jnp.mean(d_hat * hat_f, -1, keepdims=True)
        )
        d_second_low = d_second.astype(BF16)
        reduce_acc[...] += tn(d_second_low, act_low)
        d_pre_low = (nt(d_second_low, wr_ref[...]) * slope).astype(BF16)
        expand_acc[...] += tn(first_low, d_pre_low)
        d_first = d_second + nt(d_pre_low, we_ref[...])
        d_hat = d_first * gain_a
        d_resid = rstd_a * (
            d_hat - jnp.mean(d_hat, -1, keepdims=True) - hat_a * jnp.mean(d_hat * hat_a, -1, keepdims=True)
        )
        resid_grad[sel, :] = d_resid
        d_resid_low = d_resid.astype(BF16)
        out_acc[...] += tn(mixed_low, d_resid_low)
        d_mixed[sel, :] = nt(d_resid_low, wo_ref[...]).astype(BF16)
        return carry

    lax.fori_loop(0, ROWS * BLK // chunk, feed, 0)

    first_half = lax.broadcasted_iota(jnp.int32, (64, BLK), 0) < 32

    def block_diagonal(turned, pair):
        piece = turned[64 * pair : 64 * pair + 64]
        return jnp.concatenate(
            [jnp.where(first_half, piece, 0.0), jnp.where(first_half, 0.0, piece)], 1
        ).astype(BF16)

    def backward(row, carry):
        start = pl.multiple_of(row * BLK, BLK)
        keys = ks[row]
        values = vs[row]
        query = qs[pl.ds(start, BLK), :]
        grad = d_mixed[pl.ds(start, BLK), :]
        query_t = query.astype(F32).T
        grad_t = grad.astype(F32).T
        inner_full = grad.astype(F32) * mixed[pl.ds(start, BLK), :]
        d_query = jnp.zeros((BLK, D), F32)
        key_parts = []
        value_parts = []
        for pair in range(HEADS // 2):
            both = jnp.concatenate([grad * head_low[2 * pair], grad * head_low[2 * pair + 1]], 0)
            inner = jnp.concatenate(
                [
                    jnp.sum(inner_full * head_f32[2 * pair], -1, keepdims=True),
                    jnp.sum(inner_full * head_f32[2 * pair + 1], -1, keepdims=True),
                ],
                0,
            )
            probs_low = ps[row, 2 * pair * BLK : (2 * pair + 2) * BLK, :]
            d_probs = nt(both, values)
            d_scores = (probs_low.astype(F32) * ((d_probs - inner) * scale)).astype(BF16)
            got = nn(d_scores, keys)
            d_query = d_query + got[:BLK] * head_f32[2 * pair] + got[BLK:] * head_f32[2 * pair + 1]
            key_parts.append(nn(block_diagonal(query_t, pair), d_scores).astype(BF16))
            value_parts.append(nn(block_diagonal(grad_t, pair), probs_low).astype(BF16))
        d_keys_t = jnp.concatenate(key_parts, 0)
        d_values_t = jnp.concatenate(value_parts, 0)
        tile_rows = fs[row]
        pair_acc[0:D, :] += nn(d_keys_t, tile_rows)
        pair_acc[D : 2 * D, :] += nn(d_values_t, tile_rows)
        d_rows_t = nn(wk_ref[...], d_keys_t) + nn(wv_ref[...], d_values_t)
        near_ids = [node * ROWS + row, local_ref[row, 0], local_ref[row, 1]]
        for tile in range(TILES):
            piece = d_rows_t[:, tile * BLK : (tile + 1) * BLK].T
            if tile < NEAR:
                near_ref[near_ids[tile]] += piece
            else:
                back_ref[slot_ref[row, tile - NEAR]] = piece.astype(BF16)
        d_query_low = d_query.astype(BF16)
        query_acc[...] += tn(tile_rows[:BLK], d_query_low)
        rows_ref[pl.ds(start, BLK), :] = resid_grad[pl.ds(start, BLK), :] + nt(d_query_low, wq_ref[...])
        return carry

    lax.fori_loop(0, ROWS, backward, 0)

    place = 0
    for acc in (query_acc, pair_acc, out_acc, expand_acc, reduce_acc):
        for top in range(0, acc.shape[0], D):
            for left in range(0, acc.shape[1], BLK):
                grads_ref[place : place + D, :] = acc[top : top + D, left : left + BLK].astype(BF16)
                place += D


LINE = 8
PLANE = 16
LINE_ROWS = 6144 // LINE
PLANE_ROWS = LINE_ROWS // PLANE


def return_kernel(
    wanted_ref, back_ref, near_ref, grads_ref,
    own_ref, cross_ref, sum_ref,
    recv, acc, cross_send, line_recv, line_sum, plane_recv, plane_sum, plane_all,
    far_send, far_recv, x_send, x_recv, ls_send, ls_recv, ps_send, ps_recv, pg_send, pg_recv, lg_send, lg_recv,
    local_sem,
):
    dom = lax.axis_index("dom")
    node = lax.axis_index("node")
    core = lax.rem(dom, 2)
    member = node * 2 + core
    spot = dom // 2

    def line_peer(step):
        other = lax.rem(member + step, LINE)
        return other, (dom - core + lax.rem(other, 2), other // 2)

    def plane_peer(step):
        other = lax.rem(spot + step, PLANE)
        return other, (other * 2 + core, node)

    barrier = pltpu.get_barrier_semaphore()
    for offset in OFFSETS:
        pl.semaphore_signal(barrier, inc=1, device_id=(dom_peer(dom, offset), node), device_id_type=MESH)
    for step in range(1, N_NODE):
        for flip in range(2):
            pl.semaphore_signal(
                barrier, inc=1,
                device_id=(dom - core + lax.rem(core + flip, 2), lax.rem(node + step, N_NODE)),
                device_id_type=MESH,
            )
    pl.semaphore_wait(barrier, len(OFFSETS) + 2 * (N_NODE - 1))

    line_copies = []
    for step in range(1, LINE):
        other, device = line_peer(step)
        copy = pltpu.make_async_remote_copy(
            src_ref=grads_ref.at[pl.ds(pl.multiple_of(other * LINE_ROWS, LINE_ROWS), LINE_ROWS)],
            dst_ref=line_recv.at[step - 1],
            send_sem=ls_send.at[step - 1], recv_sem=ls_recv.at[step - 1],
            device_id=device, device_id_type=MESH,
        )
        copy.start()
        line_copies.append(copy)
    far_copies = []
    for index, offset in enumerate(OFFSETS):
        peer = dom_peer(dom, offset)
        copy = pltpu.make_async_remote_copy(
            src_ref=back_ref.at[peer], dst_ref=recv.at[index],
            send_sem=far_send.at[index], recv_sem=far_recv.at[index],
            device_id=(peer, node), device_id_type=MESH,
        )
        copy.start()
        far_copies.append(copy)
    own_copy = pltpu.make_async_copy(back_ref.at[dom], recv.at[N_DOM - 1], local_sem)
    own_copy.start()
    acc[...] = near_ref[...]

    def combine(index, source):
        first = wanted_ref[source, 0, 0]
        second = wanted_ref[source, 0, 1]

        def add(block, carry):
            take_first = (first == block).astype(F32)
            take_second = (second == block).astype(F32)
            acc[block] += recv[index, 0].astype(F32) * take_first + recv[index, 1].astype(F32) * take_second
            return carry

        lax.fori_loop(0, PART, add, 0)

    own_copy.wait()
    combine(N_DOM - 1, dom)
    for copy in line_copies:
        copy.wait()
    mine = pl.ds(pl.multiple_of(member * LINE_ROWS, LINE_ROWS), LINE_ROWS)
    total = grads_ref[mine, :].astype(F32)
    for step in range(1, LINE):
        total = total + line_recv[step - 1].astype(F32)
    line_sum[...] = total.astype(BF16)
    plane_copies = []
    for step in range(1, PLANE):
        other, device = plane_peer(step)
        copy = pltpu.make_async_remote_copy(
            src_ref=line_sum.at[pl.ds(pl.multiple_of(other * PLANE_ROWS, PLANE_ROWS), PLANE_ROWS)],
            dst_ref=plane_recv.at[step - 1],
            send_sem=ps_send.at[step - 1], recv_sem=ps_recv.at[step - 1],
            device_id=device, device_id_type=MESH,
        )
        copy.start()
        plane_copies.append(copy)

    def take(begin, end):
        for index in range(begin, end):
            far_copies[index].wait()
            combine(index, dom_peer(dom, OFFSETS[index], -1))

    take(0, 8)
    for copy in plane_copies:
        copy.wait()
    spot_rows = pl.ds(pl.multiple_of(spot * PLANE_ROWS, PLANE_ROWS), PLANE_ROWS)
    total = line_sum[spot_rows, :].astype(F32)
    for step in range(1, PLANE):
        total = total + plane_recv[step - 1].astype(F32)
    plane_sum[...] = total.astype(BF16)
    gather_copies = []
    for step in range(1, PLANE):
        other, device = plane_peer(step)
        copy = pltpu.make_async_remote_copy(
            src_ref=plane_sum, dst_ref=plane_all.at[spot_rows],
            send_sem=pg_send.at[step - 1], recv_sem=pg_recv.at[step - 1],
            device_id=device, device_id_type=MESH,
        )
        copy.start()
        gather_copies.append(copy)
    plane_all[spot_rows, :] = plane_sum[...]
    take(8, 16)
    for copy in gather_copies:
        copy.wait()
    spread_copies = []
    for step in range(1, LINE):
        other, device = line_peer(step)
        copy = pltpu.make_async_remote_copy(
            src_ref=plane_all, dst_ref=sum_ref.at[mine],
            send_sem=lg_send.at[step - 1], recv_sem=lg_recv.at[step - 1],
            device_id=device, device_id_type=MESH,
        )
        copy.start()
        spread_copies.append(copy)
    sum_ref[mine, :] = plane_all[...]
    take(16, len(OFFSETS))

    cross_send[...] = acc[...].astype(BF16)
    cross_copies = []
    for step in range(1, N_NODE):
        other = lax.rem(node + step, N_NODE)
        copy = pltpu.make_async_remote_copy(
            src_ref=cross_send.at[pl.ds(other * ROWS, ROWS)], dst_ref=cross_ref.at[step - 1],
            send_sem=x_send.at[step - 1], recv_sem=x_recv.at[step - 1],
            device_id=(dom, other), device_id_type=MESH,
        )
        copy.start()
        cross_copies.append(copy)
    own_ref[...] = acc[pl.ds(node * ROWS, ROWS)]
    for copy in spread_copies:
        copy.wait()
    for copy in cross_copies:
        copy.wait()


def finish_kernel(factor, rows_ref, own_ref, cross_ref, sum_ref, dx_ref, gq, gk, gv, go, ge, gr):
    for row in range(ROWS):
        total = rows_ref[row * BLK : (row + 1) * BLK, :] + own_ref[row]
        for step in range(N_NODE - 1):
            total = total + cross_ref[step, row].astype(F32)
        dx_ref[row * BLK : (row + 1) * BLK, :] = total.astype(BF16)

    def piece(index):
        return sum_ref[index * D : (index + 1) * D, :].astype(F32) * factor

    for half in range(2):
        span = slice(half * BLK, (half + 1) * BLK)
        gq[:, span] = piece(half)
        gk[span, :] = piece(2 + half).T
        gv[span, :] = piece(4 + half).T
        go[:, span] = piece(6 + half)
    for part in range(8):
        span = slice(part * BLK, (part + 1) * BLK)
        ge[:, span] = piece(8 + part)
        gr[span, :] = piece(16 + part).T


def vmem(shape, dtype):
    return pltpu.VMEM(shape, dtype)


IN_VMEM = pl.BlockSpec(memory_space=pltpu.VMEM)
IN_SMEM = pl.BlockSpec(memory_space=pltpu.SMEM)
ANYWHERE = pl.BlockSpec(memory_space=pl.ANY)


def on_device(
    features, w_query, w_key, w_value, w_out, w_expand, w_reduce, gain_attn, gain_ffn,
    tile_mask, local_block, remote_slot, remote_block, d_out,
):
    rows = features.shape[0]
    dma = pltpu.SemaphoreType.DMA
    peers = len(OFFSETS)
    ids = jnp.pad(remote_block.reshape(N_DOM, 1, 2), ((0, 0), (0, 0), (0, BLK - 2)))
    part, far, wanted, bias = pl.pallas_call(
        exchange_kernel,
        out_shape=(
            jax.ShapeDtypeStruct((PART, BLK, D), BF16),
            jax.ShapeDtypeStruct((N_DOM, 2, BLK, D), BF16),
            jax.ShapeDtypeStruct((N_DOM, 1, BLK), jnp.int32),
            jax.ShapeDtypeStruct((rows, KEYS), BF16),
        ),
        in_specs=[IN_VMEM] * 3,
        out_specs=(IN_VMEM, ANYWHERE, IN_VMEM, IN_VMEM),
        scratch_shapes=[
            vmem((peers, 2, BLK, D), BF16), vmem((2, BLK, D), BF16), pltpu.SMEM((N_DOM, 1, BLK), jnp.int32),
            dma((N_NODE - 1,)), dma((N_NODE - 1,)), dma((peers,)), dma((peers,)), dma((peers,)), dma((peers,)),
            dma((2,)),
        ],
        compiler_params=pltpu.CompilerParams(
            collective_id=1, has_side_effects=True, vmem_limit_bytes=VMEM_LIMIT
        ),
        name="exchange",
    )(features.reshape(ROWS, BLK, D), ids, tile_mask)

    lanes = jnp.arange(D)[None, :] // (D // HEADS) == jnp.arange(HEADS)[:, None]
    output, back, near, d_rows, grads = pl.pallas_call(
        layer_kernel,
        out_shape=(
            jax.ShapeDtypeStruct((rows, D), BF16),
            jax.ShapeDtypeStruct((2 * N_DOM, BLK, D), BF16),
            jax.ShapeDtypeStruct((PART, BLK, D), F32),
            jax.ShapeDtypeStruct((rows, D), F32),
            jax.ShapeDtypeStruct((6144, BLK), BF16),
        ),
        in_specs=[IN_SMEM, IN_SMEM, IN_VMEM, IN_VMEM, ANYWHERE] + [IN_VMEM] * 11,
        out_specs=(IN_VMEM,) * 5,
        scratch_shapes=[
            vmem((ROWS, KEYS, D), BF16), vmem((ROWS, KEYS, D), BF16), vmem((ROWS, KEYS, D), BF16),
            vmem((rows, D), BF16), vmem((ROWS, HEADS * BLK, KEYS), BF16), vmem((rows, D), F32),
            vmem((rows, D), BF16), vmem((rows, D), F32), vmem((2 * D, D), F32), vmem((D, D), F32),
            vmem((D, 4 * D), F32), vmem((D, 4 * D), F32), vmem((D, D), F32), dma((16,)),
        ],
        compiler_params=pltpu.CompilerParams(vmem_limit_bytes=VMEM_LIMIT),
        name="layer",
    )(
        local_block, remote_slot, features, part, far.reshape(2 * N_DOM, BLK, D), bias, d_out,
        w_query, w_key, w_value, w_out, w_expand, w_reduce, gain_attn.reshape(1, D), gain_ffn.reshape(1, D),
        lanes.astype(F32),
    )

    own, cross, summed = pl.pallas_call(
        return_kernel,
        out_shape=(
            jax.ShapeDtypeStruct((ROWS, BLK, D), F32),
            jax.ShapeDtypeStruct((N_NODE - 1, ROWS, BLK, D), BF16),
            jax.ShapeDtypeStruct((6144, BLK), BF16),
        ),
        in_specs=[IN_SMEM, ANYWHERE, IN_VMEM, IN_VMEM],
        out_specs=(IN_VMEM,) * 3,
        scratch_shapes=[
            vmem((N_DOM, 2, BLK, D), BF16), vmem((PART, BLK, D), F32), vmem((PART, BLK, D), BF16),
            vmem((LINE - 1, LINE_ROWS, BLK), BF16), vmem((LINE_ROWS, BLK), BF16),
            vmem((PLANE - 1, PLANE_ROWS, BLK), BF16), vmem((PLANE_ROWS, BLK), BF16), vmem((LINE_ROWS, BLK), BF16),
            dma((peers,)), dma((peers,)), dma((N_NODE - 1,)), dma((N_NODE - 1,)),
            dma((LINE - 1,)), dma((LINE - 1,)), dma((PLANE - 1,)), dma((PLANE - 1,)),
            dma((PLANE - 1,)), dma((PLANE - 1,)), dma((LINE - 1,)), dma((LINE - 1,)), dma,
        ],
        compiler_params=pltpu.CompilerParams(
            collective_id=2, has_side_effects=True, vmem_limit_bytes=VMEM_LIMIT
        ),
        name="give_back",
    )(wanted, back.reshape(N_DOM, 2, BLK, D), near, grads)

    factor = 1.0 / math.sqrt(rows * N_DOM * N_NODE)
    finished = pl.pallas_call(
        functools.partial(finish_kernel, factor),
        out_shape=(
            jax.ShapeDtypeStruct((rows, D), BF16),
            jax.ShapeDtypeStruct((D, D), F32),
            jax.ShapeDtypeStruct((D, D), F32),
            jax.ShapeDtypeStruct((D, D), F32),
            jax.ShapeDtypeStruct((D, D), F32),
            jax.ShapeDtypeStruct((D, 4 * D), F32),
            jax.ShapeDtypeStruct((4 * D, D), F32),
        ),
        in_specs=[IN_VMEM] * 4,
        out_specs=(IN_VMEM,) * 7,
        compiler_params=pltpu.CompilerParams(vmem_limit_bytes=VMEM_LIMIT),
        name="finish",
    )(d_rows, own, cross, summed)
    return (output,) + tuple(finished)


def solution(mesh):
    split = P(("dom", "node"), None)
    placed = (
        (split,) + (P(),) * 8 + (P(("dom", "node"), None, None), split, split, P("dom", "node", None), split)
    )
    return jax.shard_map(
        on_device, mesh=mesh, in_specs=placed, out_specs=(split, split) + (P(),) * 6, check_vma=False
    )
```

```python
import functools
import math

import jax
import jax.numpy as jnp
from jax import lax
from jax.experimental import pallas as pl
from jax.experimental.pallas import tpu as pltpu
from jax.sharding import PartitionSpec as P

HEADS = 8
EPSILON = 1e-05
MESH = pl.DeviceIdType.MESH
F32 = jnp.float32
BF16 = jnp.bfloat16
NEG = -1e30
VMEM_LIMIT = 56 << 20

D = 256
BLK = 128
TILES = 7
NEAR = 3
ROWS = 4
PART = 16
KEYS = TILES * BLK
N_DOM = 32
N_NODE = 4
CHUNKS = 2
SPAN = BLK // (2 * CHUNKS)

_GROUPS = [
    [(2, 2)],
    [(2, 1), (2, 3)],
    [(1, 2), (3, 2)],
    [(1, 1), (3, 3)],
    [(1, 3), (3, 1)],
    [(2, 0), (0, 2)],
    [(1, 0), (3, 0), (0, 1), (0, 3)],
]
OFFSETS = [(a, b, c) for group in _GROUPS for c in range(2) for a, b in group] + [(0, 0, 1)]


def dom_peer(dom, offset, sign=1):
    core = lax.rem(dom, 2)
    y = lax.rem(dom // 2, 4)
    z = dom // 8
    dz, dy, dc = offset
    return (
        lax.rem(z + (dz if sign > 0 else 4 - dz), 4) * 8
        + lax.rem(y + (dy if sign > 0 else 4 - dy), 4) * 2
        + lax.rem(core + dc, 2)
    )


def nt(a, b):
    return lax.dot_general(a, b, (((1,), (1,)), ((), ())), preferred_element_type=F32)


def tn(a, b):
    return lax.dot_general(a, b, (((0,), (0,)), ((), ())), preferred_element_type=F32)


def nn(a, b):
    return jnp.dot(a, b, preferred_element_type=F32)


def place():
    dom = lax.axis_index("dom")
    return dom // 8, lax.rem(dom // 2, 4), lax.rem(dom, 2), lax.axis_index("node")


def device(z, y, core, node):
    return (z * 8 + y * 2 + core, node)


def four(value):
    return lax.rem(value, 4)


def two(value):
    return lax.rem(value, 2)


def plane_peers(z, y, core):
    peers = [(z, y, two(core + 1))]
    for step in range(1, 4):
        for flip in range(2):
            peers.append((four(z + step), y, two(core + flip)))
            peers.append((z, four(y + step), two(core + flip)))
    return peers


def first_phase(chunk, sources, relays, sends, recvs):
    z, y, core, node = place()
    copies = []
    for step in range(1, 4):
        for half in range(2):
            target = four((z, y)[half] + step)
            copy = pltpu.make_async_remote_copy(
                src_ref=sources[half].at[chunk, pl.ds(target * 8, 8)],
                dst_ref=relays[half].at[chunk, step - 1],
                send_sem=sends.at[chunk, half, step - 1], recv_sem=recvs.at[chunk, half, step - 1],
                device_id=(device(target, y, core, node), device(z, target, core, node))[half],
                device_id_type=MESH,
            )
            copy.start()
            copies.append((half, step, copy))
    return copies


def second_phase(chunk, half, group, sources, relays, lands, sends, recvs):
    z, y, core, node = place()
    copies = []
    for step in range(4):
        for flip in range(2):
            if step == 0 and flip == 0:
                continue
            target = four((y, z)[half] + step)
            side = two(core + flip)
            if group == 0:
                source = sources[half].at[chunk, (z, y)[half] * 8 + target * 2 + side]
            else:
                source = relays[half].at[chunk, group - 1, target * 2 + side]
            copy = pltpu.make_async_remote_copy(
                src_ref=source, dst_ref=lands[half].at[chunk, group, step, flip],
                send_sem=sends.at[chunk, half, group, step, flip],
                recv_sem=recvs.at[chunk, half, group, step, flip],
                device_id=(device(z, target, side, node), device(target, y, side, node))[half],
                device_id_type=MESH,
            )
            copy.start()
            copies.append(copy)
    return copies


def origin(half, group, step, flip):
    z, y, core, node = place()
    far, near = 4 - group, 4 - step
    if half == 0:
        return four(z + far) * 8 + four(y + near) * 2 + two(core + flip)
    return four(z + near) * 8 + four(y + far) * 2 + two(core + flip)


def exchange_kernel(
    feat_ref, table_ref, mask_ref, part_0, part_1, land_a, land_b, wanted_ref, bias_ref,
    ids, stage_a, stage_b, relay_a, relay_b, ids_smem,
    near_send, near_recv, id_send, id_recv, send1, recv1, send2, recv2, own_sem, local_sem,
):
    dom = lax.axis_index("dom")
    z, y, core, node = place()
    stages, relays, lands = (stage_a, stage_b), (relay_a, relay_b), (land_a, land_b)
    parts = (part_0, part_1)
    barrier = pltpu.get_barrier_semaphore()
    for offset in OFFSETS:
        pl.semaphore_signal(barrier, inc=1, device_id=(dom_peer(dom, offset), node), device_id_type=MESH)
    for step in range(1, N_NODE):
        pl.semaphore_signal(
            barrier, inc=1, device_id=(dom, lax.rem(node + step, N_NODE)), device_id_type=MESH
        )
    lane = lax.broadcasted_iota(jnp.int32, (1, BLK), 1)
    for peer in range(N_DOM):
        ids[peer] = jnp.where(
            lane == 0, table_ref[0, 2 * peer], jnp.where(lane == 1, table_ref[0, 2 * peer + 1], 0)
        )
    pl.semaphore_wait(barrier, len(OFFSETS) + N_NODE - 1)

    id_copies = []
    for index, offset in enumerate(OFFSETS):
        peer = dom_peer(dom, offset)
        copy = pltpu.make_async_remote_copy(
            src_ref=ids.at[peer], dst_ref=wanted_ref.at[dom],
            send_sem=id_send.at[index], recv_sem=id_recv.at[index],
            device_id=(peer, node), device_id_type=MESH,
        )
        copy.start()
        id_copies.append(copy)
    near_copies = []
    for chunk in range(CHUNKS):
        for step in range(1, N_NODE):
            copy = pltpu.make_async_remote_copy(
                src_ref=feat_ref.at[:, pl.ds(chunk * 2 * SPAN, 2 * SPAN)],
                dst_ref=parts[chunk].at[pl.ds(node * ROWS, ROWS)],
                send_sem=near_send.at[chunk, step - 1], recv_sem=near_recv.at[chunk, step - 1],
                device_id=(dom, lax.rem(node + step, N_NODE)), device_id_type=MESH,
            )
            copy.start()
            near_copies.append(copy)
    for chunk in range(CHUNKS):
        parts[chunk][pl.ds(node * ROWS, ROWS)] = feat_ref[:, chunk * 2 * SPAN : (chunk + 1) * 2 * SPAN]
    wanted_ref[dom] = ids[dom]
    for copy in id_copies:
        copy.wait()
    to_smem = pltpu.make_async_copy(wanted_ref, ids_smem, local_sem)
    to_smem.start()
    to_smem.wait()

    def stage(chunk):
        def body(peer, carry):
            turned = lax.rem(peer // 2, 4) * 8 + (peer // 8) * 2 + lax.rem(peer, 2)
            for slot in range(2):
                block = ids_smem[peer, 0, slot]
                stage_a[chunk, peer, slot] = parts[chunk][block, 0:SPAN]
                stage_b[chunk, turned, slot] = parts[chunk][block, SPAN : 2 * SPAN]
            return carry

        lax.fori_loop(0, N_DOM, body, 0)

    def keep(chunk, half, group):
        if group == 0:
            source = stages[half].at[chunk, (dom, y * 8 + z * 2 + core)[half]]
        else:
            source = relays[half].at[chunk, group - 1, (y, z)[half] * 2 + core]
        copy = pltpu.make_async_copy(
            source, lands[half].at[chunk, group, 0, 0], own_sem.at[chunk, half, group]
        )
        copy.start()
        return copy

    first = []
    second = []
    kept = []
    for chunk in range(CHUNKS):
        for copy in near_copies[chunk * (N_NODE - 1) : (chunk + 1) * (N_NODE - 1)]:
            copy.wait()
        stage(chunk)
        first.append(first_phase(chunk, stages, relays, send1, recv1))
        for half in range(2):
            second += second_phase(chunk, half, 0, stages, relays, lands, send2, recv2)
            kept.append(keep(chunk, half, 0))

    def to_bias(row, carry):
        start = pl.multiple_of(row * BLK, BLK)
        diagonal = lax.broadcasted_iota(jnp.int32, (BLK, BLK), 0) == lax.broadcasted_iota(
            jnp.int32, (BLK, BLK), 1
        )
        for tile in range(TILES):
            allowed = mask_ref[tile, pl.ds(start, BLK), :] > 0
            if tile == 0:
                allowed = jnp.logical_or(allowed, diagonal)
            bias_ref[pl.ds(start, BLK), tile * BLK : (tile + 1) * BLK] = jnp.where(
                allowed, 0.0, NEG
            ).astype(BF16)
        return carry

    lax.fori_loop(0, ROWS, to_bias, 0)
    for chunk in range(CHUNKS):
        for half, step, copy in first[chunk]:
            copy.wait()
            second += second_phase(chunk, half, step, stages, relays, lands, send2, recv2)
            kept.append(keep(chunk, half, step))
    for copy in kept:
        copy.wait()
    for copy in second:
        copy.wait()


def layer_kernel(
    local_ref, slot_ref, feat_ref, part_0, part_1, land_a, land_b, bias_ref, d_out_ref,
    wq_ref, wk_ref, wv_ref, wo_ref, we_ref, wr_ref, gain_a_ref, gain_f_ref,
    out_ref, back_a, back_b, near_ref, rows_ref, grads_ref,
    fs, ks, vs, qs, ps, mixed, d_mixed, resid_grad, pair_acc, query_acc, expand_acc, reduce_acc, out_acc, sems,
):
    scale = 1.0 / math.sqrt(D // HEADS)
    log2e = math.log2(math.e)
    here_z, here_y, here_core, node = place()
    copies = []
    for row in range(ROWS):
        for tile in range(TILES - NEAR):
            slot = slot_ref[row, tile]
            asked = slot // 2
            dz = four(here_z + 4 - asked // 8)
            dy = four(here_y + 4 - four(asked // 2))
            dc = two(here_core + two(asked))
            for chunk in range(CHUNKS):
                for half in range(2):
                    group, step = ((dz, dy), (dy, dz))[half]
                    copy = pltpu.make_async_copy(
                        (land_a, land_b)[half].at[chunk, group, step, dc, two(slot)],
                        fs.at[row, pl.ds((NEAR + tile) * BLK + (2 * chunk + half) * SPAN, SPAN)],
                        sems.at[row * (TILES - NEAR) + tile, chunk, half],
                    )
                    copy.start()
                    copies.append(copy)
    for row in range(ROWS):
        fs[row, 0:BLK] = feat_ref[row * BLK : (row + 1) * BLK]
        for tile in range(NEAR - 1):
            for chunk, part_ref in enumerate((part_0, part_1)):
                top = (tile + 1) * BLK + chunk * 2 * SPAN
                fs[row, top : top + 2 * SPAN] = part_ref[local_ref[tile, row]]
    back_a[...] = jnp.zeros(back_a.shape, BF16)
    back_b[...] = jnp.zeros(back_b.shape, BF16)
    near_ref[...] = jnp.zeros(near_ref.shape, F32)
    pair_acc[...] = jnp.zeros(pair_acc.shape, F32)
    query_acc[...] = jnp.zeros(query_acc.shape, F32)
    expand_acc[...] = jnp.zeros(expand_acc.shape, F32)
    reduce_acc[...] = jnp.zeros(reduce_acc.shape, F32)
    out_acc[...] = jnp.zeros(out_acc.shape, F32)
    qs[...] = nn(feat_ref[...], wq_ref[...]).astype(BF16)
    for copy in copies:
        copy.wait()

    lane_head = lax.broadcasted_iota(jnp.int32, (1, D), 1) // (D // HEADS)
    head_f32 = [(lane_head == h).astype(F32) for h in range(HEADS)]
    head_low = [mask.astype(BF16) for mask in head_f32]

    def forward(row, carry):
        start = pl.multiple_of(row * BLK, BLK)
        tile_rows = fs[row]
        keys = nn(tile_rows, wk_ref[...]).astype(BF16)
        ks[row] = keys
        values = nn(tile_rows, wv_ref[...]).astype(BF16)
        vs[row] = values
        query = qs[pl.ds(start, BLK), :]
        bias = bias_ref[pl.ds(start, BLK), :].astype(F32)
        total = jnp.zeros((BLK, D), F32)
        for pair in range(HEADS // 2):
            both = jnp.concatenate([query * head_low[2 * pair], query * head_low[2 * pair + 1]], 0)
            scores = nt(both, keys) * (scale * log2e)
            for half in range(2):
                mine = scores[half * BLK : (half + 1) * BLK] + bias
                top = jnp.max(mine, -1, keepdims=True)
                weight = jnp.exp2(mine - top)
                norm = 1.0 / jnp.sum(weight, -1, keepdims=True)
                ps[row, (2 * pair + half) * BLK : (2 * pair + half + 1) * BLK, :] = (weight * norm).astype(BF16)
            got = nn(ps[row, 2 * pair * BLK : (2 * pair + 2) * BLK, :], values)
            total = total + got[:BLK] * head_f32[2 * pair] + got[BLK:] * head_f32[2 * pair + 1]
        mixed[pl.ds(start, BLK), :] = total
        return carry

    lax.fori_loop(0, ROWS, forward, 0)

    chunk = 256

    def feed(step, carry):
        start = pl.multiple_of(step * chunk, chunk)
        sel = pl.ds(start, chunk)
        mixed_low = mixed[sel, :].astype(BF16)
        gain_a = gain_a_ref[...]
        gain_f = gain_f_ref[...]
        residual = feat_ref[sel, :].astype(F32) + nn(mixed_low, wo_ref[...])
        center = residual - jnp.mean(residual, -1, keepdims=True)
        rstd_a = lax.rsqrt(jnp.mean(center * center, -1, keepdims=True) + EPSILON)
        hat_a = center * rstd_a
        first_low = (hat_a * gain_a).astype(BF16)
        pre = nn(first_low, we_ref[...])
        root = math.sqrt(2.0 / math.pi)
        square = pre * pre
        tanh = jnp.tanh(root * (pre + 0.044715 * (square * pre)))
        half = 0.5 * (1.0 + tanh)
        act_low = (pre * half).astype(BF16)
        slope = half + 0.5 * pre * (1.0 - tanh * tanh) * (root * (1.0 + 3.0 * 0.044715 * square))
        second = first_low.astype(F32) + nn(act_low, wr_ref[...])
        center = second - jnp.mean(second, -1, keepdims=True)
        rstd_f = lax.rsqrt(jnp.mean(center * center, -1, keepdims=True) + EPSILON)
        hat_f = center * rstd_f
        out_ref[sel, :] = (hat_f * gain_f).astype(BF16)
        d_hat = d_out_ref[sel, :].astype(F32) * gain_f
        d_second = rstd_f * (
            d_hat - jnp.mean(d_hat, -1, keepdims=True) - hat_f * jnp.mean(d_hat * hat_f, -1, keepdims=True)
        )
        d_second_low = d_second.astype(BF16)
        reduce_acc[...] += tn(d_second_low, act_low)
        d_pre_low = (nt(d_second_low, wr_ref[...]) * slope).astype(BF16)
        expand_acc[...] += tn(first_low, d_pre_low)
        d_first = d_second + nt(d_pre_low, we_ref[...])
        d_hat = d_first * gain_a
        d_resid = rstd_a * (
            d_hat - jnp.mean(d_hat, -1, keepdims=True) - hat_a * jnp.mean(d_hat * hat_a, -1, keepdims=True)
        )
        resid_grad[sel, :] = d_resid
        d_resid_low = d_resid.astype(BF16)
        out_acc[...] += tn(mixed_low, d_resid_low)
        d_mixed[sel, :] = nt(d_resid_low, wo_ref[...]).astype(BF16)
        return carry

    lax.fori_loop(0, ROWS * BLK // chunk, feed, 0)

    first_half = lax.broadcasted_iota(jnp.int32, (64, BLK), 0) < 32

    def block_diagonal(turned, pair):
        piece = turned[64 * pair : 64 * pair + 64]
        return jnp.concatenate(
            [jnp.where(first_half, piece, 0.0), jnp.where(first_half, 0.0, piece)], 1
        ).astype(BF16)

    def backward(row, carry):
        start = pl.multiple_of(row * BLK, BLK)
        keys = ks[row]
        values = vs[row]
        query = qs[pl.ds(start, BLK), :]
        grad = d_mixed[pl.ds(start, BLK), :]
        query_t = query.astype(F32).T
        grad_t = grad.astype(F32).T
        inner_full = grad.astype(F32) * mixed[pl.ds(start, BLK), :]
        d_query = jnp.zeros((BLK, D), F32)
        key_parts = []
        value_parts = []
        for pair in range(HEADS // 2):
            both = jnp.concatenate([grad * head_low[2 * pair], grad * head_low[2 * pair + 1]], 0)
            inner = jnp.concatenate(
                [
                    jnp.sum(inner_full * head_f32[2 * pair], -1, keepdims=True),
                    jnp.sum(inner_full * head_f32[2 * pair + 1], -1, keepdims=True),
                ],
                0,
            )
            probs_low = ps[row, 2 * pair * BLK : (2 * pair + 2) * BLK, :]
            d_probs = nt(both, values)
            d_scores = (probs_low.astype(F32) * ((d_probs - inner) * scale)).astype(BF16)
            got = nn(d_scores, keys)
            d_query = d_query + got[:BLK] * head_f32[2 * pair] + got[BLK:] * head_f32[2 * pair + 1]
            key_parts.append(nn(block_diagonal(query_t, pair), d_scores).astype(BF16))
            value_parts.append(nn(block_diagonal(grad_t, pair), probs_low).astype(BF16))
        d_keys_t = jnp.concatenate(key_parts, 0)
        d_values_t = jnp.concatenate(value_parts, 0)
        tile_rows = fs[row]
        pair_acc[0:D, :] += nn(d_keys_t, tile_rows)
        pair_acc[D : 2 * D, :] += nn(d_values_t, tile_rows)
        d_rows_t = nn(wk_ref[...], d_keys_t) + nn(wv_ref[...], d_values_t)
        near_ids = [node * ROWS + row, local_ref[0, row], local_ref[1, row]]
        for tile in range(TILES):
            piece = d_rows_t[:, tile * BLK : (tile + 1) * BLK].T
            if tile < NEAR:
                near_ref[near_ids[tile]] += piece
            else:
                piece = piece.astype(BF16)
                slot = slot_ref[row, tile - NEAR]
                asked = slot // 2
                turned = four(asked // 2) * 8 + (asked // 8) * 2 + two(asked)
                for chunk in range(CHUNKS):
                    top = 2 * chunk * SPAN
                    back_a[chunk, asked, two(slot)] = piece[top : top + SPAN]
                    back_b[chunk, turned, two(slot)] = piece[top + SPAN : top + 2 * SPAN]
        d_query_low = d_query.astype(BF16)
        query_acc[...] += tn(tile_rows[:BLK], d_query_low)
        rows_ref[pl.ds(start, BLK), :] = resid_grad[pl.ds(start, BLK), :] + nt(d_query_low, wq_ref[...])
        return carry

    lax.fori_loop(0, ROWS, backward, 0)

    spot = 0
    for acc in (query_acc, pair_acc, out_acc, expand_acc, reduce_acc):
        for top in range(0, acc.shape[0], D):
            for left in range(0, acc.shape[1], BLK):
                grads_ref[spot : spot + D, :] = acc[top : top + D, left : left + BLK].astype(BF16)
                spot += D


SUM_ROWS = 6144
CORE_ROWS = SUM_ROWS // 2
X_ROWS = CORE_ROWS // 4
Z_ROWS = X_ROWS // 4
Y_ROWS = Z_ROWS // 4


def rows_at(index, size):
    return pl.ds(pl.multiple_of(index * size, size), size)


def return_kernel(
    wanted_ref, back_a, back_b, near_ref, grads_ref,
    own_ref, cross_ref, sum_ref,
    relay_a, relay_b, land_a, land_b, acc, chosen, cross_send,
    core_recv, core_sum, x_recv, x_sum, z_recv, z_sum, y_recv, y_sum, z_all, x_all,
    send1, recv1, send2, recv2, own_sem, cross_sems, core_sems, x_sems, z_sems, y_sems,
):
    dom = lax.axis_index("dom")
    z, y, core, node = place()
    sources, relays, lands = (back_a, back_b), (relay_a, relay_b), (land_a, land_b)

    barrier = pltpu.get_barrier_semaphore()
    peers = [device(*peer, node) for peer in plane_peers(z, y, core)]
    peers += [(dom, four(node + step)) for step in range(1, N_NODE)]
    for peer in peers:
        pl.semaphore_signal(barrier, inc=1, device_id=peer, device_id_type=MESH)
    pl.semaphore_wait(barrier, len(peers))

    def push(src, dst, sems, key, target):
        copy = pltpu.make_async_remote_copy(
            src_ref=src, dst_ref=dst, send_sem=sems.at[(0,) + key], recv_sem=sems.at[(1,) + key],
            device_id=target, device_id_type=MESH,
        )
        copy.start()
        return copy

    sibling = device(z, y, two(core + 1), node)
    axes = [
        (node, lambda other: device(z, y, core, other)),
        (z, lambda other: device(other, y, core, node)),
        (y, lambda other: device(z, other, core, node)),
    ]

    def scatter(axis, src, dst, sems, size):
        index, target = axes[axis]
        copies = []
        for step in range(1, 4):
            other = four(index + step)
            copies.append(push(src.at[rows_at(other, size)], dst.at[step - 1], sems, (0, step - 1), target(other)))
        return copies

    def gather(axis, src, dst, sems, size):
        index, target = axes[axis]
        mine = rows_at(index, size)
        copies = []
        for step in range(1, 4):
            copies.append(push(src, dst.at[mine], sems, (1, step - 1), target(four(index + step))))
        dst[mine, :] = src[...]
        return copies

    def finish(copies):
        for copy in copies:
            copy.wait()

    def add_up(axis, src, recv, out, size):
        total = src[rows_at(axes[axis][0], size), :].astype(F32)
        for step in range(3):
            total = total + recv[step].astype(F32)
        out[...] = total.astype(BF16)

    core_mine = rows_at(core, CORE_ROWS)
    core_copy = push(grads_ref.at[rows_at(two(core + 1), CORE_ROWS)], core_recv, core_sems, (0,), sibling)
    first = []
    second = {}
    kept = {}

    def keep(chunk, half):
        copy = pltpu.make_async_copy(
            sources[half].at[chunk, (dom, y * 8 + z * 2 + core)[half]],
            lands[half].at[chunk, 0, 0, 0], own_sem.at[chunk, half],
        )
        copy.start()
        return copy

    for chunk in range(CHUNKS):
        first.append(first_phase(chunk, sources, relays, send1, recv1))
        for half in range(2):
            second[chunk, half, 0] = second_phase(chunk, half, 0, sources, relays, lands, send2, recv2)
            kept[chunk, half] = keep(chunk, half)

    core_copy.wait()
    core_sum[...] = (grads_ref[core_mine, :].astype(F32) + core_recv[...].astype(F32)).astype(BF16)
    x_copies = scatter(0, core_sum, x_recv, x_sems, X_ROWS)

    block_of = lax.broadcasted_iota(jnp.int32, (256, 256), 0) // 16
    same_row = lax.rem(lax.broadcasted_iota(jnp.int32, (256, 256), 0), 16) == lax.rem(
        lax.broadcasted_iota(jnp.int32, (256, 256), 1), 16
    )
    slot_of = lax.broadcasted_iota(jnp.int32, (1, 256), 1) // 16
    for half in range(2):
        for group in range(4):
            names = jnp.zeros((1, 256), jnp.int32)
            for step in range(4):
                for flip in range(2):
                    source = origin(half, group, step, flip)
                    for slot in range(2):
                        names = jnp.where(
                            slot_of == step * 4 + flip * 2 + slot, wanted_ref[source, 0, slot], names
                        )
            chosen[half, group] = jnp.logical_and(names == block_of, same_row).astype(F32).astype(BF16)

    def forward(chunk):
        for half, step, copy in first[chunk]:
            copy.wait()
            second[chunk, half, step] = second_phase(chunk, half, step, sources, relays, lands, send2, recv2)
            lands[half][chunk, step, 0, 0] = relays[half][chunk, step - 1, (y, z)[half] * 2 + core]

    def combine(chunk, group):
        for half in range(2):
            finish(second[chunk, half, group])
            if group == 0:
                kept[chunk, half].wait()
            for top in range(0, SPAN, 16):
                rows = slice((2 * chunk + half) * SPAN + top, (2 * chunk + half) * SPAN + top + 16)
                arrived = lands[half][chunk, group, :, :, :, top : top + 16, :].reshape(256, D)
                added = nn(chosen[half, group], arrived).reshape(PART, 16, D)
                if group == 0:
                    acc[:, rows, :] = near_ref[:, rows, :] + added
                else:
                    acc[:, rows, :] += added

    def cross(chunk):
        rows = slice(2 * chunk * SPAN, 2 * (chunk + 1) * SPAN)
        cross_send[chunk] = acc[:, rows, :].astype(BF16)
        copies = []
        for step in range(1, N_NODE):
            other = four(node + step)
            copies.append(
                push(
                    cross_send.at[chunk, pl.ds(other * ROWS, ROWS)], cross_ref.at[step - 1, chunk],
                    cross_sems, (chunk, step - 1), (dom, other),
                )
            )
        return copies

    forward(0)
    finish(x_copies)
    add_up(0, core_sum, x_recv, x_sum, X_ROWS)
    z_copies = scatter(1, x_sum, z_recv, z_sems, Z_ROWS)
    for chunk in range(1, CHUNKS):
        forward(chunk)
    finish(z_copies)
    add_up(1, x_sum, z_recv, z_sum, Z_ROWS)
    y_copies = scatter(2, z_sum, y_recv, y_sems, Y_ROWS)
    combine(0, 0)
    finish(y_copies)
    add_up(2, z_sum, y_recv, y_sum, Y_ROWS)
    y_copies = gather(2, y_sum, z_all, y_sems, Y_ROWS)
    combine(0, 1)
    finish(y_copies)
    z_copies = gather(1, z_all, x_all, z_sems, Z_ROWS)
    combine(0, 2)
    finish(z_copies)
    my_part = sum_ref.at[core_mine]
    x_copies = gather(0, x_all, my_part, x_sems, X_ROWS)
    combine(0, 3)
    crossing = cross(0)
    finish(x_copies)
    core_copy = push(my_part, my_part, core_sems, (1,), sibling)
    for chunk in range(1, CHUNKS):
        for group in range(4):
            combine(chunk, group)
        crossing += cross(chunk)
    own_ref[...] = acc[pl.ds(node * ROWS, ROWS)]
    core_copy.wait()
    finish(crossing)


def finish_kernel(factor, rows_ref, own_ref, cross_ref, sum_ref, dx_ref, gq, gk, gv, go, ge, gr):
    for row in range(ROWS):
        for chunk in range(CHUNKS):
            rows = slice(2 * chunk * SPAN, 2 * (chunk + 1) * SPAN)
            span = slice(row * BLK + rows.start, row * BLK + rows.stop)
            total = rows_ref[span, :] + own_ref[row, rows, :]
            for step in range(N_NODE - 1):
                total = total + cross_ref[step, chunk, row].astype(F32)
            dx_ref[span, :] = total.astype(BF16)

    def piece(index):
        return sum_ref[index * D : (index + 1) * D, :].astype(F32) * factor

    for half in range(2):
        span = slice(half * BLK, (half + 1) * BLK)
        gq[:, span] = piece(half)
        gk[span, :] = piece(2 + half).T
        gv[span, :] = piece(4 + half).T
        go[:, span] = piece(6 + half)
    for part in range(8):
        span = slice(part * BLK, (part + 1) * BLK)
        ge[:, span] = piece(8 + part)
        gr[span, :] = piece(16 + part).T


def vmem(shape, dtype):
    return pltpu.VMEM(shape, dtype)


IN_VMEM = pl.BlockSpec(memory_space=pltpu.VMEM)
IN_SMEM = pl.BlockSpec(memory_space=pltpu.SMEM)
ANYWHERE = pl.BlockSpec(memory_space=pl.ANY)


def on_device(
    features, w_query, w_key, w_value, w_out, w_expand, w_reduce, gain_attn, gain_ffn,
    tile_mask, local_block, remote_slot, remote_block, d_out,
):
    rows = features.shape[0]
    dma = pltpu.SemaphoreType.DMA
    peers = len(OFFSETS)
    land = (CHUNKS, 4, 4, 2, 2, SPAN, D)
    staged = (CHUNKS, N_DOM, 2, SPAN, D)
    relay = (CHUNKS, 3, 8, 2, SPAN, D)
    phase_sems = [dma((CHUNKS, 2, 3)), dma((CHUNKS, 2, 3)), dma((CHUNKS, 2, 4, 4, 2)), dma((CHUNKS, 2, 4, 4, 2))]
    part_0, part_1, land_a, land_b, wanted, bias = pl.pallas_call(
        exchange_kernel,
        out_shape=(
            jax.ShapeDtypeStruct((PART, 2 * SPAN, D), BF16),
            jax.ShapeDtypeStruct((PART, 2 * SPAN, D), BF16),
            jax.ShapeDtypeStruct(land, BF16),
            jax.ShapeDtypeStruct(land, BF16),
            jax.ShapeDtypeStruct((N_DOM, 1, BLK), jnp.int32),
            jax.ShapeDtypeStruct((rows, KEYS), BF16),
        ),
        in_specs=[IN_VMEM, IN_SMEM, IN_VMEM],
        out_specs=(IN_VMEM, IN_VMEM, ANYWHERE, ANYWHERE, IN_VMEM, IN_VMEM),
        scratch_shapes=[
            vmem((N_DOM, 1, BLK), jnp.int32), vmem(staged, BF16), vmem(staged, BF16),
            vmem(relay, BF16), vmem(relay, BF16), pltpu.SMEM((N_DOM, 1, BLK), jnp.int32),
            dma((CHUNKS, N_NODE - 1)), dma((CHUNKS, N_NODE - 1)), dma((peers,)), dma((peers,)),
        ]
        + phase_sems
        + [dma((CHUNKS, 2, 4)), dma],
        compiler_params=pltpu.CompilerParams(
            collective_id=1, has_side_effects=True, vmem_limit_bytes=VMEM_LIMIT
        ),
        name="exchange",
    )(features.reshape(ROWS, BLK, D), remote_block.reshape(1, 2 * N_DOM), jnp.transpose(tile_mask, (1, 0, 2)))

    output, back_a, back_b, near, d_rows, grads = pl.pallas_call(
        layer_kernel,
        out_shape=(
            jax.ShapeDtypeStruct((rows, D), BF16),
            jax.ShapeDtypeStruct(staged, BF16),
            jax.ShapeDtypeStruct(staged, BF16),
            jax.ShapeDtypeStruct((PART, BLK, D), F32),
            jax.ShapeDtypeStruct((rows, D), F32),
            jax.ShapeDtypeStruct((SUM_ROWS, BLK), BF16),
        ),
        in_specs=[IN_SMEM, IN_SMEM, IN_VMEM, IN_VMEM, IN_VMEM, ANYWHERE, ANYWHERE] + [IN_VMEM] * 10,
        out_specs=(IN_VMEM,) * 6,
        scratch_shapes=[
            vmem((ROWS, KEYS, D), BF16), vmem((ROWS, KEYS, D), BF16), vmem((ROWS, KEYS, D), BF16),
            vmem((rows, D), BF16), vmem((ROWS, HEADS * BLK, KEYS), BF16), vmem((rows, D), F32),
            vmem((rows, D), BF16), vmem((rows, D), F32), vmem((2 * D, D), F32), vmem((D, D), F32),
            vmem((D, 4 * D), F32), vmem((D, 4 * D), F32), vmem((D, D), F32), dma((16, CHUNKS, 2)),
        ],
        compiler_params=pltpu.CompilerParams(vmem_limit_bytes=VMEM_LIMIT),
        name="layer",
    )(
        local_block.T, remote_slot, features, part_0, part_1, land_a, land_b, bias, d_out,
        w_query, w_key, w_value, w_out, w_expand, w_reduce, gain_attn.reshape(1, D), gain_ffn.reshape(1, D),
    )

    own, cross, summed = pl.pallas_call(
        return_kernel,
        out_shape=(
            jax.ShapeDtypeStruct((ROWS, BLK, D), F32),
            jax.ShapeDtypeStruct((N_NODE - 1, CHUNKS, ROWS, 2 * SPAN, D), BF16),
            jax.ShapeDtypeStruct((SUM_ROWS, BLK), BF16),
        ),
        in_specs=[IN_SMEM, ANYWHERE, ANYWHERE, IN_VMEM, IN_VMEM],
        out_specs=(IN_VMEM,) * 3,
        scratch_shapes=[
            vmem(relay, BF16), vmem(relay, BF16), vmem(land, BF16), vmem(land, BF16),
            vmem((PART, BLK, D), F32), vmem((2, 4, 256, 256), BF16), vmem((CHUNKS, PART, 2 * SPAN, D), BF16),
            vmem((CORE_ROWS, BLK), BF16), vmem((CORE_ROWS, BLK), BF16),
            vmem((3, X_ROWS, BLK), BF16), vmem((X_ROWS, BLK), BF16),
            vmem((3, Z_ROWS, BLK), BF16), vmem((Z_ROWS, BLK), BF16),
            vmem((3, Y_ROWS, BLK), BF16), vmem((Y_ROWS, BLK), BF16),
            vmem((Z_ROWS, BLK), BF16), vmem((X_ROWS, BLK), BF16),
        ]
        + phase_sems
        + [dma((CHUNKS, 2)), dma((2, CHUNKS, 3)), dma((2, 2)), dma((2, 2, 3)), dma((2, 2, 3)), dma((2, 2, 3))],
        compiler_params=pltpu.CompilerParams(
            collective_id=2, has_side_effects=True, vmem_limit_bytes=VMEM_LIMIT
        ),
        name="give_back",
    )(wanted, back_a, back_b, near, grads)

    factor = 1.0 / math.sqrt(rows * N_DOM * N_NODE)
    finished = pl.pallas_call(
        functools.partial(finish_kernel, factor),
        out_shape=(
            jax.ShapeDtypeStruct((rows, D), BF16),
            jax.ShapeDtypeStruct((D, D), F32),
            jax.ShapeDtypeStruct((D, D), F32),
            jax.ShapeDtypeStruct((D, D), F32),
            jax.ShapeDtypeStruct((D, D), F32),
            jax.ShapeDtypeStruct((D, 4 * D), F32),
            jax.ShapeDtypeStruct((4 * D, D), F32),
        ),
        in_specs=[IN_VMEM] * 4,
        out_specs=(IN_VMEM,) * 7,
        compiler_params=pltpu.CompilerParams(vmem_limit_bytes=VMEM_LIMIT),
        name="finish",
    )(d_rows, own, cross, summed)
    return (output,) + tuple(finished)


def solution(mesh):
    split = P(("dom", "node"), None)
    placed = (
        (split,) + (P(),) * 8 + (P(("dom", "node"), None, None), split, split, P("dom", "node", None), split)
    )
    return jax.shard_map(
        on_device, mesh=mesh, in_specs=placed, out_specs=(split, split) + (P(),) * 6, check_vma=False
    )
```

```python
import functools
import math

import jax
import jax.numpy as jnp
from jax import lax
from jax.experimental import pallas as pl
from jax.experimental.pallas import tpu as pltpu
from jax.sharding import PartitionSpec as P

HEADS = 8
EPSILON = 1e-05
MESH = pl.DeviceIdType.MESH
F32 = jnp.float32
BF16 = jnp.bfloat16
NEG = -1e30
VMEM_LIMIT = 60 << 20

D = 256
BLK = 128
TILES = 7
NEAR = 3
ROWS = 4
PART = 16
KEYS = TILES * BLK
FAR = ROWS * (TILES - NEAR)
N_DOM = 32
N_NODE = 4
CHUNKS = 2
SPAN = BLK // (2 * CHUNKS)

_GROUPS = [
    [(2, 2)],
    [(2, 1), (2, 3)],
    [(1, 2), (3, 2)],
    [(1, 1), (3, 3)],
    [(1, 3), (3, 1)],
    [(2, 0), (0, 2)],
    [(1, 0), (3, 0), (0, 1), (0, 3)],
]
OFFSETS = [(a, b, c) for group in _GROUPS for c in range(2) for a, b in group] + [(0, 0, 1)]


def dom_peer(dom, offset, sign=1):
    core = lax.rem(dom, 2)
    y = lax.rem(dom // 2, 4)
    z = dom // 8
    dz, dy, dc = offset
    return (
        lax.rem(z + (dz if sign > 0 else 4 - dz), 4) * 8
        + lax.rem(y + (dy if sign > 0 else 4 - dy), 4) * 2
        + lax.rem(core + dc, 2)
    )


def nt(a, b):
    return lax.dot_general(a, b, (((1,), (1,)), ((), ())), preferred_element_type=F32)


def tn(a, b):
    return lax.dot_general(a, b, (((0,), (0,)), ((), ())), preferred_element_type=F32)


def nn(a, b):
    return jnp.dot(a, b, preferred_element_type=F32)


def place():
    dom = lax.axis_index("dom")
    return dom // 8, lax.rem(dom // 2, 4), lax.rem(dom, 2), lax.axis_index("node")


def device(z, y, core, node):
    return (z * 8 + y * 2 + core, node)


def four(value):
    return lax.rem(value, 4)


def two(value):
    return lax.rem(value, 2)


def first_phase(chunk, sources, relays, sends, recvs):
    z, y, core, node = place()
    copies = []
    for step in range(1, 4):
        for half in range(2):
            target = four((z, y)[half] + step)
            copy = pltpu.make_async_remote_copy(
                src_ref=sources[half].at[chunk, pl.ds(target * 8, 8)],
                dst_ref=relays[half].at[chunk, step - 1],
                send_sem=sends.at[chunk, half, step - 1], recv_sem=recvs.at[chunk, half, step - 1],
                device_id=(device(target, y, core, node), device(z, target, core, node))[half],
                device_id_type=MESH,
            )
            copy.start()
            copies.append((half, step, copy))
    return copies


def second_phase(chunk, half, group, sources, relays, lands, sends, recvs):
    z, y, core, node = place()
    copies = []
    for step in range(4):
        for flip in range(2):
            if step == 0 and flip == 0:
                continue
            target = four((y, z)[half] + step)
            side = two(core + flip)
            if group == 0:
                source = sources[half].at[chunk, (z, y)[half] * 8 + target * 2 + side]
            else:
                source = relays[half].at[chunk, group - 1, target * 2 + side]
            copy = pltpu.make_async_remote_copy(
                src_ref=source, dst_ref=lands[half].at[chunk, group, step, flip],
                send_sem=sends.at[chunk, half, group, step, flip],
                recv_sem=recvs.at[chunk, half, group, step, flip],
                device_id=(device(z, target, side, node), device(target, y, side, node))[half],
                device_id_type=MESH,
            )
            copy.start()
            copies.append(copy)
    return copies


def origin(half, group, step, flip):
    z, y, core, node = place()
    far, near = 4 - group, 4 - step
    if half == 0:
        return four(z + far) * 8 + four(y + near) * 2 + two(core + flip)
    return four(z + near) * 8 + four(y + far) * 2 + two(core + flip)


def exchange_kernel(
    feat_ref, table_ref, slot_ref, mask_ref, part_0, part_1, land_a, land_b, wanted_ref, bias_ref, tile_ref,
    ids, stage_a, stage_b, relay_a, relay_b, ids_smem,
    near_send, near_recv, id_send, id_recv, send1, recv1, send2, recv2, own_sem, local_sem,
):
    dom = lax.axis_index("dom")
    z, y, core, node = place()
    stages, relays, lands = (stage_a, stage_b), (relay_a, relay_b), (land_a, land_b)
    parts = (part_0, part_1)
    barrier = pltpu.get_barrier_semaphore()
    for offset in OFFSETS:
        pl.semaphore_signal(barrier, inc=1, device_id=(dom_peer(dom, offset), node), device_id_type=MESH)
    for step in range(1, N_NODE):
        pl.semaphore_signal(
            barrier, inc=1, device_id=(dom, lax.rem(node + step, N_NODE)), device_id_type=MESH
        )
    lane = lax.broadcasted_iota(jnp.int32, (1, BLK), 1)
    for peer in range(N_DOM):
        ids[peer] = jnp.where(
            lane == 0, table_ref[0, 2 * peer], jnp.where(lane == 1, table_ref[0, 2 * peer + 1], 0)
        )
    pl.semaphore_wait(barrier, len(OFFSETS) + N_NODE - 1)

    id_copies = []
    for index, offset in enumerate(OFFSETS):
        peer = dom_peer(dom, offset)
        copy = pltpu.make_async_remote_copy(
            src_ref=ids.at[peer], dst_ref=wanted_ref.at[dom],
            send_sem=id_send.at[index], recv_sem=id_recv.at[index],
            device_id=(peer, node), device_id_type=MESH,
        )
        copy.start()
        id_copies.append(copy)
    near_copies = []
    for chunk in range(CHUNKS):
        for step in range(1, N_NODE):
            copy = pltpu.make_async_remote_copy(
                src_ref=feat_ref.at[:, pl.ds(chunk * 2 * SPAN, 2 * SPAN)],
                dst_ref=parts[chunk].at[pl.ds(node * ROWS, ROWS)],
                send_sem=near_send.at[chunk, step - 1], recv_sem=near_recv.at[chunk, step - 1],
                device_id=(dom, lax.rem(node + step, N_NODE)), device_id_type=MESH,
            )
            copy.start()
            near_copies.append(copy)
    for chunk in range(CHUNKS):
        parts[chunk][pl.ds(node * ROWS, ROWS)] = feat_ref[:, chunk * 2 * SPAN : (chunk + 1) * 2 * SPAN]
    wanted_ref[dom] = ids[dom]
    for copy in id_copies:
        copy.wait()
    to_smem = pltpu.make_async_copy(wanted_ref, ids_smem, local_sem)
    to_smem.start()
    to_smem.wait()

    def stage(chunk):
        def body(peer, carry):
            turned = lax.rem(peer // 2, 4) * 8 + (peer // 8) * 2 + lax.rem(peer, 2)
            for slot in range(2):
                block = ids_smem[peer, 0, slot]
                stage_a[chunk, peer, slot] = parts[chunk][block, 0:SPAN]
                stage_b[chunk, turned, slot] = parts[chunk][block, SPAN : 2 * SPAN]
            return carry

        lax.fori_loop(0, N_DOM, body, 0)

    def keep(chunk, half, group):
        if group == 0:
            source = stages[half].at[chunk, (dom, y * 8 + z * 2 + core)[half]]
        else:
            source = relays[half].at[chunk, group - 1, (y, z)[half] * 2 + core]
        copy = pltpu.make_async_copy(
            source, lands[half].at[chunk, group, 0, 0], own_sem.at[chunk, half, group]
        )
        copy.start()
        return copy

    first = []
    second = []
    kept = []
    for chunk in range(CHUNKS):
        for copy in near_copies[chunk * (N_NODE - 1) : (chunk + 1) * (N_NODE - 1)]:
            copy.wait()
        stage(chunk)
        first.append(first_phase(chunk, stages, relays, send1, recv1))
        for half in range(2):
            second += second_phase(chunk, half, 0, stages, relays, lands, send2, recv2)
            kept.append(keep(chunk, half, 0))

    def to_bias(row, carry):
        start = pl.multiple_of(row * BLK, BLK)
        diagonal = lax.broadcasted_iota(jnp.int32, (BLK, BLK), 0) == lax.broadcasted_iota(
            jnp.int32, (BLK, BLK), 1
        )
        for tile in range(TILES):
            allowed = mask_ref[tile, pl.ds(start, BLK), :] > 0
            if tile == 0:
                allowed = jnp.logical_or(allowed, diagonal)
            bias_ref[pl.ds(start, BLK), tile * BLK : (tile + 1) * BLK] = jnp.where(
                allowed, 0.0, NEG
            ).astype(BF16)
        return carry

    lax.fori_loop(0, ROWS, to_bias, 0)

    def tile_of(slot, carry):
        found = jnp.int32(FAR)
        for row in range(ROWS):
            for tile in range(TILES - NEAR):
                found = jnp.where(slot_ref[row, tile] == slot, row * (TILES - NEAR) + tile, found)
        tile_ref[0, slot] = found
        return carry

    lax.fori_loop(0, 2 * N_DOM, tile_of, 0)
    for chunk in range(CHUNKS):
        for half, step, copy in first[chunk]:
            copy.wait()
            second += second_phase(chunk, half, step, stages, relays, lands, send2, recv2)
            kept.append(keep(chunk, half, step))
    for copy in kept:
        copy.wait()
    for copy in second:
        copy.wait()


SUM_ROWS = (4096, 2048)


def rows_at(index, size):
    return pl.ds(pl.multiple_of(index * size, size), size)


def layer_kernel(
    local_ref, slot_ref, tile_ref, wanted_ref, feat_ref, part_0, part_1, far_a, far_b, bias_ref, d_out_ref,
    wq_ref, wk_ref, wv_ref, wo_ref, we_ref, wr_ref, gain_a_ref, gain_f_ref,
    out_ref, base_ref, cross_ref, sum_0, sum_1,
    fs, ks, vs, qs, ps, mixed, d_mixed, d_query, far_keys_t, far_values_t, near_keys_t, near_values_t,
    far_tiles, near_tiles, pair_acc, query_acc, expand_acc, reduce_acc, out_acc,
    grads_0, grads_1, stage_a, stage_b, relay_a, relay_b, land_a, land_b, acc, chosen, cross_send,
    core_recv_0, core_sum_0, x_recv_0, x_sum_0, spot_recv_0, spot_sum_0, x_all_0,
    core_recv_1, core_sum_1, x_recv_1, x_sum_1, spot_recv_1, spot_sum_1, x_all_1,
    send1, recv1, send2, recv2, cross_sems, core_sems, x_sems, spot_sems,
):
    dom = lax.axis_index("dom")
    z, y, core, node = place()
    sources, relays, lands = (stage_a, stage_b), (relay_a, relay_b), (land_a, land_b)
    barrier = pltpu.get_barrier_semaphore()
    peers = [(dom_peer(dom, offset), node) for offset in OFFSETS]
    peers += [(dom, four(node + step)) for step in range(1, N_NODE)]
    for peer in peers:
        pl.semaphore_signal(barrier, inc=1, device_id=peer, device_id_type=MESH)

    scale = 1.0 / math.sqrt(D // HEADS)
    log2e = math.log2(math.e)
    expand_acc[...] = jnp.zeros(expand_acc.shape, F32)
    reduce_acc[...] = jnp.zeros(reduce_acc.shape, F32)
    out_acc[...] = jnp.zeros(out_acc.shape, F32)
    qs[...] = nn(feat_ref[...], wq_ref[...]).astype(BF16)
    lane_head = lax.broadcasted_iota(jnp.int32, (1, D), 1) // (D // HEADS)
    head_f32 = [(lane_head == h).astype(F32) for h in range(HEADS)]
    head_low = [mask.astype(BF16) for mask in head_f32]

    def forward_row(row, carry):
        start = pl.multiple_of(row * BLK, BLK)
        fs[row, 0:BLK] = feat_ref[pl.ds(start, BLK), :]
        for tile in range(NEAR - 1):
            block = local_ref[tile, row]
            for chunk, part_ref in enumerate((part_0, part_1)):
                top = (tile + 1) * BLK + chunk * 2 * SPAN
                fs[row, top : top + 2 * SPAN] = part_ref[block]
        for tile in range(TILES - NEAR):
            slot = slot_ref[row, tile]
            asked = slot // 2
            dz = four(z + 4 - asked // 8)
            dy = four(y + 4 - four(asked // 2))
            dc = two(core + two(asked))
            for chunk in range(CHUNKS):
                top = (NEAR + tile) * BLK + 2 * chunk * SPAN
                fs[row, top : top + SPAN] = far_a[chunk, dz, dy, dc, two(slot)]
                fs[row, top + SPAN : top + 2 * SPAN] = far_b[chunk, dy, dz, dc, two(slot)]
        tile_rows = fs[row]
        keys = nn(tile_rows, wk_ref[...]).astype(BF16)
        ks[row] = keys
        values = nn(tile_rows, wv_ref[...]).astype(BF16)
        vs[row] = values
        query = qs[pl.ds(start, BLK), :]
        bias = bias_ref[pl.ds(start, BLK), :].astype(F32)
        total = jnp.zeros((BLK, D), F32)
        for pair in range(HEADS // 2):
            both = jnp.concatenate([query * head_low[2 * pair], query * head_low[2 * pair + 1]], 0)
            scores = nt(both, keys) * (scale * log2e)
            for half in range(2):
                mine = scores[half * BLK : (half + 1) * BLK] + bias
                top = jnp.max(mine, -1, keepdims=True)
                weight = jnp.exp2(mine - top)
                norm = 1.0 / jnp.sum(weight, -1, keepdims=True)
                ps[row, (2 * pair + half) * BLK : (2 * pair + half + 1) * BLK, :] = (weight * norm).astype(BF16)
            got = nn(ps[row, 2 * pair * BLK : (2 * pair + 2) * BLK, :], values)
            total = total + got[:BLK] * head_f32[2 * pair] + got[BLK:] * head_f32[2 * pair + 1]
        mixed[pl.ds(start, BLK), :] = total
        return carry

    lax.fori_loop(0, ROWS, forward_row, 0)

    size = 256

    def feed(step, carry):
        start = pl.multiple_of(step * size, size)
        sel = pl.ds(start, size)
        mixed_low = mixed[sel, :].astype(BF16)
        gain_a = gain_a_ref[...]
        gain_f = gain_f_ref[...]
        residual = feat_ref[sel, :].astype(F32) + nn(mixed_low, wo_ref[...])
        center = residual - jnp.mean(residual, -1, keepdims=True)
        rstd_a = lax.rsqrt(jnp.mean(center * center, -1, keepdims=True) + EPSILON)
        hat_a = center * rstd_a
        first_low = (hat_a * gain_a).astype(BF16)
        pre = nn(first_low, we_ref[...])
        root = math.sqrt(2.0 / math.pi)
        square = pre * pre
        tanh = jnp.tanh(root * (pre + 0.044715 * (square * pre)))
        half = 0.5 * (1.0 + tanh)
        act_low = (pre * half).astype(BF16)
        slope = half + 0.5 * pre * (1.0 - tanh * tanh) * (root * (1.0 + 3.0 * 0.044715 * square))
        second = first_low.astype(F32) + nn(act_low, wr_ref[...])
        center = second - jnp.mean(second, -1, keepdims=True)
        rstd_f = lax.rsqrt(jnp.mean(center * center, -1, keepdims=True) + EPSILON)
        hat_f = center * rstd_f
        out_ref[sel, :] = (hat_f * gain_f).astype(BF16)
        d_hat = d_out_ref[sel, :].astype(F32) * gain_f
        d_second = rstd_f * (
            d_hat - jnp.mean(d_hat, -1, keepdims=True) - hat_f * jnp.mean(d_hat * hat_f, -1, keepdims=True)
        )
        d_second_low = d_second.astype(BF16)
        reduce_acc[...] += tn(d_second_low, act_low)
        d_pre_low = (nt(d_second_low, wr_ref[...]) * slope).astype(BF16)
        expand_acc[...] += tn(first_low, d_pre_low)
        d_first = d_second + nt(d_pre_low, we_ref[...])
        d_hat = d_first * gain_a
        d_resid = rstd_a * (
            d_hat - jnp.mean(d_hat, -1, keepdims=True) - hat_a * jnp.mean(d_hat * hat_a, -1, keepdims=True)
        )
        base_ref[sel, :] = d_resid
        d_resid_low = d_resid.astype(BF16)
        out_acc[...] += tn(mixed_low, d_resid_low)
        d_mixed[sel, :] = nt(d_resid_low, wo_ref[...]).astype(BF16)
        return carry

    lax.fori_loop(0, ROWS * BLK // size, feed, 0)

    def pack(accs, grads):
        spot = 0
        for total in accs:
            for top in range(0, total.shape[0], D):
                for left in range(0, total.shape[1], BLK):
                    grads[spot : spot + D, :] = total[top : top + D, left : left + BLK].astype(BF16)
                    spot += D

    def push(src, dst, sems, key, target):
        copy = pltpu.make_async_remote_copy(
            src_ref=src, dst_ref=dst, send_sem=sems.at[(0,) + key], recv_sem=sems.at[(1,) + key],
            device_id=target, device_id_type=MESH,
        )
        copy.start()
        return copy

    def finish(copies):
        for copy in copies:
            copy.wait()

    spot_here = z * 4 + y
    x_line = [four(node + step) for step in range(1, 4)]
    x_line = [(other, (dom, other)) for other in x_line]
    spots = [lax.rem(spot_here + step, 16) for step in range(1, 16)]
    spots = [(other, (other * 2 + core, node)) for other in spots]
    sibling = device(z, y, two(core + 1), node)

    def reduction(number, grads, total_ref, core_recv, core_sum, x_recv, x_sum, spot_recv, spot_sum, x_all):
        core_rows = SUM_ROWS[number] // 2
        x_rows = core_rows // 4
        spot_rows = x_rows // 16
        mine = rows_at(core, core_rows)

        def scatter(members, src, dst, sems, count):
            return [
                push(src.at[rows_at(other, count)], dst.at[index], sems, (number, 0, index), target)
                for index, (other, target) in enumerate(members)
            ]

        def gather(members, own, src, dst, sems, count):
            copies = [
                push(src, dst.at[rows_at(own, count)], sems, (number, 1, index), target)
                for index, (other, target) in enumerate(members)
            ]
            dst[rows_at(own, count), :] = src[...]
            return copies

        def add_up(own, src, recv, out, count):
            total = src[rows_at(own, count), :].astype(F32)
            for index in range(recv.shape[0]):
                total = total + recv[index].astype(F32)
            out[...] = total.astype(BF16)

        copy = push(grads.at[rows_at(two(core + 1), core_rows)], core_recv, core_sems, (number, 0), sibling)
        yield
        copy.wait()
        core_sum[...] = (grads[mine, :].astype(F32) + core_recv[...].astype(F32)).astype(BF16)
        copies = scatter(x_line, core_sum, x_recv, x_sems, x_rows)
        yield
        finish(copies)
        add_up(node, core_sum, x_recv, x_sum, x_rows)
        copies = scatter(spots, x_sum, spot_recv, spot_sems, spot_rows)
        yield
        finish(copies)
        add_up(spot_here, x_sum, spot_recv, spot_sum, spot_rows)
        copies = gather(spots, spot_here, spot_sum, x_all, spot_sems, spot_rows)
        yield
        finish(copies)
        my_part = total_ref.at[mine]
        copies = gather(x_line, node, x_all, my_part, x_sems, x_rows)
        yield
        finish(copies)
        copy = push(my_part, my_part, core_sems, (number, 1), sibling)
        yield
        copy.wait()
        yield

    first_half = lax.broadcasted_iota(jnp.int32, (64, BLK), 0) < 32

    def block_diagonal(turned, pair):
        piece = turned[64 * pair : 64 * pair + 64]
        return jnp.concatenate(
            [jnp.where(first_half, piece, 0.0), jnp.where(first_half, 0.0, piece)], 1
        ).astype(BF16)

    def backward(row, begin, end):
        start = pl.multiple_of(row * BLK, BLK)
        keys = ks[row, begin:end]
        values = vs[row, begin:end]
        query = qs[pl.ds(start, BLK), :]
        grad = d_mixed[pl.ds(start, BLK), :]
        query_t = query.astype(F32).T
        grad_t = grad.astype(F32).T
        inner_full = grad.astype(F32) * mixed[pl.ds(start, BLK), :]
        query_part = jnp.zeros((BLK, D), F32)
        key_parts = []
        value_parts = []
        for pair in range(HEADS // 2):
            both = jnp.concatenate([grad * head_low[2 * pair], grad * head_low[2 * pair + 1]], 0)
            inner = jnp.concatenate(
                [
                    jnp.sum(inner_full * head_f32[2 * pair], -1, keepdims=True),
                    jnp.sum(inner_full * head_f32[2 * pair + 1], -1, keepdims=True),
                ],
                0,
            )
            probs_low = ps[row, 2 * pair * BLK : (2 * pair + 2) * BLK, begin:end]
            d_probs = nt(both, values)
            d_scores = (probs_low.astype(F32) * ((d_probs - inner) * scale)).astype(BF16)
            got = nn(d_scores, keys)
            query_part = query_part + got[:BLK] * head_f32[2 * pair] + got[BLK:] * head_f32[2 * pair + 1]
            key_parts.append(nn(block_diagonal(query_t, pair), d_scores).astype(BF16))
            value_parts.append(nn(block_diagonal(grad_t, pair), probs_low).astype(BF16))
        d_keys_t = jnp.concatenate(key_parts, 0)
        d_values_t = jnp.concatenate(value_parts, 0)
        return d_keys_t, d_values_t, nn(wk_ref[...], d_keys_t) + nn(wv_ref[...], d_values_t), query_part

    def backward_far(row, carry):
        d_keys_t, d_values_t, d_rows_t, query_part = backward(row, NEAR * BLK, KEYS)
        far_keys_t[row] = d_keys_t
        far_values_t[row] = d_values_t
        d_query[rows_at(row, BLK), :] = query_part
        for tile in range(TILES - NEAR):
            piece = d_rows_t[:, tile * BLK : (tile + 1) * BLK].T
            far_tiles[row * (TILES - NEAR) + tile] = piece.astype(BF16)
        return carry

    def backward_near(row, carry):
        d_keys_t, d_values_t, d_rows_t, query_part = backward(row, 0, NEAR * BLK)
        near_keys_t[row] = d_keys_t
        near_values_t[row] = d_values_t
        d_query[rows_at(row, BLK), :] += query_part
        for tile in range(NEAR):
            piece = d_rows_t[:, tile * BLK : (tile + 1) * BLK].T
            near_tiles[row * NEAR + tile] = piece.astype(BF16)
        return carry

    def key_grads(row, carry):
        near_rows = fs[row, : NEAR * BLK]
        far_rows = fs[row, NEAR * BLK :]
        pair_acc[0:D, :] += nn(near_keys_t[row], near_rows) + nn(far_keys_t[row], far_rows)
        pair_acc[D : 2 * D, :] += nn(near_values_t[row], near_rows) + nn(far_values_t[row], far_rows)
        return carry

    def stage(chunk):
        def body(peer, carry):
            turned = four(peer // 2) * 8 + (peer // 8) * 2 + two(peer)
            for slot in range(2):
                tile = tile_ref[0, 2 * peer + slot]
                top = 2 * chunk * SPAN
                stage_a[chunk, peer, slot] = far_tiles[tile, top : top + SPAN]
                stage_b[chunk, turned, slot] = far_tiles[tile, top + SPAN : top + 2 * SPAN]
            return carry

        lax.fori_loop(0, N_DOM, body, 0)

    block_of = lax.broadcasted_iota(jnp.int32, (256, 256), 0) // 16
    same_row = lax.rem(lax.broadcasted_iota(jnp.int32, (256, 256), 0), 16) == lax.rem(
        lax.broadcasted_iota(jnp.int32, (256, 256), 1), 16
    )
    slot_of = lax.broadcasted_iota(jnp.int32, (1, 256), 1) // 16

    def selection(values):
        names = jnp.full((1, 256), -1, jnp.int32)
        for index, value in enumerate(values):
            names = jnp.where(slot_of == index, value, names)
        return jnp.logical_and(names == block_of, same_row).astype(F32).astype(BF16)

    def relay_on(chunk):
        for half, step, copy in first[chunk]:
            copy.wait()
            second[chunk, half, step] = second_phase(chunk, half, step, sources, relays, lands, send2, recv2)
            lands[half][chunk, step, 0, 0] = relays[half][chunk, step - 1, (y, z)[half] * 2 + core]

    def combine(chunk, group):
        for half in range(2):
            finish(second[chunk, half, group])
            for top in range(0, SPAN, 16):
                rows = slice((2 * chunk + half) * SPAN + top, (2 * chunk + half) * SPAN + top + 16)
                arrived = lands[half][chunk, group, :, :, :, top : top + 16, :].reshape(256, D)
                acc[:, rows, :] += nn(chosen[half, group], arrived).reshape(PART, 16, D)

    def cross(chunk):
        rows = slice(2 * chunk * SPAN, 2 * (chunk + 1) * SPAN)
        cross_send[chunk] = acc[:, rows, :].astype(BF16)
        copies = []
        for step in range(1, N_NODE):
            other = four(node + step)
            copies.append(
                push(
                    cross_send.at[chunk, pl.ds(other * ROWS, ROWS)], cross_ref.at[step - 1, chunk],
                    cross_sems, (chunk, step - 1), (dom, other),
                )
            )
        return copies

    pack((expand_acc, reduce_acc), grads_0)
    pl.semaphore_wait(barrier, len(peers))
    wide = reduction(
        0, grads_0, sum_0, core_recv_0, core_sum_0, x_recv_0, x_sum_0, spot_recv_0, spot_sum_0, x_all_0
    )
    next(wide)
    far_tiles[FAR] = jnp.zeros((BLK, D), BF16)
    lax.fori_loop(0, 2, backward_far, 0)
    next(wide)
    lax.fori_loop(2, ROWS, backward_far, 0)

    first = []
    second = {}
    for chunk in range(CHUNKS):
        stage(chunk)
        if chunk == 0:
            next(wide)
        first.append(first_phase(chunk, sources, relays, send1, recv1))
        for half in range(2):
            second[chunk, half, 0] = second_phase(chunk, half, 0, sources, relays, lands, send2, recv2)
            lands[half][chunk, 0, 0, 0] = sources[half][chunk, (dom, y * 8 + z * 2 + core)[half]]

    near_tiles[ROWS * NEAR : PART] = jnp.zeros((PART - ROWS * NEAR, BLK, D), BF16)
    lax.fori_loop(0, ROWS, backward_near, 0)
    pair_acc[...] = jnp.zeros(pair_acc.shape, F32)
    lax.fori_loop(0, ROWS, key_grads, 0)
    d_query_low = d_query[...].astype(BF16)
    query_acc[...] = tn(feat_ref[...], d_query_low)
    pack((query_acc, pair_acc, out_acc), grads_1)
    narrow = reduction(
        1, grads_1, sum_1, core_recv_1, core_sum_1, x_recv_1, x_sum_1, spot_recv_1, spot_sum_1, x_all_1
    )
    next(narrow)
    next(wide)
    base_ref[...] += nt(d_query_low, wq_ref[...])
    next(narrow)
    relay_on(0)
    next(narrow)
    next(wide)
    near_names = []
    for row in range(ROWS):
        near_names += [node * ROWS + row, local_ref[0, row], local_ref[1, row]]
    near_chosen = selection(near_names)
    for top in range(0, BLK, 16):
        rows = slice(top, top + 16)
        acc[:, rows, :] = nn(near_chosen, near_tiles[:, rows, :].reshape(256, D)).reshape(PART, 16, D)
    for half in range(2):
        for group in range(4):
            chosen[half, group] = selection(
                [
                    wanted_ref[origin(half, group, step, flip), 0, slot]
                    for step in range(4)
                    for flip in range(2)
                    for slot in range(2)
                ]
            )
    for chunk in range(1, CHUNKS):
        relay_on(chunk)
    combine(0, 0)
    combine(0, 1)
    next(narrow)
    next(wide)
    combine(0, 2)
    combine(0, 3)
    crossing = cross(0)
    next(narrow)
    next(wide)
    for chunk in range(1, CHUNKS):
        for group in range(4):
            combine(chunk, group)
        crossing += cross(chunk)
    next(narrow)
    base_ref[...] += acc[pl.ds(node * ROWS, ROWS)].reshape(ROWS * BLK, D)
    next(narrow)
    finish(crossing)


def finish_kernel(factor, result_ref, base_ref, cross_ref, sum_0, sum_1, out_ref, dx_ref, gq, gk, gv, go, ge, gr):
    out_ref[...] = result_ref[...]
    for row in range(ROWS):
        for chunk in range(CHUNKS):
            span = slice(row * BLK + 2 * chunk * SPAN, row * BLK + 2 * (chunk + 1) * SPAN)
            total = base_ref[span, :]
            for step in range(N_NODE - 1):
                total = total + cross_ref[step, chunk, row].astype(F32)
            dx_ref[span, :] = total.astype(BF16)

    def piece(ref, index):
        return ref[index * D : (index + 1) * D, :].astype(F32) * factor

    for half in range(2):
        span = slice(half * BLK, (half + 1) * BLK)
        gq[:, span] = piece(sum_1, half)
        gk[span, :] = piece(sum_1, 2 + half).T
        gv[span, :] = piece(sum_1, 4 + half).T
        go[:, span] = piece(sum_1, 6 + half)
    for part in range(8):
        span = slice(part * BLK, (part + 1) * BLK)
        ge[:, span] = piece(sum_0, part)
        gr[span, :] = piece(sum_0, 8 + part).T


def vmem(shape, dtype):
    return pltpu.VMEM(shape, dtype)


IN_VMEM = pl.BlockSpec(memory_space=pltpu.VMEM)
IN_SMEM = pl.BlockSpec(memory_space=pltpu.SMEM)
ANYWHERE = pl.BlockSpec(memory_space=pl.ANY)


def on_device(
    features, w_query, w_key, w_value, w_out, w_expand, w_reduce, gain_attn, gain_ffn,
    tile_mask, local_block, remote_slot, remote_block, d_out,
):
    rows = features.shape[0]
    dma = pltpu.SemaphoreType.DMA
    peers = len(OFFSETS)
    land = (CHUNKS, 4, 4, 2, 2, SPAN, D)
    staged = (CHUNKS, N_DOM, 2, SPAN, D)
    relay = (CHUNKS, 3, 8, 2, SPAN, D)
    phase_sems = [dma((CHUNKS, 2, 3)), dma((CHUNKS, 2, 3)), dma((CHUNKS, 2, 4, 4, 2)), dma((CHUNKS, 2, 4, 4, 2))]
    part_0, part_1, land_a, land_b, wanted, bias, tile_of = pl.pallas_call(
        exchange_kernel,
        out_shape=(
            jax.ShapeDtypeStruct((PART, 2 * SPAN, D), BF16),
            jax.ShapeDtypeStruct((PART, 2 * SPAN, D), BF16),
            jax.ShapeDtypeStruct(land, BF16),
            jax.ShapeDtypeStruct(land, BF16),
            jax.ShapeDtypeStruct((N_DOM, 1, BLK), jnp.int32),
            jax.ShapeDtypeStruct((rows, KEYS), BF16),
            jax.ShapeDtypeStruct((1, 2 * N_DOM), jnp.int32),
        ),
        in_specs=[IN_VMEM, IN_SMEM, IN_SMEM, IN_VMEM],
        out_specs=(IN_VMEM, IN_VMEM, ANYWHERE, ANYWHERE, IN_VMEM, IN_VMEM, IN_SMEM),
        scratch_shapes=[
            vmem((N_DOM, 1, BLK), jnp.int32), vmem(staged, BF16), vmem(staged, BF16),
            vmem(relay, BF16), vmem(relay, BF16), pltpu.SMEM((N_DOM, 1, BLK), jnp.int32),
            dma((CHUNKS, N_NODE - 1)), dma((CHUNKS, N_NODE - 1)), dma((peers,)), dma((peers,)),
        ]
        + phase_sems
        + [dma((CHUNKS, 2, 4)), dma],
        compiler_params=pltpu.CompilerParams(
            collective_id=1, has_side_effects=True, vmem_limit_bytes=VMEM_LIMIT
        ),
        name="exchange",
    )(features.reshape(ROWS, BLK, D), remote_block.reshape(1, 2 * N_DOM), remote_slot, jnp.transpose(tile_mask, (1, 0, 2)))

    sum_scratch = []
    for total in SUM_ROWS:
        half, eighth, spot = total // 2, total // 8, total // 128
        sum_scratch += [
            vmem((half, BLK), BF16), vmem((half, BLK), BF16), vmem((3, eighth, BLK), BF16), vmem((eighth, BLK), BF16),
            vmem((15, spot, BLK), BF16), vmem((spot, BLK), BF16), vmem((eighth, BLK), BF16),
        ]
    result, base, cross, sum_0, sum_1 = pl.pallas_call(
        layer_kernel,
        out_shape=(
            jax.ShapeDtypeStruct((rows, D), BF16),
            jax.ShapeDtypeStruct((rows, D), F32),
            jax.ShapeDtypeStruct((N_NODE - 1, CHUNKS, ROWS, 2 * SPAN, D), BF16),
            jax.ShapeDtypeStruct((SUM_ROWS[0], BLK), BF16),
            jax.ShapeDtypeStruct((SUM_ROWS[1], BLK), BF16),
        ),
        in_specs=[IN_SMEM] * 4 + [IN_VMEM] * 15,
        out_specs=(IN_VMEM,) * 5,
        scratch_shapes=[
            vmem((ROWS, KEYS, D), BF16), vmem((ROWS, KEYS, D), BF16), vmem((ROWS, KEYS, D), BF16),
            vmem((rows, D), BF16), vmem((ROWS, HEADS * BLK, KEYS), BF16), vmem((rows, D), F32),
            vmem((rows, D), BF16), vmem((rows, D), F32),
            vmem((ROWS, D, KEYS - NEAR * BLK), BF16), vmem((ROWS, D, KEYS - NEAR * BLK), BF16),
            vmem((ROWS, D, NEAR * BLK), BF16), vmem((ROWS, D, NEAR * BLK), BF16),
            vmem((FAR + 1, BLK, D), BF16), vmem((PART, BLK, D), BF16),
            vmem((2 * D, D), F32), vmem((D, D), F32), vmem((D, 4 * D), F32), vmem((D, 4 * D), F32), vmem((D, D), F32),
            vmem((SUM_ROWS[0], BLK), BF16), vmem((SUM_ROWS[1], BLK), BF16), vmem(staged, BF16), vmem(staged, BF16),
            vmem(relay, BF16), vmem(relay, BF16), vmem(land, BF16), vmem(land, BF16),
            vmem((PART, BLK, D), F32), vmem((2, 4, 256, 256), BF16), vmem((CHUNKS, PART, 2 * SPAN, D), BF16),
        ]
        + sum_scratch
        + phase_sems
        + [dma((2, CHUNKS, 3)), dma((2, 2, 2)), dma((2, 2, 2, 3)), dma((2, 2, 2, 15))],
        compiler_params=pltpu.CompilerParams(
            collective_id=2, has_side_effects=True, vmem_limit_bytes=VMEM_LIMIT
        ),
        name="layer",
    )(
        local_block.T, remote_slot, tile_of, wanted, features, part_0, part_1, land_a, land_b, bias, d_out,
        w_query, w_key, w_value, w_out, w_expand, w_reduce, gain_attn.reshape(1, D), gain_ffn.reshape(1, D),
    )

    factor = 1.0 / math.sqrt(rows * N_DOM * N_NODE)
    return pl.pallas_call(
        functools.partial(finish_kernel, factor),
        out_shape=(
            jax.ShapeDtypeStruct((rows, D), BF16),
            jax.ShapeDtypeStruct((rows, D), BF16),
            jax.ShapeDtypeStruct((D, D), F32),
            jax.ShapeDtypeStruct((D, D), F32),
            jax.ShapeDtypeStruct((D, D), F32),
            jax.ShapeDtypeStruct((D, D), F32),
            jax.ShapeDtypeStruct((D, 4 * D), F32),
            jax.ShapeDtypeStruct((4 * D, D), F32),
        ),
        in_specs=[IN_VMEM] * 5,
        out_specs=(IN_VMEM,) * 8,
        compiler_params=pltpu.CompilerParams(vmem_limit_bytes=VMEM_LIMIT),
        name="finish",
    )(result, base, cross, sum_0, sum_1)


def solution(mesh):
    split = P(("dom", "node"), None)
    placed = (
        (split,) + (P(),) * 8 + (P(("dom", "node"), None, None), split, split, P("dom", "node", None), split)
    )
    return jax.shard_map(
        on_device, mesh=mesh, in_specs=placed, out_specs=(split, split) + (P(),) * 6, check_vma=False
    )
```

```python
import functools
import math

import jax
import jax.numpy as jnp
from jax import lax
from jax.experimental import pallas as pl
from jax.experimental.pallas import tpu as pltpu
from jax.sharding import PartitionSpec as P

HEADS = 8
EPSILON = 1e-05
MESH = pl.DeviceIdType.MESH
F32 = jnp.float32
BF16 = jnp.bfloat16
NEG = -1e30
VMEM_LIMIT = 60 << 20

D = 256
BLK = 128
TILES = 7
NEAR = 3
ROWS = 4
PART = 16
KEYS = TILES * BLK
FAR = ROWS * (TILES - NEAR)
N_DOM = 32
N_NODE = 4
CHUNKS = 2
SPAN = BLK // (2 * CHUNKS)

_GROUPS = [
    [(2, 2)],
    [(2, 1), (2, 3)],
    [(1, 2), (3, 2)],
    [(1, 1), (3, 3)],
    [(1, 3), (3, 1)],
    [(2, 0), (0, 2)],
    [(1, 0), (3, 0), (0, 1), (0, 3)],
]
OFFSETS = [(a, b, c) for group in _GROUPS for c in range(2) for a, b in group] + [(0, 0, 1)]


def dom_peer(dom, offset, sign=1):
    core = lax.rem(dom, 2)
    y = lax.rem(dom // 2, 4)
    z = dom // 8
    dz, dy, dc = offset
    return (
        lax.rem(z + (dz if sign > 0 else 4 - dz), 4) * 8
        + lax.rem(y + (dy if sign > 0 else 4 - dy), 4) * 2
        + lax.rem(core + dc, 2)
    )


def nt(a, b):
    return lax.dot_general(a, b, (((1,), (1,)), ((), ())), preferred_element_type=F32)


def tn(a, b):
    return lax.dot_general(a, b, (((0,), (0,)), ((), ())), preferred_element_type=F32)


def nn(a, b):
    return jnp.dot(a, b, preferred_element_type=F32)


def place():
    dom = lax.axis_index("dom")
    return dom // 8, lax.rem(dom // 2, 4), lax.rem(dom, 2), lax.axis_index("node")


def device(z, y, core, node):
    return (z * 8 + y * 2 + core, node)


def four(value):
    return lax.rem(value, 4)


def two(value):
    return lax.rem(value, 2)


def first_phase(chunk, sources, relays, sends, recvs):
    z, y, core, node = place()
    copies = []
    for step in range(1, 4):
        for half in range(2):
            target = four((z, y)[half] + step)
            copy = pltpu.make_async_remote_copy(
                src_ref=sources[half].at[chunk, pl.ds(target * 8, 8)],
                dst_ref=relays[half].at[chunk, step - 1],
                send_sem=sends.at[chunk, half, step - 1], recv_sem=recvs.at[chunk, half, step - 1],
                device_id=(device(target, y, core, node), device(z, target, core, node))[half],
                device_id_type=MESH,
            )
            copy.start()
            copies.append((half, step, copy))
    return copies


def second_phase(chunk, half, group, sources, relays, lands, sends, recvs):
    z, y, core, node = place()
    copies = []
    for step in range(4):
        for flip in range(2):
            if step == 0 and flip == 0:
                continue
            target = four((y, z)[half] + step)
            side = two(core + flip)
            if group == 0:
                source = sources[half].at[chunk, (z, y)[half] * 8 + target * 2 + side]
            else:
                source = relays[half].at[chunk, group - 1, target * 2 + side]
            copy = pltpu.make_async_remote_copy(
                src_ref=source, dst_ref=lands[half].at[chunk, group, step, flip],
                send_sem=sends.at[chunk, half, group, step, flip],
                recv_sem=recvs.at[chunk, half, group, step, flip],
                device_id=(device(z, target, side, node), device(target, y, side, node))[half],
                device_id_type=MESH,
            )
            copy.start()
            copies.append(copy)
    return copies


def origin(half, group, step, flip):
    z, y, core, node = place()
    far, near = 4 - group, 4 - step
    if half == 0:
        return four(z + far) * 8 + four(y + near) * 2 + two(core + flip)
    return four(z + near) * 8 + four(y + far) * 2 + two(core + flip)


def dom_at(half, along, across, side):
    first, other = ((along, across), (across, along))[half]
    return first * 8 + other * 2 + side


def exchange_kernel(
    feat_ref, table_ref, slot_ref, mask_ref,
    part_0, part_a, part_b, land_a, land_b, wanted_ref, bias_ref, tile_ref,
    row_ref, stage_a, stage_b, relay_a, relay_b, ids_smem, held_a1, held_a2, held_a3, held_b1, held_b2, held_b3,
    near_send, near_recv, id_send, id_recv, send1, recv1, send2, recv2, line_send, line_recv, x_send, x_recv,
    own_sem, local_sem,
):
    dom = lax.axis_index("dom")
    z, y, core, node = place()
    axis = (z, y)
    stages, relays, lands = (stage_a, stage_b), (relay_a, relay_b), (land_a, land_b)
    held = ((part_a, held_a1, held_a2, held_a3), (part_b, held_b1, held_b2, held_b3))
    barrier = pltpu.get_barrier_semaphore()
    for offset in OFFSETS:
        pl.semaphore_signal(barrier, inc=1, device_id=(dom_peer(dom, offset), node), device_id_type=MESH)
    x_line = [(dom, four(node + step)) for step in range(1, N_NODE)]
    for target in x_line:
        pl.semaphore_signal(barrier, inc=1, device_id=target, device_id_type=MESH)
    row_ref[:, 0 : 2 * N_DOM] = table_ref[...]
    mine = pl.ds(node * ROWS, ROWS)
    part_0[mine] = feat_ref[:, 0 : 2 * SPAN]
    for half in range(2):
        held[half][0][mine] = feat_ref[:, (2 + half) * SPAN : (3 + half) * SPAN]
    pl.semaphore_wait(barrier, len(OFFSETS) + N_NODE - 1)

    def push(src, dst, send, recv, target):
        copy = pltpu.make_async_remote_copy(
            src_ref=src, dst_ref=dst, send_sem=send, recv_sem=recv, device_id=target, device_id_type=MESH
        )
        copy.start()
        return copy

    id_copies = [
        push(row_ref, wanted_ref.at[dom], id_send.at[index], id_recv.at[index], (dom_peer(dom, offset), node))
        for index, offset in enumerate(OFFSETS)
    ]
    near_copies = [
        push(
            feat_ref.at[:, pl.ds(0, 2 * SPAN)], part_0.at[mine], near_send.at[index], near_recv.at[index], target
        )
        for index, target in enumerate(x_line)
    ]
    line_copies = []
    for step in range(1, 4):
        for half in range(2):
            target = (device(four(z + step), y, core, node), device(z, four(y + step), core, node))[half]
            copy = push(
                feat_ref.at[:, pl.ds((2 + half) * SPAN, SPAN)], held[half][step].at[mine],
                line_send.at[half, step - 1], line_recv.at[half, step - 1], target,
            )
            line_copies.append((half, step, copy))
    x_copies = {}

    def spread(half, group):
        if group == 0:
            source = feat_ref.at[:, pl.ds((2 + half) * SPAN, SPAN)]
        else:
            source = held[half][group].at[mine]
        x_copies[half, group] = [
            push(
                source, held[half][group].at[mine],
                x_send.at[half, group, index], x_recv.at[half, group, index], target,
            )
            for index, target in enumerate(x_line)
        ]

    for half in range(2):
        spread(half, 0)
    wanted_ref[dom] = row_ref[...]
    for copy in id_copies:
        copy.wait()
    to_smem = pltpu.make_async_copy(wanted_ref, ids_smem, local_sem)
    to_smem.start()
    to_smem.wait()

    def stage(peer, carry):
        turned = four(peer // 2) * 8 + (peer // 8) * 2 + two(peer)
        for slot in range(2):
            block = ids_smem[peer, 0, 2 * dom + slot]
            stage_a[0, peer, slot] = part_0[block, 0:SPAN]
            stage_b[0, turned, slot] = part_0[block, SPAN : 2 * SPAN]
        return carry

    def pick(half, group):
        owner = dom_at(half, four(axis[half] + 4 - group), axis[1 - half], core)

        def body(index, carry):
            asker = dom_at(half, axis[half], index // 2, two(index))
            for slot in range(2):
                block = ids_smem[asker, 0, 2 * owner + slot]
                rows = held[half][group][block]
                if group == 0:
                    stages[half][1, axis[half] * 8 + index, slot] = rows
                else:
                    relays[half][1, group - 1, index, slot] = rows
            return carry

        lax.fori_loop(0, 8, body, 0)

    second = []
    kept = []

    def deliver(chunk, half, group):
        second.extend(second_phase(chunk, half, group, stages, relays, lands, send2, recv2))
        if group == 0:
            source = stages[half].at[chunk, axis[half] * 8 + axis[1 - half] * 2 + core]
        else:
            source = relays[half].at[chunk, group - 1, axis[1 - half] * 2 + core]
        copy = pltpu.make_async_copy(
            source, lands[half].at[chunk, group, 0, 0], own_sem.at[chunk, half, group]
        )
        copy.start()
        kept.append(copy)

    for copy in near_copies:
        copy.wait()
    lax.fori_loop(0, N_DOM, stage, 0)
    first = first_phase(0, stages, relays, send1, recv1)
    for half in range(2):
        deliver(0, half, 0)
    for half, step, copy in line_copies:
        copy.wait()
        spread(half, step)
    for half in range(2):
        for copy in x_copies[half, 0]:
            copy.wait()
        pick(half, 0)
        deliver(1, half, 0)

    def to_bias(row, carry):
        start = pl.multiple_of(row * BLK, BLK)
        diagonal = lax.broadcasted_iota(jnp.int32, (BLK, BLK), 0) == lax.broadcasted_iota(
            jnp.int32, (BLK, BLK), 1
        )
        for tile in range(TILES):
            allowed = mask_ref[tile, pl.ds(start, BLK), :] > 0
            if tile == 0:
                allowed = jnp.logical_or(allowed, diagonal)
            bias_ref[pl.ds(start, BLK), tile * BLK : (tile + 1) * BLK] = jnp.where(
                allowed, 0.0, NEG
            ).astype(BF16)
        return carry

    lax.fori_loop(0, ROWS, to_bias, 0)

    def tile_of(slot, carry):
        found = jnp.int32(FAR)
        for row in range(ROWS):
            for tile in range(TILES - NEAR):
                found = jnp.where(slot_ref[row, tile] == slot, row * (TILES - NEAR) + tile, found)
        tile_ref[0, slot] = found
        return carry

    lax.fori_loop(0, 2 * N_DOM, tile_of, 0)
    for half, step, copy in first:
        copy.wait()
        deliver(0, half, step)
    for group in range(1, 4):
        for half in range(2):
            for copy in x_copies[half, group]:
                copy.wait()
            pick(half, group)
            deliver(1, half, group)
    for copy in kept:
        copy.wait()
    for copy in second:
        copy.wait()


SUM_ROWS = (4096, 2048)


def rows_at(index, size):
    return pl.ds(pl.multiple_of(index * size, size), size)


def layer_kernel(
    local_ref, slot_ref, tile_ref, wanted_ref, feat_ref, part_0, part_a, part_b, far_a, far_b, bias_ref, d_out_ref,
    wq_ref, wk_ref, wv_ref, wo_ref, we_ref, wr_ref, gain_a_ref, gain_f_ref,
    out_ref, base_ref, cross_ref, sum_0, sum_1,
    fs, ks, vs, qs, ps, mixed, d_mixed, d_query, far_keys_t, far_values_t, near_keys_t, near_values_t,
    far_tiles, near_tiles, pair_acc, query_acc, expand_acc, reduce_acc, out_acc,
    grads_0, grads_1, stage_a, stage_b, relay_a, relay_b, land_a, land_b, acc, chosen, cross_send,
    core_recv_0, core_sum_0, x_recv_0, x_sum_0, spot_recv_0, spot_sum_0, x_all_0,
    core_recv_1, core_sum_1, x_recv_1, x_sum_1, spot_recv_1, spot_sum_1, x_all_1,
    send1, recv1, send2, recv2, cross_sems, core_sems, x_sems, spot_sems,
):
    dom = lax.axis_index("dom")
    z, y, core, node = place()
    sources, relays, lands = (stage_a, stage_b), (relay_a, relay_b), (land_a, land_b)
    barrier = pltpu.get_barrier_semaphore()
    peers = [(dom_peer(dom, offset), node) for offset in OFFSETS]
    peers += [(dom, four(node + step)) for step in range(1, N_NODE)]
    for peer in peers:
        pl.semaphore_signal(barrier, inc=1, device_id=peer, device_id_type=MESH)

    scale = 1.0 / math.sqrt(D // HEADS)
    log2e = math.log2(math.e)
    expand_acc[...] = jnp.zeros(expand_acc.shape, F32)
    reduce_acc[...] = jnp.zeros(reduce_acc.shape, F32)
    out_acc[...] = jnp.zeros(out_acc.shape, F32)
    qs[...] = nn(feat_ref[...], wq_ref[...]).astype(BF16)
    lane_head = lax.broadcasted_iota(jnp.int32, (1, D), 1) // (D // HEADS)
    head_f32 = [(lane_head == h).astype(F32) for h in range(HEADS)]
    head_low = [mask.astype(BF16) for mask in head_f32]

    def forward_row(row, carry):
        start = pl.multiple_of(row * BLK, BLK)
        fs[row, 0:BLK] = feat_ref[pl.ds(start, BLK), :]
        for tile in range(NEAR - 1):
            block = local_ref[tile, row]
            top = (tile + 1) * BLK
            fs[row, top : top + 2 * SPAN] = part_0[block]
            fs[row, top + 2 * SPAN : top + 3 * SPAN] = part_a[block]
            fs[row, top + 3 * SPAN : top + 4 * SPAN] = part_b[block]
        for tile in range(TILES - NEAR):
            slot = slot_ref[row, tile]
            asked = slot // 2
            dz = four(z + 4 - asked // 8)
            dy = four(y + 4 - four(asked // 2))
            dc = two(core + two(asked))
            for chunk in range(CHUNKS):
                top = (NEAR + tile) * BLK + 2 * chunk * SPAN
                fs[row, top : top + SPAN] = far_a[chunk, dz, dy, dc, two(slot)]
                fs[row, top + SPAN : top + 2 * SPAN] = far_b[chunk, dy, dz, dc, two(slot)]
        tile_rows = fs[row]
        keys = nn(tile_rows, wk_ref[...]).astype(BF16)
        ks[row] = keys
        values = nn(tile_rows, wv_ref[...]).astype(BF16)
        vs[row] = values
        query = qs[pl.ds(start, BLK), :]
        bias = bias_ref[pl.ds(start, BLK), :].astype(F32)
        total = jnp.zeros((BLK, D), F32)
        for pair in range(HEADS // 2):
            both = jnp.concatenate([query * head_low[2 * pair], query * head_low[2 * pair + 1]], 0)
            scores = nt(both, keys) * (scale * log2e)
            for half in range(2):
                mine = scores[half * BLK : (half + 1) * BLK] + bias
                top = jnp.max(mine, -1, keepdims=True)
                weight = jnp.exp2(mine - top)
                norm = 1.0 / jnp.sum(weight, -1, keepdims=True)
                ps[row, (2 * pair + half) * BLK : (2 * pair + half + 1) * BLK, :] = (weight * norm).astype(BF16)
            got = nn(ps[row, 2 * pair * BLK : (2 * pair + 2) * BLK, :], values)
            total = total + got[:BLK] * head_f32[2 * pair] + got[BLK:] * head_f32[2 * pair + 1]
        mixed[pl.ds(start, BLK), :] = total
        return carry

    lax.fori_loop(0, ROWS, forward_row, 0)

    size = 256

    def feed(step, carry):
        start = pl.multiple_of(step * size, size)
        sel = pl.ds(start, size)
        mixed_low = mixed[sel, :].astype(BF16)
        gain_a = gain_a_ref[...]
        gain_f = gain_f_ref[...]
        residual = feat_ref[sel, :].astype(F32) + nn(mixed_low, wo_ref[...])
        center = residual - jnp.mean(residual, -1, keepdims=True)
        rstd_a = lax.rsqrt(jnp.mean(center * center, -1, keepdims=True) + EPSILON)
        hat_a = center * rstd_a
        first_low = (hat_a * gain_a).astype(BF16)
        pre = nn(first_low, we_ref[...])
        root = math.sqrt(2.0 / math.pi)
        square = pre * pre
        tanh = jnp.tanh(root * (pre + 0.044715 * (square * pre)))
        half = 0.5 * (1.0 + tanh)
        act_low = (pre * half).astype(BF16)
        slope = half + 0.5 * pre * (1.0 - tanh * tanh) * (root * (1.0 + 3.0 * 0.044715 * square))
        second = first_low.astype(F32) + nn(act_low, wr_ref[...])
        center = second - jnp.mean(second, -1, keepdims=True)
        rstd_f = lax.rsqrt(jnp.mean(center * center, -1, keepdims=True) + EPSILON)
        hat_f = center * rstd_f
        out_ref[sel, :] = (hat_f * gain_f).astype(BF16)
        d_hat = d_out_ref[sel, :].astype(F32) * gain_f
        d_second = rstd_f * (
            d_hat - jnp.mean(d_hat, -1, keepdims=True) - hat_f * jnp.mean(d_hat * hat_f, -1, keepdims=True)
        )
        d_second_low = d_second.astype(BF16)
        reduce_acc[...] += tn(d_second_low, act_low)
        d_pre_low = (nt(d_second_low, wr_ref[...]) * slope).astype(BF16)
        expand_acc[...] += tn(first_low, d_pre_low)
        d_first = d_second + nt(d_pre_low, we_ref[...])
        d_hat = d_first * gain_a
        d_resid = rstd_a * (
            d_hat - jnp.mean(d_hat, -1, keepdims=True) - hat_a * jnp.mean(d_hat * hat_a, -1, keepdims=True)
        )
        base_ref[sel, :] = d_resid
        d_resid_low = d_resid.astype(BF16)
        out_acc[...] += tn(mixed_low, d_resid_low)
        d_mixed[sel, :] = nt(d_resid_low, wo_ref[...]).astype(BF16)
        return carry

    lax.fori_loop(0, ROWS * BLK // size, feed, 0)

    def pack(accs, grads):
        spot = 0
        for total in accs:
            for top in range(0, total.shape[0], D):
                for left in range(0, total.shape[1], BLK):
                    grads[spot : spot + D, :] = total[top : top + D, left : left + BLK].astype(BF16)
                    spot += D

    def push(src, dst, sems, key, target):
        copy = pltpu.make_async_remote_copy(
            src_ref=src, dst_ref=dst, send_sem=sems.at[(0,) + key], recv_sem=sems.at[(1,) + key],
            device_id=target, device_id_type=MESH,
        )
        copy.start()
        return copy

    def finish(copies):
        for copy in copies:
            copy.wait()

    spot_here = z * 4 + y
    x_line = [four(node + step) for step in range(1, 4)]
    x_line = [(other, (dom, other)) for other in x_line]
    spots = [lax.rem(spot_here + step, 16) for step in range(1, 16)]
    spots = [(other, (other * 2 + core, node)) for other in spots]
    sibling = device(z, y, two(core + 1), node)

    def reduction(number, grads, total_ref, core_recv, core_sum, x_recv, x_sum, spot_recv, spot_sum, x_all):
        core_rows = SUM_ROWS[number] // 2
        x_rows = core_rows // 4
        spot_rows = x_rows // 16
        mine = rows_at(core, core_rows)

        def scatter(members, src, dst, sems, count):
            return [
                push(src.at[rows_at(other, count)], dst.at[index], sems, (number, 0, index), target)
                for index, (other, target) in enumerate(members)
            ]

        def gather(members, own, src, dst, sems, count):
            copies = [
                push(src, dst.at[rows_at(own, count)], sems, (number, 1, index), target)
                for index, (other, target) in enumerate(members)
            ]
            dst[rows_at(own, count), :] = src[...]
            return copies

        def add_up(own, src, recv, out, count):
            total = src[rows_at(own, count), :].astype(F32)
            for index in range(recv.shape[0]):
                total = total + recv[index].astype(F32)
            out[...] = total.astype(BF16)

        copy = push(grads.at[rows_at(two(core + 1), core_rows)], core_recv, core_sems, (number, 0), sibling)
        yield
        copy.wait()
        core_sum[...] = (grads[mine, :].astype(F32) + core_recv[...].astype(F32)).astype(BF16)
        copies = scatter(x_line, core_sum, x_recv, x_sems, x_rows)
        yield
        finish(copies)
        add_up(node, core_sum, x_recv, x_sum, x_rows)
        copies = scatter(spots, x_sum, spot_recv, spot_sems, spot_rows)
        yield
        finish(copies)
        add_up(spot_here, x_sum, spot_recv, spot_sum, spot_rows)
        copies = gather(spots, spot_here, spot_sum, x_all, spot_sems, spot_rows)
        yield
        finish(copies)
        my_part = total_ref.at[mine]
        copies = gather(x_line, node, x_all, my_part, x_sems, x_rows)
        yield
        finish(copies)
        copy = push(my_part, my_part, core_sems, (number, 1), sibling)
        yield
        copy.wait()
        yield

    first_half = lax.broadcasted_iota(jnp.int32, (64, BLK), 0) < 32

    def block_diagonal(turned, pair):
        piece = turned[64 * pair : 64 * pair + 64]
        return jnp.concatenate(
            [jnp.where(first_half, piece, 0.0), jnp.where(first_half, 0.0, piece)], 1
        ).astype(BF16)

    def backward(row, begin, end):
        start = pl.multiple_of(row * BLK, BLK)
        keys = ks[row, begin:end]
        values = vs[row, begin:end]
        query = qs[pl.ds(start, BLK), :]
        grad = d_mixed[pl.ds(start, BLK), :]
        query_t = query.astype(F32).T
        grad_t = grad.astype(F32).T
        inner_full = grad.astype(F32) * mixed[pl.ds(start, BLK), :]
        query_part = jnp.zeros((BLK, D), F32)
        key_parts = []
        value_parts = []
        for pair in range(HEADS // 2):
            both = jnp.concatenate([grad * head_low[2 * pair], grad * head_low[2 * pair + 1]], 0)
            inner = jnp.concatenate(
                [
                    jnp.sum(inner_full * head_f32[2 * pair], -1, keepdims=True),
                    jnp.sum(inner_full * head_f32[2 * pair + 1], -1, keepdims=True),
                ],
                0,
            )
            probs_low = ps[row, 2 * pair * BLK : (2 * pair + 2) * BLK, begin:end]
            d_probs = nt(both, values)
            d_scores = (probs_low.astype(F32) * ((d_probs - inner) * scale)).astype(BF16)
            got = nn(d_scores, keys)
            query_part = query_part + got[:BLK] * head_f32[2 * pair] + got[BLK:] * head_f32[2 * pair + 1]
            key_parts.append(nn(block_diagonal(query_t, pair), d_scores).astype(BF16))
            value_parts.append(nn(block_diagonal(grad_t, pair), probs_low).astype(BF16))
        d_keys_t = jnp.concatenate(key_parts, 0)
        d_values_t = jnp.concatenate(value_parts, 0)
        return d_keys_t, d_values_t, nn(wk_ref[...], d_keys_t) + nn(wv_ref[...], d_values_t), query_part

    def backward_far(row, carry):
        d_keys_t, d_values_t, d_rows_t, query_part = backward(row, NEAR * BLK, KEYS)
        far_keys_t[row] = d_keys_t
        far_values_t[row] = d_values_t
        d_query[rows_at(row, BLK), :] = query_part
        for tile in range(TILES - NEAR):
            piece = d_rows_t[:, tile * BLK : (tile + 1) * BLK].T
            far_tiles[row * (TILES - NEAR) + tile] = piece.astype(BF16)
        return carry

    def backward_near(row, carry):
        d_keys_t, d_values_t, d_rows_t, query_part = backward(row, 0, NEAR * BLK)
        near_keys_t[row] = d_keys_t
        near_values_t[row] = d_values_t
        d_query[rows_at(row, BLK), :] += query_part
        for tile in range(NEAR):
            piece = d_rows_t[:, tile * BLK : (tile + 1) * BLK].T
            near_tiles[row * NEAR + tile] = piece.astype(BF16)
        return carry

    def key_grads(row, carry):
        near_rows = fs[row, : NEAR * BLK]
        far_rows = fs[row, NEAR * BLK :]
        pair_acc[0:D, :] += nn(near_keys_t[row], near_rows) + nn(far_keys_t[row], far_rows)
        pair_acc[D : 2 * D, :] += nn(near_values_t[row], near_rows) + nn(far_values_t[row], far_rows)
        return carry

    def stage(chunk):
        def body(peer, carry):
            turned = four(peer // 2) * 8 + (peer // 8) * 2 + two(peer)
            for slot in range(2):
                tile = tile_ref[0, 2 * peer + slot]
                top = 2 * chunk * SPAN
                stage_a[chunk, peer, slot] = far_tiles[tile, top : top + SPAN]
                stage_b[chunk, turned, slot] = far_tiles[tile, top + SPAN : top + 2 * SPAN]
            return carry

        lax.fori_loop(0, N_DOM, body, 0)

    block_of = lax.broadcasted_iota(jnp.int32, (256, 256), 0) // 16
    same_row = lax.rem(lax.broadcasted_iota(jnp.int32, (256, 256), 0), 16) == lax.rem(
        lax.broadcasted_iota(jnp.int32, (256, 256), 1), 16
    )
    slot_of = lax.broadcasted_iota(jnp.int32, (1, 256), 1) // 16

    def selection(values):
        names = jnp.full((1, 256), -1, jnp.int32)
        for index, value in enumerate(values):
            names = jnp.where(slot_of == index, value, names)
        return jnp.logical_and(names == block_of, same_row).astype(F32).astype(BF16)

    def relay_on(chunk):
        for half, step, copy in first[chunk]:
            copy.wait()
            second[chunk, half, step] = second_phase(chunk, half, step, sources, relays, lands, send2, recv2)
            lands[half][chunk, step, 0, 0] = relays[half][chunk, step - 1, (y, z)[half] * 2 + core]

    def combine(chunk, group):
        for half in range(2):
            finish(second[chunk, half, group])
            for top in range(0, SPAN, 16):
                rows = slice((2 * chunk + half) * SPAN + top, (2 * chunk + half) * SPAN + top + 16)
                arrived = lands[half][chunk, group, :, :, :, top : top + 16, :].reshape(256, D)
                acc[:, rows, :] += nn(chosen[half, group], arrived).reshape(PART, 16, D)

    def cross(chunk):
        rows = slice(2 * chunk * SPAN, 2 * (chunk + 1) * SPAN)
        cross_send[chunk] = acc[:, rows, :].astype(BF16)
        copies = []
        for step in range(1, N_NODE):
            other = four(node + step)
            copies.append(
                push(
                    cross_send.at[chunk, pl.ds(other * ROWS, ROWS)], cross_ref.at[step - 1, chunk],
                    cross_sems, (chunk, step - 1), (dom, other),
                )
            )
        return copies

    pack((expand_acc, reduce_acc), grads_0)
    pl.semaphore_wait(barrier, len(peers))
    wide = reduction(
        0, grads_0, sum_0, core_recv_0, core_sum_0, x_recv_0, x_sum_0, spot_recv_0, spot_sum_0, x_all_0
    )
    next(wide)
    far_tiles[FAR] = jnp.zeros((BLK, D), BF16)
    lax.fori_loop(0, 2, backward_far, 0)
    next(wide)
    lax.fori_loop(2, ROWS, backward_far, 0)

    first = []
    second = {}
    for chunk in range(CHUNKS):
        stage(chunk)
        if chunk == 0:
            next(wide)
        first.append(first_phase(chunk, sources, relays, send1, recv1))
        for half in range(2):
            second[chunk, half, 0] = second_phase(chunk, half, 0, sources, relays, lands, send2, recv2)
            lands[half][chunk, 0, 0, 0] = sources[half][chunk, (dom, y * 8 + z * 2 + core)[half]]

    near_tiles[ROWS * NEAR : PART] = jnp.zeros((PART - ROWS * NEAR, BLK, D), BF16)
    lax.fori_loop(0, ROWS, backward_near, 0)
    pair_acc[...] = jnp.zeros(pair_acc.shape, F32)
    lax.fori_loop(0, ROWS, key_grads, 0)
    d_query_low = d_query[...].astype(BF16)
    query_acc[...] = tn(feat_ref[...], d_query_low)
    pack((query_acc, pair_acc, out_acc), grads_1)
    narrow = reduction(
        1, grads_1, sum_1, core_recv_1, core_sum_1, x_recv_1, x_sum_1, spot_recv_1, spot_sum_1, x_all_1
    )
    next(narrow)
    next(wide)
    base_ref[...] += nt(d_query_low, wq_ref[...])
    next(narrow)
    relay_on(0)
    next(narrow)
    next(wide)
    near_names = []
    for row in range(ROWS):
        near_names += [node * ROWS + row, local_ref[0, row], local_ref[1, row]]
    near_chosen = selection(near_names)
    for top in range(0, BLK, 16):
        rows = slice(top, top + 16)
        acc[:, rows, :] = nn(near_chosen, near_tiles[:, rows, :].reshape(256, D)).reshape(PART, 16, D)
    for half in range(2):
        for group in range(4):
            chosen[half, group] = selection(
                [
                    wanted_ref[origin(half, group, step, flip), 0, 2 * dom + slot]
                    for step in range(4)
                    for flip in range(2)
                    for slot in range(2)
                ]
            )
    for chunk in range(1, CHUNKS):
        relay_on(chunk)
    combine(0, 0)
    combine(0, 1)
    next(narrow)
    next(wide)
    combine(0, 2)
    combine(0, 3)
    crossing = cross(0)
    next(narrow)
    next(wide)
    for chunk in range(1, CHUNKS):
        for group in range(4):
            combine(chunk, group)
        crossing += cross(chunk)
    next(narrow)
    base_ref[...] += acc[pl.ds(node * ROWS, ROWS)].reshape(ROWS * BLK, D)
    next(narrow)
    finish(crossing)


def finish_kernel(factor, result_ref, base_ref, cross_ref, sum_0, sum_1, out_ref, dx_ref, gq, gk, gv, go, ge, gr):
    out_ref[...] = result_ref[...]
    for row in range(ROWS):
        for chunk in range(CHUNKS):
            span = slice(row * BLK + 2 * chunk * SPAN, row * BLK + 2 * (chunk + 1) * SPAN)
            total = base_ref[span, :]
            for step in range(N_NODE - 1):
                total = total + cross_ref[step, chunk, row].astype(F32)
            dx_ref[span, :] = total.astype(BF16)

    def piece(ref, index):
        return ref[index * D : (index + 1) * D, :].astype(F32) * factor

    for half in range(2):
        span = slice(half * BLK, (half + 1) * BLK)
        gq[:, span] = piece(sum_1, half)
        gk[span, :] = piece(sum_1, 2 + half).T
        gv[span, :] = piece(sum_1, 4 + half).T
        go[:, span] = piece(sum_1, 6 + half)
    for part in range(8):
        span = slice(part * BLK, (part + 1) * BLK)
        ge[:, span] = piece(sum_0, part)
        gr[span, :] = piece(sum_0, 8 + part).T


def vmem(shape, dtype):
    return pltpu.VMEM(shape, dtype)


IN_VMEM = pl.BlockSpec(memory_space=pltpu.VMEM)
IN_SMEM = pl.BlockSpec(memory_space=pltpu.SMEM)
ANYWHERE = pl.BlockSpec(memory_space=pl.ANY)


def on_device(
    features, w_query, w_key, w_value, w_out, w_expand, w_reduce, gain_attn, gain_ffn,
    tile_mask, local_block, remote_slot, remote_block, d_out,
):
    rows = features.shape[0]
    dma = pltpu.SemaphoreType.DMA
    peers = len(OFFSETS)
    land = (CHUNKS, 4, 4, 2, 2, SPAN, D)
    staged = (CHUNKS, N_DOM, 2, SPAN, D)
    relay = (CHUNKS, 3, 8, 2, SPAN, D)
    phase_sems = [dma((CHUNKS, 2, 3)), dma((CHUNKS, 2, 3)), dma((CHUNKS, 2, 4, 4, 2)), dma((CHUNKS, 2, 4, 4, 2))]
    part_0, part_a, part_b, land_a, land_b, wanted, bias, tile_of = pl.pallas_call(
        exchange_kernel,
        out_shape=(
            jax.ShapeDtypeStruct((PART, 2 * SPAN, D), BF16),
            jax.ShapeDtypeStruct((PART, SPAN, D), BF16),
            jax.ShapeDtypeStruct((PART, SPAN, D), BF16),
            jax.ShapeDtypeStruct(land, BF16),
            jax.ShapeDtypeStruct(land, BF16),
            jax.ShapeDtypeStruct((N_DOM, 1, BLK), jnp.int32),
            jax.ShapeDtypeStruct((rows, KEYS), BF16),
            jax.ShapeDtypeStruct((1, 2 * N_DOM), jnp.int32),
        ),
        in_specs=[IN_VMEM, IN_VMEM, IN_SMEM, IN_VMEM],
        out_specs=(IN_VMEM, IN_VMEM, IN_VMEM, ANYWHERE, ANYWHERE, IN_VMEM, IN_VMEM, IN_SMEM),
        scratch_shapes=[
            vmem((1, BLK), jnp.int32), vmem(staged, BF16), vmem(staged, BF16),
            vmem(relay, BF16), vmem(relay, BF16), pltpu.SMEM((N_DOM, 1, BLK), jnp.int32),
        ]
        + [vmem((PART, SPAN, D), BF16)] * 6
        + [dma((N_NODE - 1,)), dma((N_NODE - 1,)), dma((peers,)), dma((peers,))]
        + phase_sems
        + [dma((2, 3)), dma((2, 3)), dma((2, 4, 3)), dma((2, 4, 3)), dma((CHUNKS, 2, 4)), dma],
        compiler_params=pltpu.CompilerParams(
            collective_id=1, has_side_effects=True, vmem_limit_bytes=VMEM_LIMIT
        ),
        name="exchange",
    )(features.reshape(ROWS, BLK, D), remote_block.reshape(1, 2 * N_DOM), remote_slot, jnp.transpose(tile_mask, (1, 0, 2)))

    sum_scratch = []
    for total in SUM_ROWS:
        half, eighth, spot = total // 2, total // 8, total // 128
        sum_scratch += [
            vmem((half, BLK), BF16), vmem((half, BLK), BF16), vmem((3, eighth, BLK), BF16), vmem((eighth, BLK), BF16),
            vmem((15, spot, BLK), BF16), vmem((spot, BLK), BF16), vmem((eighth, BLK), BF16),
        ]
    result, base, cross, sum_0, sum_1 = pl.pallas_call(
        layer_kernel,
        out_shape=(
            jax.ShapeDtypeStruct((rows, D), BF16),
            jax.ShapeDtypeStruct((rows, D), F32),
            jax.ShapeDtypeStruct((N_NODE - 1, CHUNKS, ROWS, 2 * SPAN, D), BF16),
            jax.ShapeDtypeStruct((SUM_ROWS[0], BLK), BF16),
            jax.ShapeDtypeStruct((SUM_ROWS[1], BLK), BF16),
        ),
        in_specs=[IN_SMEM] * 4 + [IN_VMEM] * 16,
        out_specs=(IN_VMEM,) * 5,
        scratch_shapes=[
            vmem((ROWS, KEYS, D), BF16), vmem((ROWS, KEYS, D), BF16), vmem((ROWS, KEYS, D), BF16),
            vmem((rows, D), BF16), vmem((ROWS, HEADS * BLK, KEYS), BF16), vmem((rows, D), F32),
            vmem((rows, D), BF16), vmem((rows, D), F32),
            vmem((ROWS, D, KEYS - NEAR * BLK), BF16), vmem((ROWS, D, KEYS - NEAR * BLK), BF16),
            vmem((ROWS, D, NEAR * BLK), BF16), vmem((ROWS, D, NEAR * BLK), BF16),
            vmem((FAR + 1, BLK, D), BF16), vmem((PART, BLK, D), BF16),
            vmem((2 * D, D), F32), vmem((D, D), F32), vmem((D, 4 * D), F32), vmem((D, 4 * D), F32), vmem((D, D), F32),
            vmem((SUM_ROWS[0], BLK), BF16), vmem((SUM_ROWS[1], BLK), BF16), vmem(staged, BF16), vmem(staged, BF16),
            vmem(relay, BF16), vmem(relay, BF16), vmem(land, BF16), vmem(land, BF16),
            vmem((PART, BLK, D), F32), vmem((2, 4, 256, 256), BF16), vmem((CHUNKS, PART, 2 * SPAN, D), BF16),
        ]
        + sum_scratch
        + phase_sems
        + [dma((2, CHUNKS, 3)), dma((2, 2, 2)), dma((2, 2, 2, 3)), dma((2, 2, 2, 15))],
        compiler_params=pltpu.CompilerParams(
            collective_id=2, has_side_effects=True, vmem_limit_bytes=VMEM_LIMIT
        ),
        name="layer",
    )(
        local_block.T, remote_slot, tile_of, wanted, features, part_0, part_a, part_b, land_a, land_b, bias, d_out,
        w_query, w_key, w_value, w_out, w_expand, w_reduce, gain_attn.reshape(1, D), gain_ffn.reshape(1, D),
    )

    factor = 1.0 / math.sqrt(rows * N_DOM * N_NODE)
    return pl.pallas_call(
        functools.partial(finish_kernel, factor),
        out_shape=(
            jax.ShapeDtypeStruct((rows, D), BF16),
            jax.ShapeDtypeStruct((rows, D), BF16),
            jax.ShapeDtypeStruct((D, D), F32),
            jax.ShapeDtypeStruct((D, D), F32),
            jax.ShapeDtypeStruct((D, D), F32),
            jax.ShapeDtypeStruct((D, D), F32),
            jax.ShapeDtypeStruct((D, 4 * D), F32),
            jax.ShapeDtypeStruct((4 * D, D), F32),
        ),
        in_specs=[IN_VMEM] * 5,
        out_specs=(IN_VMEM,) * 8,
        compiler_params=pltpu.CompilerParams(vmem_limit_bytes=VMEM_LIMIT),
        name="finish",
    )(result, base, cross, sum_0, sum_1)


def solution(mesh):
    split = P(("dom", "node"), None)
    placed = (
        (split,) + (P(),) * 8 + (P(("dom", "node"), None, None), split, split, P("dom", "node", None), split)
    )
    return jax.shard_map(
        on_device, mesh=mesh, in_specs=placed, out_specs=(split, split) + (P(),) * 6, check_vma=False
    )
```

```python
import functools
import math

import jax
import jax.numpy as jnp
from jax import lax
from jax.experimental import pallas as pl
from jax.experimental.pallas import tpu as pltpu
from jax.sharding import PartitionSpec as P

HEADS = 8
EPSILON = 1e-05
MESH = pl.DeviceIdType.MESH
F32 = jnp.float32
BF16 = jnp.bfloat16
NEG = -1e30
VMEM_LIMIT = 62 << 20

D = 256
BLK = 128
TILES = 7
NEAR = 3
ROWS = 4
PART = 16
KEYS = TILES * BLK
FAR = ROWS * (TILES - NEAR)
N_DOM = 32
N_NODE = 4
CHUNKS = 2
SPAN = BLK // (2 * CHUNKS)

_GROUPS = [
    [(2, 2)],
    [(2, 1), (2, 3)],
    [(1, 2), (3, 2)],
    [(1, 1), (3, 3)],
    [(1, 3), (3, 1)],
    [(2, 0), (0, 2)],
    [(1, 0), (3, 0), (0, 1), (0, 3)],
]
OFFSETS = [(a, b, c) for group in _GROUPS for c in range(2) for a, b in group] + [(0, 0, 1)]


def dom_peer(dom, offset, sign=1):
    core = lax.rem(dom, 2)
    y = lax.rem(dom // 2, 4)
    z = dom // 8
    dz, dy, dc = offset
    return (
        lax.rem(z + (dz if sign > 0 else 4 - dz), 4) * 8
        + lax.rem(y + (dy if sign > 0 else 4 - dy), 4) * 2
        + lax.rem(core + dc, 2)
    )


def nt(a, b):
    return lax.dot_general(a, b, (((1,), (1,)), ((), ())), preferred_element_type=F32)


def tn(a, b):
    return lax.dot_general(a, b, (((0,), (0,)), ((), ())), preferred_element_type=F32)


def nn(a, b):
    return jnp.dot(a, b, preferred_element_type=F32)


def place():
    dom = lax.axis_index("dom")
    return dom // 8, lax.rem(dom // 2, 4), lax.rem(dom, 2), lax.axis_index("node")


def device(z, y, core, node):
    return (z * 8 + y * 2 + core, node)


def four(value):
    return lax.rem(value, 4)


def two(value):
    return lax.rem(value, 2)


def first_phase(chunk, sources, relays, sends, recvs):
    z, y, core, node = place()
    copies = []
    for step in range(1, 4):
        for half in range(2):
            target = four((z, y)[half] + step)
            copy = pltpu.make_async_remote_copy(
                src_ref=sources[half].at[chunk, pl.ds(target * 8, 8)],
                dst_ref=relays[half].at[chunk, step - 1],
                send_sem=sends.at[chunk, half, step - 1], recv_sem=recvs.at[chunk, half, step - 1],
                device_id=(device(target, y, core, node), device(z, target, core, node))[half],
                device_id_type=MESH,
            )
            copy.start()
            copies.append((half, step, copy))
    return copies


def second_phase(chunk, half, group, sources, relays, lands, sends, recvs):
    z, y, core, node = place()
    copies = []
    for step in range(4):
        for flip in range(2):
            if step == 0 and flip == 0:
                continue
            target = four((y, z)[half] + step)
            side = two(core + flip)
            if group == 0:
                source = sources[half].at[chunk, (z, y)[half] * 8 + target * 2 + side]
            else:
                source = relays[half].at[chunk, group - 1, target * 2 + side]
            copy = pltpu.make_async_remote_copy(
                src_ref=source, dst_ref=lands[half].at[chunk, group, step, flip],
                send_sem=sends.at[chunk, half, group, step, flip],
                recv_sem=recvs.at[chunk, half, group, step, flip],
                device_id=(device(z, target, side, node), device(target, y, side, node))[half],
                device_id_type=MESH,
            )
            copy.start()
            copies.append(copy)
    return copies


def origin(half, group, step, flip):
    z, y, core, node = place()
    far, near = 4 - group, 4 - step
    if half == 0:
        return four(z + far) * 8 + four(y + near) * 2 + two(core + flip)
    return four(z + near) * 8 + four(y + far) * 2 + two(core + flip)


def dom_at(half, along, across, side):
    first, other = ((along, across), (across, along))[half]
    return first * 8 + other * 2 + side


def exchange_kernel(
    feat_ref, table_ref, slot_ref, mask_ref,
    part_0, part_a, part_b, land_a, land_b, wanted_ref, bias_ref, tile_ref,
    row_ref, stage_a, stage_b, relay_a, relay_b, ids_smem, held_a1, held_a2, held_a3, held_b1, held_b2, held_b3,
    near_send, near_recv, id_send, id_recv, send1, recv1, send2, recv2, line_send, line_recv, x_send, x_recv,
    own_sem, local_sem,
):
    dom = lax.axis_index("dom")
    z, y, core, node = place()
    axis = (z, y)
    stages, relays, lands = (stage_a, stage_b), (relay_a, relay_b), (land_a, land_b)
    held = ((part_a, held_a1, held_a2, held_a3), (part_b, held_b1, held_b2, held_b3))
    barrier = pltpu.get_barrier_semaphore()
    for offset in OFFSETS:
        pl.semaphore_signal(barrier, inc=1, device_id=(dom_peer(dom, offset), node), device_id_type=MESH)
    x_line = [(dom, four(node + step)) for step in range(1, N_NODE)]
    for target in x_line:
        pl.semaphore_signal(barrier, inc=1, device_id=target, device_id_type=MESH)
    row_ref[:, 0 : 2 * N_DOM] = table_ref[...]
    mine = pl.ds(node * ROWS, ROWS)
    part_0[mine] = feat_ref[:, 0 : 2 * SPAN]
    for half in range(2):
        held[half][0][mine] = feat_ref[:, (2 + half) * SPAN : (3 + half) * SPAN]
    pl.semaphore_wait(barrier, len(OFFSETS) + N_NODE - 1)

    def push(src, dst, send, recv, target):
        copy = pltpu.make_async_remote_copy(
            src_ref=src, dst_ref=dst, send_sem=send, recv_sem=recv, device_id=target, device_id_type=MESH
        )
        copy.start()
        return copy

    id_copies = [
        push(row_ref, wanted_ref.at[dom], id_send.at[index], id_recv.at[index], (dom_peer(dom, offset), node))
        for index, offset in enumerate(OFFSETS)
    ]
    near_copies = [
        push(
            feat_ref.at[:, pl.ds(0, 2 * SPAN)], part_0.at[mine], near_send.at[index], near_recv.at[index], target
        )
        for index, target in enumerate(x_line)
    ]
    line_copies = []
    for step in range(1, 4):
        for half in range(2):
            target = (device(four(z + step), y, core, node), device(z, four(y + step), core, node))[half]
            copy = push(
                feat_ref.at[:, pl.ds((2 + half) * SPAN, SPAN)], held[half][step].at[mine],
                line_send.at[half, step - 1], line_recv.at[half, step - 1], target,
            )
            line_copies.append((half, step, copy))
    x_copies = {}

    def spread(half, group):
        if group == 0:
            source = feat_ref.at[:, pl.ds((2 + half) * SPAN, SPAN)]
        else:
            source = held[half][group].at[mine]
        x_copies[half, group] = [
            push(
                source, held[half][group].at[mine],
                x_send.at[half, group, index], x_recv.at[half, group, index], target,
            )
            for index, target in enumerate(x_line)
        ]

    for half in range(2):
        spread(half, 0)
    wanted_ref[dom] = row_ref[...]
    for copy in id_copies:
        copy.wait()
    to_smem = pltpu.make_async_copy(wanted_ref, ids_smem, local_sem)
    to_smem.start()
    to_smem.wait()

    def stage(peer, carry):
        turned = four(peer // 2) * 8 + (peer // 8) * 2 + two(peer)
        for slot in range(2):
            block = ids_smem[peer, 0, 2 * dom + slot]
            stage_a[0, peer, slot] = part_0[block, 0:SPAN]
            stage_b[0, turned, slot] = part_0[block, SPAN : 2 * SPAN]
        return carry

    def pick(half, group):
        owner = dom_at(half, four(axis[half] + 4 - group), axis[1 - half], core)

        def body(index, carry):
            asker = dom_at(half, axis[half], index // 2, two(index))
            for slot in range(2):
                block = ids_smem[asker, 0, 2 * owner + slot]
                rows = held[half][group][block]
                if group == 0:
                    stages[half][1, axis[half] * 8 + index, slot] = rows
                else:
                    relays[half][1, group - 1, index, slot] = rows
            return carry

        lax.fori_loop(0, 8, body, 0)

    second = []
    kept = []

    def deliver(chunk, half, group):
        second.extend(second_phase(chunk, half, group, stages, relays, lands, send2, recv2))
        if group == 0:
            source = stages[half].at[chunk, axis[half] * 8 + axis[1 - half] * 2 + core]
        else:
            source = relays[half].at[chunk, group - 1, axis[1 - half] * 2 + core]
        copy = pltpu.make_async_copy(
            source, lands[half].at[chunk, group, 0, 0], own_sem.at[chunk, half, group]
        )
        copy.start()
        kept.append(copy)

    for copy in near_copies:
        copy.wait()
    lax.fori_loop(0, N_DOM, stage, 0)
    first = first_phase(0, stages, relays, send1, recv1)
    for half in range(2):
        deliver(0, half, 0)
    for half, step, copy in line_copies:
        copy.wait()
        spread(half, step)
    for half in range(2):
        for copy in x_copies[half, 0]:
            copy.wait()
        pick(half, 0)
        deliver(1, half, 0)

    def to_bias(row, carry):
        start = pl.multiple_of(row * BLK, BLK)
        diagonal = lax.broadcasted_iota(jnp.int32, (BLK, BLK), 0) == lax.broadcasted_iota(
            jnp.int32, (BLK, BLK), 1
        )
        for tile in range(TILES):
            allowed = mask_ref[tile, pl.ds(start, BLK), :] > 0
            if tile == 0:
                allowed = jnp.logical_or(allowed, diagonal)
            bias_ref[pl.ds(start, BLK), tile * BLK : (tile + 1) * BLK] = jnp.where(
                allowed, 0.0, NEG
            ).astype(BF16)
        return carry

    lax.fori_loop(0, ROWS, to_bias, 0)

    def tile_of(slot, carry):
        found = jnp.int32(FAR)
        for row in range(ROWS):
            for tile in range(TILES - NEAR):
                found = jnp.where(slot_ref[row, tile] == slot, row * (TILES - NEAR) + tile, found)
        tile_ref[0, slot] = found
        return carry

    lax.fori_loop(0, 2 * N_DOM, tile_of, 0)
    for half, step, copy in first:
        copy.wait()
        deliver(0, half, step)
    for group in range(1, 4):
        for half in range(2):
            for copy in x_copies[half, group]:
                copy.wait()
            pick(half, group)
            deliver(1, half, group)
    for copy in kept:
        copy.wait()
    for copy in second:
        copy.wait()


SUM_ROWS = (4096, 2048)


def rows_at(index, size):
    return pl.ds(pl.multiple_of(index * size, size), size)


def layer_kernel(
    local_ref, slot_ref, tile_ref, wanted_ref, feat_ref, part_0, part_a, part_b, far_a, far_b, bias_ref, d_out_ref,
    wq_ref, wk_ref, wv_ref, wo_ref, we_ref, wr_ref, gain_a_ref, gain_f_ref,
    out_ref, base_ref, cross_ref, sum_0, sum_1,
    fs, ks, vs, qs, ps, mixed, d_mixed, d_query, far_keys_t, far_values_t, near_keys_t, near_values_t,
    far_tiles, near_tiles, pair_acc, query_acc, expand_acc, reduce_acc, out_acc,
    grads_0, grads_1, stage_a, stage_b, relay_a, relay_b, land_a, land_b, acc, near_acc, chosen, cross_send,
    plane_a, plane_b, plane_land, line_send, line_land, axis_send, axis_land, axis_own,
    core_recv_0, core_sum_0, x_recv_0, x_sum_0, spot_recv_0, spot_sum_0, x_all_0,
    core_recv_1, core_sum_1, x_recv_1, x_sum_1, spot_recv_1, spot_sum_1, x_all_1,
    send1, recv1, send2, recv2, plane_sems, line_sems, axis_sems, cross_sems, core_sems, x_sems, spot_sems,
):
    dom = lax.axis_index("dom")
    z, y, core, node = place()
    axis = (z, y)
    sources, relays, lands = (stage_a, stage_b), (relay_a, relay_b), (land_a, land_b)
    planes = (plane_a, plane_b)
    barrier = pltpu.get_barrier_semaphore()
    peers = [(dom_peer(dom, offset), node) for offset in OFFSETS]
    peers += [(dom, four(node + step)) for step in range(1, N_NODE)]
    for peer in peers:
        pl.semaphore_signal(barrier, inc=1, device_id=peer, device_id_type=MESH)

    scale = 1.0 / math.sqrt(D // HEADS)
    log2e = math.log2(math.e)
    expand_acc[...] = jnp.zeros(expand_acc.shape, F32)
    reduce_acc[...] = jnp.zeros(reduce_acc.shape, F32)
    out_acc[...] = jnp.zeros(out_acc.shape, F32)
    qs[...] = nn(feat_ref[...], wq_ref[...]).astype(BF16)
    lane_head = lax.broadcasted_iota(jnp.int32, (1, D), 1) // (D // HEADS)
    head_f32 = [(lane_head == h).astype(F32) for h in range(HEADS)]
    head_low = [mask.astype(BF16) for mask in head_f32]

    def forward_row(row, carry):
        start = pl.multiple_of(row * BLK, BLK)
        fs[row, 0:BLK] = feat_ref[pl.ds(start, BLK), :]
        for tile in range(NEAR - 1):
            block = local_ref[tile, row]
            top = (tile + 1) * BLK
            fs[row, top : top + 2 * SPAN] = part_0[block]
            fs[row, top + 2 * SPAN : top + 3 * SPAN] = part_a[block]
            fs[row, top + 3 * SPAN : top + 4 * SPAN] = part_b[block]
        for tile in range(TILES - NEAR):
            slot = slot_ref[row, tile]
            asked = slot // 2
            dz = four(z + 4 - asked // 8)
            dy = four(y + 4 - four(asked // 2))
            dc = two(core + two(asked))
            for chunk in range(CHUNKS):
                top = (NEAR + tile) * BLK + 2 * chunk * SPAN
                fs[row, top : top + SPAN] = far_a[chunk, dz, dy, dc, two(slot)]
                fs[row, top + SPAN : top + 2 * SPAN] = far_b[chunk, dy, dz, dc, two(slot)]
        tile_rows = fs[row]
        keys = nn(tile_rows, wk_ref[...]).astype(BF16)
        ks[row] = keys
        values = nn(tile_rows, wv_ref[...]).astype(BF16)
        vs[row] = values
        query = qs[pl.ds(start, BLK), :]
        bias = bias_ref[pl.ds(start, BLK), :].astype(F32)
        total = jnp.zeros((BLK, D), F32)
        for pair in range(HEADS // 2):
            both = jnp.concatenate([query * head_low[2 * pair], query * head_low[2 * pair + 1]], 0)
            scores = nt(both, keys) * (scale * log2e)
            for half in range(2):
                mine = scores[half * BLK : (half + 1) * BLK] + bias
                top = jnp.max(mine, -1, keepdims=True)
                weight = jnp.exp2(mine - top)
                norm = 1.0 / jnp.sum(weight, -1, keepdims=True)
                ps[row, (2 * pair + half) * BLK : (2 * pair + half + 1) * BLK, :] = (weight * norm).astype(BF16)
            got = nn(ps[row, 2 * pair * BLK : (2 * pair + 2) * BLK, :], values)
            total = total + got[:BLK] * head_f32[2 * pair] + got[BLK:] * head_f32[2 * pair + 1]
        mixed[pl.ds(start, BLK), :] = total
        return carry

    lax.fori_loop(0, ROWS, forward_row, 0)

    size = 256

    def feed(step, carry):
        start = pl.multiple_of(step * size, size)
        sel = pl.ds(start, size)
        mixed_low = mixed[sel, :].astype(BF16)
        gain_a = gain_a_ref[...]
        gain_f = gain_f_ref[...]
        residual = feat_ref[sel, :].astype(F32) + nn(mixed_low, wo_ref[...])
        center = residual - jnp.mean(residual, -1, keepdims=True)
        rstd_a = lax.rsqrt(jnp.mean(center * center, -1, keepdims=True) + EPSILON)
        hat_a = center * rstd_a
        first_low = (hat_a * gain_a).astype(BF16)
        pre = nn(first_low, we_ref[...])
        root = math.sqrt(2.0 / math.pi)
        square = pre * pre
        tanh = jnp.tanh(root * (pre + 0.044715 * (square * pre)))
        half = 0.5 * (1.0 + tanh)
        act_low = (pre * half).astype(BF16)
        slope = half + 0.5 * pre * (1.0 - tanh * tanh) * (root * (1.0 + 3.0 * 0.044715 * square))
        second = first_low.astype(F32) + nn(act_low, wr_ref[...])
        center = second - jnp.mean(second, -1, keepdims=True)
        rstd_f = lax.rsqrt(jnp.mean(center * center, -1, keepdims=True) + EPSILON)
        hat_f = center * rstd_f
        out_ref[sel, :] = (hat_f * gain_f).astype(BF16)
        d_hat = d_out_ref[sel, :].astype(F32) * gain_f
        d_second = rstd_f * (
            d_hat - jnp.mean(d_hat, -1, keepdims=True) - hat_f * jnp.mean(d_hat * hat_f, -1, keepdims=True)
        )
        d_second_low = d_second.astype(BF16)
        reduce_acc[...] += tn(d_second_low, act_low)
        d_pre_low = (nt(d_second_low, wr_ref[...]) * slope).astype(BF16)
        expand_acc[...] += tn(first_low, d_pre_low)
        d_first = d_second + nt(d_pre_low, we_ref[...])
        d_hat = d_first * gain_a
        d_resid = rstd_a * (
            d_hat - jnp.mean(d_hat, -1, keepdims=True) - hat_a * jnp.mean(d_hat * hat_a, -1, keepdims=True)
        )
        base_ref[sel, :] = d_resid
        d_resid_low = d_resid.astype(BF16)
        out_acc[...] += tn(mixed_low, d_resid_low)
        d_mixed[sel, :] = nt(d_resid_low, wo_ref[...]).astype(BF16)
        return carry

    lax.fori_loop(0, ROWS * BLK // size, feed, 0)

    def pack(accs, grads):
        spot = 0
        for total in accs:
            for top in range(0, total.shape[0], D):
                for left in range(0, total.shape[1], BLK):
                    grads[spot : spot + D, :] = total[top : top + D, left : left + BLK].astype(BF16)
                    spot += D

    def push(src, dst, sems, key, target):
        copy = pltpu.make_async_remote_copy(
            src_ref=src, dst_ref=dst, send_sem=sems.at[(0,) + key], recv_sem=sems.at[(1,) + key],
            device_id=target, device_id_type=MESH,
        )
        copy.start()
        return copy

    def finish(copies):
        for copy in copies:
            copy.wait()

    spot_here = z * 4 + y
    x_line = [four(node + step) for step in range(1, 4)]
    x_line = [(other, (dom, other)) for other in x_line]
    spots = [lax.rem(spot_here + step, 16) for step in range(1, 16)]
    spots = [(other, (other * 2 + core, node)) for other in spots]
    sibling = device(z, y, two(core + 1), node)

    def reduction(number, grads, total_ref, core_recv, core_sum, x_recv, x_sum, spot_recv, spot_sum, x_all):
        core_rows = SUM_ROWS[number] // 2
        x_rows = core_rows // 4
        spot_rows = x_rows // 16
        mine = rows_at(core, core_rows)

        def scatter(members, src, dst, sems, count):
            return [
                push(src.at[rows_at(other, count)], dst.at[index], sems, (number, 0, index), target)
                for index, (other, target) in enumerate(members)
            ]

        def gather(members, own, src, dst, sems, count):
            copies = [
                push(src, dst.at[rows_at(own, count)], sems, (number, 1, index), target)
                for index, (other, target) in enumerate(members)
            ]
            dst[rows_at(own, count), :] = src[...]
            return copies

        def add_up(own, src, recv, out, count):
            total = src[rows_at(own, count), :].astype(F32)
            for index in range(recv.shape[0]):
                total = total + recv[index].astype(F32)
            out[...] = total.astype(BF16)

        copy = push(grads.at[rows_at(two(core + 1), core_rows)], core_recv, core_sems, (number, 0), sibling)
        yield
        copy.wait()
        core_sum[...] = (grads[mine, :].astype(F32) + core_recv[...].astype(F32)).astype(BF16)
        copies = scatter(x_line, core_sum, x_recv, x_sems, x_rows)
        yield
        finish(copies)
        add_up(node, core_sum, x_recv, x_sum, x_rows)
        copies = scatter(spots, x_sum, spot_recv, spot_sems, spot_rows)
        yield
        finish(copies)
        add_up(spot_here, x_sum, spot_recv, spot_sum, spot_rows)
        copies = gather(spots, spot_here, spot_sum, x_all, spot_sems, spot_rows)
        yield
        finish(copies)
        my_part = total_ref.at[mine]
        copies = gather(x_line, node, x_all, my_part, x_sems, x_rows)
        yield
        finish(copies)
        copy = push(my_part, my_part, core_sems, (number, 1), sibling)
        yield
        copy.wait()
        yield

    first_half = lax.broadcasted_iota(jnp.int32, (64, BLK), 0) < 32

    def block_diagonal(turned, pair):
        piece = turned[64 * pair : 64 * pair + 64]
        return jnp.concatenate(
            [jnp.where(first_half, piece, 0.0), jnp.where(first_half, 0.0, piece)], 1
        ).astype(BF16)

    def backward(row, begin, end):
        start = pl.multiple_of(row * BLK, BLK)
        keys = ks[row, begin:end]
        values = vs[row, begin:end]
        query = qs[pl.ds(start, BLK), :]
        grad = d_mixed[pl.ds(start, BLK), :]
        query_t = query.astype(F32).T
        grad_t = grad.astype(F32).T
        inner_full = grad.astype(F32) * mixed[pl.ds(start, BLK), :]
        query_part = jnp.zeros((BLK, D), F32)
        key_parts = []
        value_parts = []
        for pair in range(HEADS // 2):
            both = jnp.concatenate([grad * head_low[2 * pair], grad * head_low[2 * pair + 1]], 0)
            inner = jnp.concatenate(
                [
                    jnp.sum(inner_full * head_f32[2 * pair], -1, keepdims=True),
                    jnp.sum(inner_full * head_f32[2 * pair + 1], -1, keepdims=True),
                ],
                0,
            )
            probs_low = ps[row, 2 * pair * BLK : (2 * pair + 2) * BLK, begin:end]
            d_probs = nt(both, values)
            d_scores = (probs_low.astype(F32) * ((d_probs - inner) * scale)).astype(BF16)
            got = nn(d_scores, keys)
            query_part = query_part + got[:BLK] * head_f32[2 * pair] + got[BLK:] * head_f32[2 * pair + 1]
            key_parts.append(nn(block_diagonal(query_t, pair), d_scores).astype(BF16))
            value_parts.append(nn(block_diagonal(grad_t, pair), probs_low).astype(BF16))
        d_keys_t = jnp.concatenate(key_parts, 0)
        d_values_t = jnp.concatenate(value_parts, 0)
        return d_keys_t, d_values_t, nn(wk_ref[...], d_keys_t) + nn(wv_ref[...], d_values_t), query_part

    def backward_far(row, carry):
        d_keys_t, d_values_t, d_rows_t, query_part = backward(row, NEAR * BLK, KEYS)
        far_keys_t[row] = d_keys_t
        far_values_t[row] = d_values_t
        d_query[rows_at(row, BLK), :] = query_part
        for tile in range(TILES - NEAR):
            piece = d_rows_t[:, tile * BLK : (tile + 1) * BLK].T
            far_tiles[row * (TILES - NEAR) + tile] = piece.astype(BF16)
        return carry

    def backward_near(row, carry):
        d_keys_t, d_values_t, d_rows_t, query_part = backward(row, 0, NEAR * BLK)
        near_keys_t[row] = d_keys_t
        near_values_t[row] = d_values_t
        d_query[rows_at(row, BLK), :] += query_part
        for tile in range(NEAR):
            piece = d_rows_t[:, tile * BLK : (tile + 1) * BLK].T
            near_tiles[row * NEAR + tile] = piece.astype(BF16)
        return carry

    def key_grads(row, carry):
        near_rows = fs[row, : NEAR * BLK]
        far_rows = fs[row, NEAR * BLK :]
        pair_acc[0:D, :] += nn(near_keys_t[row], near_rows) + nn(far_keys_t[row], far_rows)
        pair_acc[D : 2 * D, :] += nn(near_values_t[row], near_rows) + nn(far_values_t[row], far_rows)
        return carry

    def stage_early(peer, carry):
        peer_z, peer_y, side = peer // 8, four(peer // 2), two(peer)
        for slot in range(2):
            tile = tile_ref[0, 2 * peer + slot]
            plane_a[peer_y * 2 + side, peer_z, slot] = far_tiles[tile, 2 * SPAN : 3 * SPAN]
            plane_b[peer_z * 2 + side, peer_y, slot] = far_tiles[tile, 3 * SPAN : 4 * SPAN]
        return carry

    def stage_late(peer, carry):
        turned = four(peer // 2) * 8 + (peer // 8) * 2 + two(peer)
        for slot in range(2):
            tile = tile_ref[0, 2 * peer + slot]
            stage_a[0, peer, slot] = far_tiles[tile, 0:SPAN]
            stage_b[0, turned, slot] = far_tiles[tile, SPAN : 2 * SPAN]
        return carry

    def send_early(half):
        copies = []
        for step in range(4):
            for flip in range(2):
                target = four(axis[1 - half] + step)
                side = two(core + flip)
                if step == 0 and flip == 0:
                    plane_land[half, 0, 0] = planes[half][target * 2 + side]
                    continue
                copies.append(
                    push(
                        planes[half].at[target * 2 + side], plane_land.at[half, step, flip],
                        plane_sems, (half, step, flip), (dom_at(half, axis[half], target, side), node),
                    )
                )
        return copies

    def sum_early(half):
        finish(early[half])
        for ahead in range(4):
            place_there = four(axis[half] + ahead)
            owner = dom_at(half, place_there, axis[1 - half], core)
            names = []
            for step in range(4):
                for flip in range(2):
                    asker = dom_at(half, axis[half], four(axis[1 - half] + 4 - step), two(core + flip))
                    names += [wanted_ref[asker, 0, 2 * owner + slot] for slot in range(2)]
            chosen[half, ahead] = selection(names)
            for top in range(0, SPAN, 16):
                arrived = plane_land[half, :, :, place_there, :, top : top + 16, :].reshape(256, D)
                total = nn(chosen[half, ahead], arrived).reshape(PART, 16, D)
                if ahead == 0:
                    total = total + near_acc[:, half * SPAN + top : half * SPAN + top + 16, :]
                line_send[half, ahead, :, top : top + 16, :] = total.astype(BF16)
        return [
            push(
                line_send.at[half, :, pl.ds(other * ROWS, ROWS)], line_land.at[half, index],
                line_sems, (half, index), target,
            )
            for index, (other, target) in enumerate(x_line)
        ]

    def turn_early(half):
        finish(lined[half])
        copies = []
        for ahead in range(4):
            total = line_send[half, ahead, pl.ds(node * ROWS, ROWS)].astype(F32)
            for index in range(3):
                total = total + line_land[half, index, ahead].astype(F32)
            if ahead == 0:
                axis_own[half] = total
            else:
                axis_send[half, ahead - 1] = total.astype(BF16)
                there = four(axis[half] + ahead)
                copies.append(
                    push(
                        axis_send.at[half, ahead - 1], axis_land.at[half, ahead - 1],
                        axis_sems, (half, ahead - 1), (dom_at(half, there, axis[1 - half], core), node),
                    )
                )
        return copies

    def end_early(half):
        finish(turned_copies[half])
        for row in range(ROWS):
            total = axis_own[half, row]
            for index in range(3):
                total = total + axis_land[half, index, row].astype(F32)
            top = row * BLK + (2 + half) * SPAN
            base_ref[top : top + SPAN, :] += total

    block_of = lax.broadcasted_iota(jnp.int32, (256, 256), 0) // 16
    same_row = lax.rem(lax.broadcasted_iota(jnp.int32, (256, 256), 0), 16) == lax.rem(
        lax.broadcasted_iota(jnp.int32, (256, 256), 1), 16
    )
    slot_of = lax.broadcasted_iota(jnp.int32, (1, 256), 1) // 16

    def selection(values):
        names = jnp.full((1, 256), -1, jnp.int32)
        for index, value in enumerate(values):
            names = jnp.where(slot_of == index, value, names)
        return jnp.logical_and(names == block_of, same_row).astype(F32).astype(BF16)

    def relay_on(arrivals):
        for half, step, copy in arrivals:
            copy.wait()
            second[half, step] = second_phase(0, half, step, sources, relays, lands, send2, recv2)
            lands[half][0, step, 0, 0] = relays[half][0, step - 1, (y, z)[half] * 2 + core]

    def combine(group):
        for half in range(2):
            finish(second[half, group])
            names = [
                wanted_ref[origin(half, group, step, flip), 0, 2 * dom + slot]
                for step in range(4)
                for flip in range(2)
                for slot in range(2)
            ]
            chosen[half, group] = selection(names)
            for top in range(0, SPAN, 16):
                rows = slice(half * SPAN + top, half * SPAN + top + 16)
                arrived = lands[half][0, group, :, :, :, top : top + 16, :].reshape(256, D)
                acc[:, rows, :] += nn(chosen[half, group], arrived).reshape(PART, 16, D)

    def cross():
        cross_send[...] = acc[...].astype(BF16)
        copies = []
        for step in range(1, N_NODE):
            other = four(node + step)
            copies.append(
                push(
                    cross_send.at[pl.ds(other * ROWS, ROWS)], cross_ref.at[step - 1],
                    cross_sems, (step - 1,), (dom, other),
                )
            )
        return copies

    pack((expand_acc, reduce_acc), grads_0)
    pl.semaphore_wait(barrier, len(peers))
    wide = reduction(
        0, grads_0, sum_0, core_recv_0, core_sum_0, x_recv_0, x_sum_0, spot_recv_0, spot_sum_0, x_all_0
    )
    next(wide)
    far_tiles[FAR] = jnp.zeros((BLK, D), BF16)
    lax.fori_loop(0, 2, backward_far, 0)
    next(wide)
    lax.fori_loop(2, ROWS, backward_far, 0)

    lax.fori_loop(0, N_DOM, stage_early, 0)
    early = [send_early(half) for half in range(2)]
    next(wide)
    lax.fori_loop(0, N_DOM, stage_late, 0)
    first = first_phase(0, sources, relays, send1, recv1)
    second = {}
    for half in range(2):
        second[half, 0] = second_phase(0, half, 0, sources, relays, lands, send2, recv2)
        lands[half][0, 0, 0, 0] = sources[half][0, (dom, y * 8 + z * 2 + core)[half]]

    near_tiles[ROWS * NEAR : PART] = jnp.zeros((PART - ROWS * NEAR, BLK, D), BF16)
    lax.fori_loop(0, ROWS, backward_near, 0)
    pair_acc[...] = jnp.zeros(pair_acc.shape, F32)
    lax.fori_loop(0, ROWS, key_grads, 0)
    d_query_low = d_query[...].astype(BF16)
    query_acc[...] = tn(feat_ref[...], d_query_low)
    pack((query_acc, pair_acc, out_acc), grads_1)
    narrow = reduction(
        1, grads_1, sum_1, core_recv_1, core_sum_1, x_recv_1, x_sum_1, spot_recv_1, spot_sum_1, x_all_1
    )
    next(narrow)
    near_names = []
    for row in range(ROWS):
        near_names += [node * ROWS + row, local_ref[0, row], local_ref[1, row]]
    near_chosen = selection(near_names)
    for top in range(0, BLK, 16):
        total = nn(near_chosen, near_tiles[:, top : top + 16, :].reshape(256, D)).reshape(PART, 16, D)
        if top < 2 * SPAN:
            acc[:, top : top + 16, :] = total
        else:
            near_acc[:, top - 2 * SPAN : top - 2 * SPAN + 16, :] = total
    next(narrow)
    next(wide)
    lined = [sum_early(half) for half in range(2)]
    base_ref[...] += nt(d_query_low, wq_ref[...])
    next(narrow)
    relay_on(first[:3])
    next(narrow)
    next(wide)
    relay_on(first[3:])
    combine(0)
    combine(1)
    turned_copies = [turn_early(half) for half in range(2)]
    next(narrow)
    next(wide)
    combine(2)
    combine(3)
    crossing = cross()
    next(narrow)
    next(wide)
    for half in range(2):
        end_early(half)
    for row in range(ROWS):
        base_ref[row * BLK : row * BLK + 2 * SPAN, :] += acc[node * ROWS + row]
    next(narrow)
    finish(crossing)


def finish_kernel(factor, result_ref, base_ref, cross_ref, sum_0, sum_1, out_ref, dx_ref, gq, gk, gv, go, ge, gr):
    out_ref[...] = result_ref[...]
    for row in range(ROWS):
        span = slice(row * BLK, row * BLK + 2 * SPAN)
        total = base_ref[span, :]
        for step in range(N_NODE - 1):
            total = total + cross_ref[step, row].astype(F32)
        dx_ref[span, :] = total.astype(BF16)
        span = slice(row * BLK + 2 * SPAN, (row + 1) * BLK)
        dx_ref[span, :] = base_ref[span, :].astype(BF16)

    def piece(ref, index):
        return ref[index * D : (index + 1) * D, :].astype(F32) * factor

    for half in range(2):
        span = slice(half * BLK, (half + 1) * BLK)
        gq[:, span] = piece(sum_1, half)
        gk[span, :] = piece(sum_1, 2 + half).T
        gv[span, :] = piece(sum_1, 4 + half).T
        go[:, span] = piece(sum_1, 6 + half)
    for part in range(8):
        span = slice(part * BLK, (part + 1) * BLK)
        ge[:, span] = piece(sum_0, part)
        gr[span, :] = piece(sum_0, 8 + part).T


def vmem(shape, dtype):
    return pltpu.VMEM(shape, dtype)


IN_VMEM = pl.BlockSpec(memory_space=pltpu.VMEM)
IN_SMEM = pl.BlockSpec(memory_space=pltpu.SMEM)
ANYWHERE = pl.BlockSpec(memory_space=pl.ANY)


def on_device(
    features, w_query, w_key, w_value, w_out, w_expand, w_reduce, gain_attn, gain_ffn,
    tile_mask, local_block, remote_slot, remote_block, d_out,
):
    rows = features.shape[0]
    dma = pltpu.SemaphoreType.DMA
    peers = len(OFFSETS)
    land = (CHUNKS, 4, 4, 2, 2, SPAN, D)
    staged = (CHUNKS, N_DOM, 2, SPAN, D)
    relay = (CHUNKS, 3, 8, 2, SPAN, D)
    phase_sems = [dma((CHUNKS, 2, 3)), dma((CHUNKS, 2, 3)), dma((CHUNKS, 2, 4, 4, 2)), dma((CHUNKS, 2, 4, 4, 2))]
    part_0, part_a, part_b, land_a, land_b, wanted, bias, tile_of = pl.pallas_call(
        exchange_kernel,
        out_shape=(
            jax.ShapeDtypeStruct((PART, 2 * SPAN, D), BF16),
            jax.ShapeDtypeStruct((PART, SPAN, D), BF16),
            jax.ShapeDtypeStruct((PART, SPAN, D), BF16),
            jax.ShapeDtypeStruct(land, BF16),
            jax.ShapeDtypeStruct(land, BF16),
            jax.ShapeDtypeStruct((N_DOM, 1, BLK), jnp.int32),
            jax.ShapeDtypeStruct((rows, KEYS), BF16),
            jax.ShapeDtypeStruct((1, 2 * N_DOM), jnp.int32),
        ),
        in_specs=[IN_VMEM, IN_VMEM, IN_SMEM, IN_VMEM],
        out_specs=(IN_VMEM, IN_VMEM, IN_VMEM, ANYWHERE, ANYWHERE, IN_VMEM, IN_VMEM, IN_SMEM),
        scratch_shapes=[
            vmem((1, BLK), jnp.int32), vmem(staged, BF16), vmem(staged, BF16),
            vmem(relay, BF16), vmem(relay, BF16), pltpu.SMEM((N_DOM, 1, BLK), jnp.int32),
        ]
        + [vmem((PART, SPAN, D), BF16)] * 6
        + [dma((N_NODE - 1,)), dma((N_NODE - 1,)), dma((peers,)), dma((peers,))]
        + phase_sems
        + [dma((2, 3)), dma((2, 3)), dma((2, 4, 3)), dma((2, 4, 3)), dma((CHUNKS, 2, 4)), dma],
        compiler_params=pltpu.CompilerParams(
            collective_id=1, has_side_effects=True, vmem_limit_bytes=VMEM_LIMIT
        ),
        name="exchange",
    )(features.reshape(ROWS, BLK, D), remote_block.reshape(1, 2 * N_DOM), remote_slot, jnp.transpose(tile_mask, (1, 0, 2)))

    sum_scratch = []
    for total in SUM_ROWS:
        half, eighth, spot = total // 2, total // 8, total // 128
        sum_scratch += [
            vmem((half, BLK), BF16), vmem((half, BLK), BF16), vmem((3, eighth, BLK), BF16), vmem((eighth, BLK), BF16),
            vmem((15, spot, BLK), BF16), vmem((spot, BLK), BF16), vmem((eighth, BLK), BF16),
        ]
    result, base, cross, sum_0, sum_1 = pl.pallas_call(
        layer_kernel,
        out_shape=(
            jax.ShapeDtypeStruct((rows, D), BF16),
            jax.ShapeDtypeStruct((rows, D), F32),
            jax.ShapeDtypeStruct((N_NODE - 1, ROWS, 2 * SPAN, D), BF16),
            jax.ShapeDtypeStruct((SUM_ROWS[0], BLK), BF16),
            jax.ShapeDtypeStruct((SUM_ROWS[1], BLK), BF16),
        ),
        in_specs=[IN_SMEM] * 4 + [IN_VMEM] * 16,
        out_specs=(IN_VMEM,) * 5,
        scratch_shapes=[
            vmem((ROWS, KEYS, D), BF16), vmem((ROWS, KEYS, D), BF16), vmem((ROWS, KEYS, D), BF16),
            vmem((rows, D), BF16), vmem((ROWS, HEADS * BLK, KEYS), BF16), vmem((rows, D), F32),
            vmem((rows, D), BF16), vmem((rows, D), F32),
            vmem((ROWS, D, KEYS - NEAR * BLK), BF16), vmem((ROWS, D, KEYS - NEAR * BLK), BF16),
            vmem((ROWS, D, NEAR * BLK), BF16), vmem((ROWS, D, NEAR * BLK), BF16),
            vmem((FAR + 1, BLK, D), BF16), vmem((PART, BLK, D), BF16),
            vmem((2 * D, D), F32), vmem((D, D), F32), vmem((D, 4 * D), F32), vmem((D, 4 * D), F32), vmem((D, D), F32),
            vmem((SUM_ROWS[0], BLK), BF16), vmem((SUM_ROWS[1], BLK), BF16),
            vmem((1,) + staged[1:], BF16), vmem((1,) + staged[1:], BF16),
            vmem((1,) + relay[1:], BF16), vmem((1,) + relay[1:], BF16),
            vmem((1,) + land[1:], BF16), vmem((1,) + land[1:], BF16),
            vmem((PART, 2 * SPAN, D), F32), vmem((PART, 2 * SPAN, D), F32),
            vmem((2, 4, 256, 256), BF16), vmem((PART, 2 * SPAN, D), BF16),
            vmem((8, 4, 2, SPAN, D), BF16), vmem((8, 4, 2, SPAN, D), BF16), vmem((2, 4, 2, 4, 2, SPAN, D), BF16),
            vmem((2, 4, PART, SPAN, D), BF16), vmem((2, 3, 4, ROWS, SPAN, D), BF16),
            vmem((2, 3, ROWS, SPAN, D), BF16), vmem((2, 3, ROWS, SPAN, D), BF16), vmem((2, ROWS, SPAN, D), F32),
        ]
        + sum_scratch
        + [dma((1, 2, 3)), dma((1, 2, 3)), dma((1, 2, 4, 4, 2)), dma((1, 2, 4, 4, 2))]
        + [dma((2, 2, 4, 2)), dma((2, 2, 3)), dma((2, 2, 3)), dma((2, 3)), dma((2, 2, 2)), dma((2, 2, 2, 3)), dma((2, 2, 2, 15))],
        compiler_params=pltpu.CompilerParams(
            collective_id=2, has_side_effects=True, vmem_limit_bytes=VMEM_LIMIT
        ),
        name="layer",
    )(
        local_block.T, remote_slot, tile_of, wanted, features, part_0, part_a, part_b, land_a, land_b, bias, d_out,
        w_query, w_key, w_value, w_out, w_expand, w_reduce, gain_attn.reshape(1, D), gain_ffn.reshape(1, D),
    )

    factor = 1.0 / math.sqrt(rows * N_DOM * N_NODE)
    return pl.pallas_call(
        functools.partial(finish_kernel, factor),
        out_shape=(
            jax.ShapeDtypeStruct((rows, D), BF16),
            jax.ShapeDtypeStruct((rows, D), BF16),
            jax.ShapeDtypeStruct((D, D), F32),
            jax.ShapeDtypeStruct((D, D), F32),
            jax.ShapeDtypeStruct((D, D), F32),
            jax.ShapeDtypeStruct((D, D), F32),
            jax.ShapeDtypeStruct((D, 4 * D), F32),
            jax.ShapeDtypeStruct((4 * D, D), F32),
        ),
        in_specs=[IN_VMEM] * 5,
        out_specs=(IN_VMEM,) * 8,
        compiler_params=pltpu.CompilerParams(vmem_limit_bytes=VMEM_LIMIT),
        name="finish",
    )(result, base, cross, sum_0, sum_1)


def solution(mesh):
    split = P(("dom", "node"), None)
    placed = (
        (split,) + (P(),) * 8 + (P(("dom", "node"), None, None), split, split, P("dom", "node", None), split)
    )
    return jax.shard_map(
        on_device, mesh=mesh, in_specs=placed, out_specs=(split, split) + (P(),) * 6, check_vma=False
    )
```

```python
import functools
import math

import jax
import jax.numpy as jnp
from jax import lax
from jax.experimental import pallas as pl
from jax.experimental.pallas import tpu as pltpu
from jax.sharding import PartitionSpec as P

HEADS = 8
EPSILON = 1e-05
MESH = pl.DeviceIdType.MESH
F32 = jnp.float32
BF16 = jnp.bfloat16
NEG = -1e30
VMEM_LIMIT = 62 << 20

D = 256
BLK = 128
TILES = 7
NEAR = 3
ROWS = 4
PART = 16
KEYS = TILES * BLK
FAR = ROWS * (TILES - NEAR)
EARLY = NEAR * BLK
LATE = EARLY + (KEYS - EARLY) // 2
N_DOM = 32
N_NODE = 4
CHUNKS = 2
SPAN = BLK // (2 * CHUNKS)

_GROUPS = [
    [(2, 2)],
    [(2, 1), (2, 3)],
    [(1, 2), (3, 2)],
    [(1, 1), (3, 3)],
    [(1, 3), (3, 1)],
    [(2, 0), (0, 2)],
    [(1, 0), (3, 0), (0, 1), (0, 3)],
]
OFFSETS = [(a, b, c) for group in _GROUPS for c in range(2) for a, b in group] + [(0, 0, 1)]


def dom_peer(dom, offset, sign=1):
    core = lax.rem(dom, 2)
    y = lax.rem(dom // 2, 4)
    z = dom // 8
    dz, dy, dc = offset
    return (
        lax.rem(z + (dz if sign > 0 else 4 - dz), 4) * 8
        + lax.rem(y + (dy if sign > 0 else 4 - dy), 4) * 2
        + lax.rem(core + dc, 2)
    )


def nt(a, b):
    return lax.dot_general(a, b, (((1,), (1,)), ((), ())), preferred_element_type=F32)


def tn(a, b):
    return lax.dot_general(a, b, (((0,), (0,)), ((), ())), preferred_element_type=F32)


def nn(a, b):
    return jnp.dot(a, b, preferred_element_type=F32)


def place():
    dom = lax.axis_index("dom")
    return dom // 8, lax.rem(dom // 2, 4), lax.rem(dom, 2), lax.axis_index("node")


def device(z, y, core, node):
    return (z * 8 + y * 2 + core, node)


def four(value):
    return lax.rem(value, 4)


def two(value):
    return lax.rem(value, 2)


def first_phase(chunk, sources, relays, sends, recvs):
    z, y, core, node = place()
    copies = []
    for step in range(1, 4):
        for half in range(2):
            target = four((z, y)[half] + step)
            copy = pltpu.make_async_remote_copy(
                src_ref=sources[half].at[chunk, pl.ds(target * 8, 8)],
                dst_ref=relays[half].at[chunk, step - 1],
                send_sem=sends.at[chunk, half, step - 1], recv_sem=recvs.at[chunk, half, step - 1],
                device_id=(device(target, y, core, node), device(z, target, core, node))[half],
                device_id_type=MESH,
            )
            copy.start()
            copies.append((half, step, copy))
    return copies


def second_phase(chunk, half, group, sources, relays, lands, sends, recvs):
    z, y, core, node = place()
    copies = []
    for step in range(4):
        for flip in range(2):
            if step == 0 and flip == 0:
                continue
            target = four((y, z)[half] + step)
            side = two(core + flip)
            if group == 0:
                source = sources[half].at[chunk, (z, y)[half] * 8 + target * 2 + side]
            else:
                source = relays[half].at[chunk, group - 1, target * 2 + side]
            copy = pltpu.make_async_remote_copy(
                src_ref=source, dst_ref=lands[half].at[chunk, group, step, flip],
                send_sem=sends.at[chunk, half, group, step, flip],
                recv_sem=recvs.at[chunk, half, group, step, flip],
                device_id=(device(z, target, side, node), device(target, y, side, node))[half],
                device_id_type=MESH,
            )
            copy.start()
            copies.append(copy)
    return copies


def origin(half, group, step, flip):
    z, y, core, node = place()
    far, near = 4 - group, 4 - step
    if half == 0:
        return four(z + far) * 8 + four(y + near) * 2 + two(core + flip)
    return four(z + near) * 8 + four(y + far) * 2 + two(core + flip)


def dom_at(half, along, across, side):
    first, other = ((along, across), (across, along))[half]
    return first * 8 + other * 2 + side


def exchange_kernel(
    feat_ref, table_ref, slot_ref, mask_ref,
    part_0, part_a, part_b, land_a, land_b, wanted_ref, bias_ref, tile_ref,
    row_ref, stage_a, stage_b, relay_a, relay_b, ids_smem, held_a1, held_a2, held_a3, held_b1, held_b2, held_b3,
    near_send, near_recv, id_send, id_recv, send1, recv1, send2, recv2, line_send, line_recv, x_send, x_recv,
    own_sem, local_sem,
):
    dom = lax.axis_index("dom")
    z, y, core, node = place()
    axis = (z, y)
    stages, relays, lands = (stage_a, stage_b), (relay_a, relay_b), (land_a, land_b)
    held = ((part_a, held_a1, held_a2, held_a3), (part_b, held_b1, held_b2, held_b3))
    barrier = pltpu.get_barrier_semaphore()
    for offset in OFFSETS:
        pl.semaphore_signal(barrier, inc=1, device_id=(dom_peer(dom, offset), node), device_id_type=MESH)
    x_line = [(dom, four(node + step)) for step in range(1, N_NODE)]
    for target in x_line:
        pl.semaphore_signal(barrier, inc=1, device_id=target, device_id_type=MESH)
    row_ref[:, 0 : 2 * N_DOM] = table_ref[...]
    mine = pl.ds(node * ROWS, ROWS)
    part_0[mine] = feat_ref[:, 0 : 2 * SPAN]
    for half in range(2):
        held[half][0][mine] = feat_ref[:, (2 + half) * SPAN : (3 + half) * SPAN]
    pl.semaphore_wait(barrier, len(OFFSETS) + N_NODE - 1)

    def push(src, dst, send, recv, target):
        copy = pltpu.make_async_remote_copy(
            src_ref=src, dst_ref=dst, send_sem=send, recv_sem=recv, device_id=target, device_id_type=MESH
        )
        copy.start()
        return copy

    id_copies = [
        push(row_ref, wanted_ref.at[dom], id_send.at[index], id_recv.at[index], (dom_peer(dom, offset), node))
        for index, offset in enumerate(OFFSETS)
    ]
    near_copies = [
        push(
            feat_ref.at[:, pl.ds(0, 2 * SPAN)], part_0.at[mine], near_send.at[index], near_recv.at[index], target
        )
        for index, target in enumerate(x_line)
    ]
    line_copies = []
    for step in range(1, 4):
        for half in range(2):
            target = (device(four(z + step), y, core, node), device(z, four(y + step), core, node))[half]
            copy = push(
                feat_ref.at[:, pl.ds((2 + half) * SPAN, SPAN)], held[half][step].at[mine],
                line_send.at[half, step - 1], line_recv.at[half, step - 1], target,
            )
            line_copies.append((half, step, copy))
    x_copies = {}

    def spread(half, group):
        if group == 0:
            source = feat_ref.at[:, pl.ds((2 + half) * SPAN, SPAN)]
        else:
            source = held[half][group].at[mine]
        x_copies[half, group] = [
            push(
                source, held[half][group].at[mine],
                x_send.at[half, group, index], x_recv.at[half, group, index], target,
            )
            for index, target in enumerate(x_line)
        ]

    for half in range(2):
        spread(half, 0)
    wanted_ref[dom] = row_ref[...]
    for copy in id_copies:
        copy.wait()
    to_smem = pltpu.make_async_copy(wanted_ref, ids_smem, local_sem)
    to_smem.start()
    to_smem.wait()

    def stage(peer, carry):
        turned = four(peer // 2) * 8 + (peer // 8) * 2 + two(peer)
        for slot in range(2):
            block = ids_smem[peer, 0, 2 * dom + slot]
            stage_a[0, peer, slot] = part_0[block, 0:SPAN]
            stage_b[0, turned, slot] = part_0[block, SPAN : 2 * SPAN]
        return carry

    def pick(half, group):
        owner = dom_at(half, four(axis[half] + 4 - group), axis[1 - half], core)

        def body(index, carry):
            asker = dom_at(half, axis[half], index // 2, two(index))
            for slot in range(2):
                block = ids_smem[asker, 0, 2 * owner + slot]
                rows = held[half][group][block]
                if group == 0:
                    stages[half][1, axis[half] * 8 + index, slot] = rows
                else:
                    relays[half][1, group - 1, index, slot] = rows
            return carry

        lax.fori_loop(0, 8, body, 0)

    second = []
    kept = []

    def deliver(chunk, half, group):
        second.extend(second_phase(chunk, half, group, stages, relays, lands, send2, recv2))
        if group == 0:
            source = stages[half].at[chunk, axis[half] * 8 + axis[1 - half] * 2 + core]
        else:
            source = relays[half].at[chunk, group - 1, axis[1 - half] * 2 + core]
        copy = pltpu.make_async_copy(
            source, lands[half].at[chunk, group, 0, 0], own_sem.at[chunk, half, group]
        )
        copy.start()
        kept.append(copy)

    for copy in near_copies:
        copy.wait()
    lax.fori_loop(0, N_DOM, stage, 0)
    first = first_phase(0, stages, relays, send1, recv1)
    for half in range(2):
        deliver(0, half, 0)
    for half, step, copy in line_copies:
        copy.wait()
        spread(half, step)
    for half in range(2):
        for copy in x_copies[half, 0]:
            copy.wait()
        pick(half, 0)
        deliver(1, half, 0)

    width = KEYS - NEAR * BLK
    wanted_key = lax.broadcasted_iota(jnp.int32, (width, width), 1)
    in_late = wanted_key // (width // 2)
    within = lax.rem(wanted_key, width // 2)
    old_key = within // (2 * SPAN) * BLK + lax.rem(within, 2 * SPAN) + (1 - in_late) * 2 * SPAN
    reorder = (lax.broadcasted_iota(jnp.int32, (width, width), 0) == old_key).astype(F32).astype(BF16)

    def to_bias(row, carry):
        start = pl.multiple_of(row * BLK, BLK)
        diagonal = lax.broadcasted_iota(jnp.int32, (BLK, BLK), 0) == lax.broadcasted_iota(
            jnp.int32, (BLK, BLK), 1
        )
        far = []
        for tile in range(TILES):
            allowed = mask_ref[tile, pl.ds(start, BLK), :] > 0
            if tile == 0:
                allowed = jnp.logical_or(allowed, diagonal)
            bias = jnp.where(allowed, 0.0, NEG).astype(BF16)
            if tile < NEAR:
                bias_ref[pl.ds(start, BLK), tile * BLK : (tile + 1) * BLK] = bias
            else:
                far.append(bias)
        bias_ref[pl.ds(start, BLK), NEAR * BLK :] = nn(jnp.concatenate(far, 1), reorder).astype(BF16)
        return carry

    lax.fori_loop(0, ROWS, to_bias, 0)

    def tile_of(slot, carry):
        found = jnp.int32(FAR)
        for row in range(ROWS):
            for tile in range(TILES - NEAR):
                found = jnp.where(slot_ref[row, tile] == slot, row * (TILES - NEAR) + tile, found)
        tile_ref[0, slot] = found
        return carry

    lax.fori_loop(0, 2 * N_DOM, tile_of, 0)
    for half, step, copy in first:
        copy.wait()
        deliver(0, half, step)
    for group in range(1, 4):
        for half in range(2):
            for copy in x_copies[half, group]:
                copy.wait()
            pick(half, group)
            deliver(1, half, group)
    for copy in kept:
        copy.wait()
    for copy in second:
        copy.wait()


SUM_ROWS = (4096, 2048)


def rows_at(index, size):
    return pl.ds(pl.multiple_of(index * size, size), size)


def layer_kernel(
    local_ref, slot_ref, tile_ref, wanted_ref, feat_ref, part_0, part_a, part_b, far_a, far_b, bias_ref, d_out_ref,
    wq_ref, wk_ref, wv_ref, wo_ref, we_ref, wr_ref, gain_a_ref, gain_f_ref,
    out_ref, base_ref, cross_ref, sum_0, sum_1,
    fs, ks, vs, qs, ps, mixed, d_mixed, d_query, far_keys_t, far_values_t, near_keys_t, near_values_t,
    far_early, far_late, near_tiles, pair_acc, query_acc, expand_acc, reduce_acc, out_acc,
    grads_0, grads_1, stage_a, stage_b, relay_a, relay_b, land_a, land_b, acc, near_acc, chosen, cross_send,
    plane_a, plane_b, plane_land, line_send, line_land, axis_send, axis_land, axis_own,
    core_recv_0, core_sum_0, x_recv_0, x_sum_0, spot_recv_0, spot_sum_0, x_all_0,
    core_recv_1, core_sum_1, spot_recv_1, spot_sum_1, x_recv_1, x_sum_1, spot_all_1,
    send1, recv1, send2, recv2, plane_sems, line_sems, axis_sems, cross_sems, core_sems, x_sems, spot_sems,
):
    dom = lax.axis_index("dom")
    z, y, core, node = place()
    axis = (z, y)
    sources, relays, lands = (stage_a, stage_b), (relay_a, relay_b), (land_a, land_b)
    planes = (plane_a, plane_b)
    barrier = pltpu.get_barrier_semaphore()
    peers = [(dom_peer(dom, offset), node) for offset in OFFSETS]
    peers += [(dom, four(node + step)) for step in range(1, N_NODE)]
    for peer in peers:
        pl.semaphore_signal(barrier, inc=1, device_id=peer, device_id_type=MESH)

    scale = 1.0 / math.sqrt(D // HEADS)
    log2e = math.log2(math.e)
    expand_acc[...] = jnp.zeros(expand_acc.shape, F32)
    reduce_acc[...] = jnp.zeros(reduce_acc.shape, F32)
    out_acc[...] = jnp.zeros(out_acc.shape, F32)
    qs[...] = nn(feat_ref[...], wq_ref[...]).astype(BF16)
    lane_head = lax.broadcasted_iota(jnp.int32, (1, D), 1) // (D // HEADS)
    head_f32 = [(lane_head == h).astype(F32) for h in range(HEADS)]
    head_low = [mask.astype(BF16) for mask in head_f32]

    def forward_row(row, carry):
        start = pl.multiple_of(row * BLK, BLK)
        fs[row, 0:BLK] = feat_ref[pl.ds(start, BLK), :]
        for tile in range(NEAR - 1):
            block = local_ref[tile, row]
            top = (tile + 1) * BLK
            fs[row, top : top + 2 * SPAN] = part_0[block]
            fs[row, top + 2 * SPAN : top + 3 * SPAN] = part_a[block]
            fs[row, top + 3 * SPAN : top + 4 * SPAN] = part_b[block]
        for tile in range(TILES - NEAR):
            slot = slot_ref[row, tile]
            asked = slot // 2
            dz = four(z + 4 - asked // 8)
            dy = four(y + 4 - four(asked // 2))
            dc = two(core + two(asked))
            for chunk in range(CHUNKS):
                top = (EARLY, LATE)[1 - chunk] + 2 * tile * SPAN
                fs[row, top : top + SPAN] = far_a[chunk, dz, dy, dc, two(slot)]
                fs[row, top + SPAN : top + 2 * SPAN] = far_b[chunk, dy, dz, dc, two(slot)]
        tile_rows = fs[row]
        keys = nn(tile_rows, wk_ref[...]).astype(BF16)
        ks[row] = keys
        values = nn(tile_rows, wv_ref[...]).astype(BF16)
        vs[row] = values
        query = qs[pl.ds(start, BLK), :]
        bias = bias_ref[pl.ds(start, BLK), :].astype(F32)
        total = jnp.zeros((BLK, D), F32)
        for pair in range(HEADS // 2):
            both = jnp.concatenate([query * head_low[2 * pair], query * head_low[2 * pair + 1]], 0)
            scores = nt(both, keys) * (scale * log2e)
            lows = []
            for half in range(2):
                mine = scores[half * BLK : (half + 1) * BLK] + bias
                top = jnp.max(mine, -1, keepdims=True)
                weight = jnp.exp2(mine - top)
                norm = 1.0 / jnp.sum(weight, -1, keepdims=True)
                lows.append((weight * norm).astype(BF16))
            probs_low = jnp.concatenate(lows, 0)
            ps[row, 2 * pair * BLK : (2 * pair + 2) * BLK, :] = probs_low
            got = nn(probs_low, values)
            total = total + got[:BLK] * head_f32[2 * pair] + got[BLK:] * head_f32[2 * pair + 1]
        mixed[pl.ds(start, BLK), :] = total
        return carry

    lax.fori_loop(0, ROWS, forward_row, 0)

    size = 256

    def feed(step, carry):
        start = pl.multiple_of(step * size, size)
        sel = pl.ds(start, size)
        mixed_low = mixed[sel, :].astype(BF16)
        gain_a = gain_a_ref[...]
        gain_f = gain_f_ref[...]
        residual = feat_ref[sel, :].astype(F32) + nn(mixed_low, wo_ref[...])
        center = residual - jnp.mean(residual, -1, keepdims=True)
        rstd_a = lax.rsqrt(jnp.mean(center * center, -1, keepdims=True) + EPSILON)
        hat_a = center * rstd_a
        first_low = (hat_a * gain_a).astype(BF16)
        pre = nn(first_low, we_ref[...])
        root = math.sqrt(2.0 / math.pi)
        square = pre * pre
        tanh = jnp.tanh(root * (pre + 0.044715 * (square * pre)))
        half = 0.5 * (1.0 + tanh)
        act_low = (pre * half).astype(BF16)
        slope = half + 0.5 * pre * (1.0 - tanh * tanh) * (root * (1.0 + 3.0 * 0.044715 * square))
        second = first_low.astype(F32) + nn(act_low, wr_ref[...])
        center = second - jnp.mean(second, -1, keepdims=True)
        rstd_f = lax.rsqrt(jnp.mean(center * center, -1, keepdims=True) + EPSILON)
        hat_f = center * rstd_f
        out_ref[sel, :] = (hat_f * gain_f).astype(BF16)
        d_hat = d_out_ref[sel, :].astype(F32) * gain_f
        d_second = rstd_f * (
            d_hat - jnp.mean(d_hat, -1, keepdims=True) - hat_f * jnp.mean(d_hat * hat_f, -1, keepdims=True)
        )
        d_second_low = d_second.astype(BF16)
        reduce_acc[...] += tn(d_second_low, act_low)
        d_pre_low = (nt(d_second_low, wr_ref[...]) * slope).astype(BF16)
        expand_acc[...] += tn(first_low, d_pre_low)
        d_first = d_second + nt(d_pre_low, we_ref[...])
        d_hat = d_first * gain_a
        d_resid = rstd_a * (
            d_hat - jnp.mean(d_hat, -1, keepdims=True) - hat_a * jnp.mean(d_hat * hat_a, -1, keepdims=True)
        )
        base_ref[sel, :] = d_resid
        d_resid_low = d_resid.astype(BF16)
        out_acc[...] += tn(mixed_low, d_resid_low)
        d_mixed[sel, :] = nt(d_resid_low, wo_ref[...]).astype(BF16)
        return carry

    lax.fori_loop(0, ROWS * BLK // size, feed, 0)

    def pack(accs, grads):
        spot = 0
        for total in accs:
            for top in range(0, total.shape[0], D):
                for left in range(0, total.shape[1], BLK):
                    grads[spot : spot + D, :] = total[top : top + D, left : left + BLK].astype(BF16)
                    spot += D

    def push(src, dst, sems, key, target):
        copy = pltpu.make_async_remote_copy(
            src_ref=src, dst_ref=dst, send_sem=sems.at[(0,) + key], recv_sem=sems.at[(1,) + key],
            device_id=target, device_id_type=MESH,
        )
        copy.start()
        return copy

    def finish(copies):
        for copy in copies:
            copy.wait()

    spot_here = z * 4 + y
    x_line = [four(node + step) for step in range(1, 4)]
    x_line = [(other, (dom, other)) for other in x_line]
    spots = [lax.rem(spot_here + step, 16) for step in range(1, 16)]
    spots = [(other, (other * 2 + core, node)) for other in spots]
    sibling = device(z, y, two(core + 1), node)

    def reduction(number, grads, total_ref, core_recv, core_sum, recvs, sums, near_all):
        lines = [(x_line, node, x_sems), (spots, spot_here, spot_sems)]
        if number == 1:
            lines.reverse()
        counts = [len(line[0]) + 1 for line in lines]
        core_rows = SUM_ROWS[number] // 2
        sizes = [core_rows // counts[0], core_rows // counts[0] // counts[1]]
        mine = rows_at(core, core_rows)

        def scatter(line, src, dst, count):
            members, own, sems = line
            return [
                push(src.at[rows_at(other, count)], dst.at[index], sems, (number, 0, index), target)
                for index, (other, target) in enumerate(members)
            ]

        def gather(line, src, dst, count):
            members, own, sems = line
            copies = [
                push(src, dst.at[rows_at(own, count)], sems, (number, 1, index), target)
                for index, (other, target) in enumerate(members)
            ]
            dst[rows_at(own, count), :] = src[...]
            return copies

        def add_up(line, src, recv, out, count):
            total = src[rows_at(line[1], count), :].astype(F32)
            for index in range(recv.shape[0]):
                total = total + recv[index].astype(F32)
            out[...] = total.astype(BF16)

        copy = push(grads.at[rows_at(two(core + 1), core_rows)], core_recv, core_sems, (number, 0), sibling)
        yield
        copy.wait()
        core_sum[...] = (grads[mine, :].astype(F32) + core_recv[...].astype(F32)).astype(BF16)
        copies = scatter(lines[0], core_sum, recvs[0], sizes[0])
        yield
        finish(copies)
        add_up(lines[0], core_sum, recvs[0], sums[0], sizes[0])
        copies = scatter(lines[1], sums[0], recvs[1], sizes[1])
        yield
        finish(copies)
        add_up(lines[1], sums[0], recvs[1], sums[1], sizes[1])
        copies = gather(lines[1], sums[1], near_all, sizes[1])
        yield
        finish(copies)
        my_part = total_ref.at[mine]
        copies = gather(lines[0], near_all, my_part, sizes[0])
        yield
        finish(copies)
        copy = push(my_part, my_part, core_sems, (number, 1), sibling)
        yield
        copy.wait()
        yield

    first_half = lax.broadcasted_iota(jnp.int32, (64, BLK), 0) < 32

    def block_diagonal(turned, pair):
        piece = turned[64 * pair : 64 * pair + 64]
        return jnp.concatenate(
            [jnp.where(first_half, piece, 0.0), jnp.where(first_half, 0.0, piece)], 1
        ).astype(BF16)

    def backward(row, begin, end):
        start = pl.multiple_of(row * BLK, BLK)
        keys = ks[row, begin:end]
        values = vs[row, begin:end]
        query = qs[pl.ds(start, BLK), :]
        grad = d_mixed[pl.ds(start, BLK), :]
        query_t = query.astype(F32).T
        grad_t = grad.astype(F32).T
        inner_full = grad.astype(F32) * mixed[pl.ds(start, BLK), :]
        query_part = jnp.zeros((BLK, D), F32)
        key_parts = []
        value_parts = []
        for pair in range(HEADS // 2):
            both = jnp.concatenate([grad * head_low[2 * pair], grad * head_low[2 * pair + 1]], 0)
            inner = jnp.concatenate(
                [
                    jnp.sum(inner_full * head_f32[2 * pair], -1, keepdims=True),
                    jnp.sum(inner_full * head_f32[2 * pair + 1], -1, keepdims=True),
                ],
                0,
            )
            probs_low = ps[row, 2 * pair * BLK : (2 * pair + 2) * BLK, begin:end]
            d_probs = nt(both, values)
            d_scores = (probs_low.astype(F32) * ((d_probs - inner) * scale)).astype(BF16)
            got = nn(d_scores, keys)
            query_part = query_part + got[:BLK] * head_f32[2 * pair] + got[BLK:] * head_f32[2 * pair + 1]
            key_parts.append(nn(block_diagonal(query_t, pair), d_scores).astype(BF16))
            value_parts.append(nn(block_diagonal(grad_t, pair), probs_low).astype(BF16))
        d_keys_t = jnp.concatenate(key_parts, 0)
        d_values_t = jnp.concatenate(value_parts, 0)
        return d_keys_t, d_values_t, nn(wk_ref[...], d_keys_t) + nn(wv_ref[...], d_values_t), query_part

    def keep_far(row, parts, begin, tiles):
        d_keys_t, d_values_t, d_rows_t = parts
        columns = slice(begin - EARLY, begin - EARLY + LATE - EARLY)
        far_keys_t[row, :, columns] = d_keys_t
        far_values_t[row, :, columns] = d_values_t
        for pair in range((TILES - NEAR) // 2):
            piece = d_rows_t[:, pair * BLK : (pair + 1) * BLK].T.astype(BF16)
            for side in range(2):
                tiles[row * (TILES - NEAR) + 2 * pair + side] = piece[side * 2 * SPAN : (side + 1) * 2 * SPAN]

    def backward_early(row, carry):
        *parts, query_part = backward(row, EARLY, LATE)
        keep_far(row, parts, EARLY, far_early)
        d_query[rows_at(row, BLK), :] = query_part
        return carry

    def backward_late(row, carry):
        *parts, query_part = backward(row, LATE, KEYS)
        keep_far(row, parts, LATE, far_late)
        d_query[rows_at(row, BLK), :] += query_part
        return carry

    def backward_near(row, carry):
        d_keys_t, d_values_t, d_rows_t, query_part = backward(row, 0, NEAR * BLK)
        near_keys_t[row] = d_keys_t
        near_values_t[row] = d_values_t
        d_query[rows_at(row, BLK), :] += query_part
        for tile in range(NEAR):
            piece = d_rows_t[:, tile * BLK : (tile + 1) * BLK].T
            near_tiles[row * NEAR + tile] = piece.astype(BF16)
        return carry

    def key_grads(row, carry):
        near_rows = fs[row, : NEAR * BLK]
        far_rows = fs[row, NEAR * BLK :]
        pair_acc[0:D, :] += nn(near_keys_t[row], near_rows) + nn(far_keys_t[row], far_rows)
        pair_acc[D : 2 * D, :] += nn(near_values_t[row], near_rows) + nn(far_values_t[row], far_rows)
        return carry

    def stage_early(peer, carry):
        peer_z, peer_y, side = peer // 8, four(peer // 2), two(peer)
        for slot in range(2):
            tile = tile_ref[0, 2 * peer + slot]
            plane_a[peer_y * 2 + side, peer_z, slot] = far_early[tile, 0:SPAN]
            plane_b[peer_z * 2 + side, peer_y, slot] = far_early[tile, SPAN : 2 * SPAN]
        return carry

    def stage_late(peer, carry):
        turned = four(peer // 2) * 8 + (peer // 8) * 2 + two(peer)
        for slot in range(2):
            tile = tile_ref[0, 2 * peer + slot]
            stage_a[0, peer, slot] = far_late[tile, 0:SPAN]
            stage_b[0, turned, slot] = far_late[tile, SPAN : 2 * SPAN]
        return carry

    def send_early(half):
        copies = []
        for step in range(4):
            for flip in range(2):
                target = four(axis[1 - half] + step)
                side = two(core + flip)
                if step == 0 and flip == 0:
                    plane_land[half, 0, 0] = planes[half][target * 2 + side]
                    continue
                copies.append(
                    push(
                        planes[half].at[target * 2 + side], plane_land.at[half, step, flip],
                        plane_sems, (half, step, flip), (dom_at(half, axis[half], target, side), node),
                    )
                )
        return copies

    def sum_early(half):
        finish(early[half])
        for ahead in range(4):
            place_there = four(axis[half] + ahead)
            owner = dom_at(half, place_there, axis[1 - half], core)
            names = []
            for step in range(4):
                for flip in range(2):
                    asker = dom_at(half, axis[half], four(axis[1 - half] + 4 - step), two(core + flip))
                    names += [wanted_ref[asker, 0, 2 * owner + slot] for slot in range(2)]
            chosen[half, ahead] = selection(names)
            for top in range(0, SPAN, 16):
                arrived = plane_land[half, :, :, place_there, :, top : top + 16, :].reshape(256, D)
                total = nn(chosen[half, ahead], arrived).reshape(PART, 16, D)
                if ahead == 0:
                    total = total + near_acc[:, half * SPAN + top : half * SPAN + top + 16, :]
                line_send[half, ahead, :, top : top + 16, :] = total.astype(BF16)
        return [
            push(
                line_send.at[half, :, pl.ds(other * ROWS, ROWS)], line_land.at[half, index],
                line_sems, (half, index), target,
            )
            for index, (other, target) in enumerate(x_line)
        ]

    def turn_early(half):
        finish(lined[half])
        copies = []
        for ahead in range(4):
            total = line_send[half, ahead, pl.ds(node * ROWS, ROWS)].astype(F32)
            for index in range(3):
                total = total + line_land[half, index, ahead].astype(F32)
            if ahead == 0:
                axis_own[half] = total
            else:
                axis_send[half, ahead - 1] = total.astype(BF16)
                there = four(axis[half] + ahead)
                copies.append(
                    push(
                        axis_send.at[half, ahead - 1], axis_land.at[half, ahead - 1],
                        axis_sems, (half, ahead - 1), (dom_at(half, there, axis[1 - half], core), node),
                    )
                )
        return copies

    def end_early(half):
        finish(turned_copies[half])
        for row in range(ROWS):
            total = axis_own[half, row]
            for index in range(3):
                total = total + axis_land[half, index, row].astype(F32)
            top = row * BLK + (2 + half) * SPAN
            base_ref[top : top + SPAN, :] += total

    block_of = lax.broadcasted_iota(jnp.int32, (256, 256), 0) // 16
    same_row = lax.rem(lax.broadcasted_iota(jnp.int32, (256, 256), 0), 16) == lax.rem(
        lax.broadcasted_iota(jnp.int32, (256, 256), 1), 16
    )
    slot_of = lax.broadcasted_iota(jnp.int32, (1, 256), 1) // 16

    def selection(values):
        names = jnp.full((1, 256), -1, jnp.int32)
        for index, value in enumerate(values):
            names = jnp.where(slot_of == index, value, names)
        return jnp.logical_and(names == block_of, same_row).astype(F32).astype(BF16)

    def relay_on(arrivals):
        for half, step, copy in arrivals:
            copy.wait()
            second[half, step] = second_phase(0, half, step, sources, relays, lands, send2, recv2)
            lands[half][0, step, 0, 0] = relays[half][0, step - 1, (y, z)[half] * 2 + core]

    def combine(group):
        for half in range(2):
            finish(second[half, group])
            names = [
                wanted_ref[origin(half, group, step, flip), 0, 2 * dom + slot]
                for step in range(4)
                for flip in range(2)
                for slot in range(2)
            ]
            chosen[half, group] = selection(names)
            for top in range(0, SPAN, 16):
                rows = slice(half * SPAN + top, half * SPAN + top + 16)
                arrived = lands[half][0, group, :, :, :, top : top + 16, :].reshape(256, D)
                acc[:, rows, :] += nn(chosen[half, group], arrived).reshape(PART, 16, D)

    def cross():
        cross_send[...] = acc[...].astype(BF16)
        copies = []
        for step in range(1, N_NODE):
            other = four(node + step)
            copies.append(
                push(
                    cross_send.at[pl.ds(other * ROWS, ROWS)], cross_ref.at[step - 1],
                    cross_sems, (step - 1,), (dom, other),
                )
            )
        return copies

    pack((expand_acc, reduce_acc), grads_0)
    pl.semaphore_wait(barrier, len(peers))
    wide = reduction(
        0, grads_0, sum_0, core_recv_0, core_sum_0, (x_recv_0, spot_recv_0), (x_sum_0, spot_sum_0), x_all_0
    )
    next(wide)
    for tiles in (far_early, far_late):
        tiles[FAR] = jnp.zeros((2 * SPAN, D), BF16)
    lax.fori_loop(0, ROWS, backward_early, 0)
    next(wide)
    lax.fori_loop(0, N_DOM, stage_early, 0)
    early = [send_early(half) for half in range(2)]
    lax.fori_loop(0, ROWS, backward_late, 0)
    lax.fori_loop(0, N_DOM, stage_late, 0)
    next(wide)
    first = first_phase(0, sources, relays, send1, recv1)
    second = {}
    for half in range(2):
        second[half, 0] = second_phase(0, half, 0, sources, relays, lands, send2, recv2)
        lands[half][0, 0, 0, 0] = sources[half][0, (dom, y * 8 + z * 2 + core)[half]]

    near_tiles[ROWS * NEAR : PART] = jnp.zeros((PART - ROWS * NEAR, BLK, D), BF16)
    lax.fori_loop(0, ROWS, backward_near, 0)
    near_names = []
    for row in range(ROWS):
        near_names += [node * ROWS + row, local_ref[0, row], local_ref[1, row]]
    near_chosen = selection(near_names)
    for top in range(0, BLK, 16):
        total = nn(near_chosen, near_tiles[:, top : top + 16, :].reshape(256, D)).reshape(PART, 16, D)
        if top < 2 * SPAN:
            acc[:, top : top + 16, :] = total
        else:
            near_acc[:, top - 2 * SPAN : top - 2 * SPAN + 16, :] = total
    lined = [sum_early(half) for half in range(2)]
    next(wide)
    pair_acc[...] = jnp.zeros(pair_acc.shape, F32)
    lax.fori_loop(0, ROWS, key_grads, 0)
    d_query_low = d_query[...].astype(BF16)
    query_acc[...] = tn(feat_ref[...], d_query_low)
    pack((query_acc, pair_acc, out_acc), grads_1)
    narrow = reduction(
        1, grads_1, sum_1, core_recv_1, core_sum_1, (spot_recv_1, x_recv_1), (spot_sum_1, x_sum_1), spot_all_1
    )
    next(narrow)
    base_ref[...] += nt(d_query_low, wq_ref[...])
    next(narrow)
    relay_on(first[:3])
    next(narrow)
    next(wide)
    relay_on(first[3:])
    combine(0)
    combine(1)
    next(narrow)
    turned_copies = [turn_early(half) for half in range(2)]
    next(narrow)
    next(wide)
    combine(2)
    combine(3)
    crossing = cross()
    next(narrow)
    next(wide)
    for half in range(2):
        end_early(half)
    for row in range(ROWS):
        base_ref[row * BLK : row * BLK + 2 * SPAN, :] += acc[node * ROWS + row]
    next(narrow)
    finish(crossing)


def finish_kernel(factor, result_ref, base_ref, cross_ref, sum_0, sum_1, out_ref, dx_ref, gq, gk, gv, go, ge, gr):
    out_ref[...] = result_ref[...]
    for row in range(ROWS):
        span = slice(row * BLK, row * BLK + 2 * SPAN)
        total = base_ref[span, :]
        for step in range(N_NODE - 1):
            total = total + cross_ref[step, row].astype(F32)
        dx_ref[span, :] = total.astype(BF16)
        span = slice(row * BLK + 2 * SPAN, (row + 1) * BLK)
        dx_ref[span, :] = base_ref[span, :].astype(BF16)

    def piece(ref, index):
        return ref[index * D : (index + 1) * D, :].astype(F32) * factor

    for half in range(2):
        span = slice(half * BLK, (half + 1) * BLK)
        gq[:, span] = piece(sum_1, half)
        gk[span, :] = piece(sum_1, 2 + half).T
        gv[span, :] = piece(sum_1, 4 + half).T
        go[:, span] = piece(sum_1, 6 + half)
    for part in range(8):
        span = slice(part * BLK, (part + 1) * BLK)
        ge[:, span] = piece(sum_0, part)
        gr[span, :] = piece(sum_0, 8 + part).T


def vmem(shape, dtype):
    return pltpu.VMEM(shape, dtype)


IN_VMEM = pl.BlockSpec(memory_space=pltpu.VMEM)
IN_SMEM = pl.BlockSpec(memory_space=pltpu.SMEM)
ANYWHERE = pl.BlockSpec(memory_space=pl.ANY)


def on_device(
    features, w_query, w_key, w_value, w_out, w_expand, w_reduce, gain_attn, gain_ffn,
    tile_mask, local_block, remote_slot, remote_block, d_out,
):
    rows = features.shape[0]
    dma = pltpu.SemaphoreType.DMA
    peers = len(OFFSETS)
    land = (CHUNKS, 4, 4, 2, 2, SPAN, D)
    staged = (CHUNKS, N_DOM, 2, SPAN, D)
    relay = (CHUNKS, 3, 8, 2, SPAN, D)
    phase_sems = [dma((CHUNKS, 2, 3)), dma((CHUNKS, 2, 3)), dma((CHUNKS, 2, 4, 4, 2)), dma((CHUNKS, 2, 4, 4, 2))]
    part_0, part_a, part_b, land_a, land_b, wanted, bias, tile_of = pl.pallas_call(
        exchange_kernel,
        out_shape=(
            jax.ShapeDtypeStruct((PART, 2 * SPAN, D), BF16),
            jax.ShapeDtypeStruct((PART, SPAN, D), BF16),
            jax.ShapeDtypeStruct((PART, SPAN, D), BF16),
            jax.ShapeDtypeStruct(land, BF16),
            jax.ShapeDtypeStruct(land, BF16),
            jax.ShapeDtypeStruct((N_DOM, 1, BLK), jnp.int32),
            jax.ShapeDtypeStruct((rows, KEYS), BF16),
            jax.ShapeDtypeStruct((1, 2 * N_DOM), jnp.int32),
        ),
        in_specs=[IN_VMEM, IN_VMEM, IN_SMEM, IN_VMEM],
        out_specs=(IN_VMEM, IN_VMEM, IN_VMEM, ANYWHERE, ANYWHERE, IN_VMEM, IN_VMEM, IN_SMEM),
        scratch_shapes=[
            vmem((1, BLK), jnp.int32), vmem(staged, BF16), vmem(staged, BF16),
            vmem(relay, BF16), vmem(relay, BF16), pltpu.SMEM((N_DOM, 1, BLK), jnp.int32),
        ]
        + [vmem((PART, SPAN, D), BF16)] * 6
        + [dma((N_NODE - 1,)), dma((N_NODE - 1,)), dma((peers,)), dma((peers,))]
        + phase_sems
        + [dma((2, 3)), dma((2, 3)), dma((2, 4, 3)), dma((2, 4, 3)), dma((CHUNKS, 2, 4)), dma],
        compiler_params=pltpu.CompilerParams(
            collective_id=1, has_side_effects=True, vmem_limit_bytes=VMEM_LIMIT
        ),
        name="exchange",
    )(features.reshape(ROWS, BLK, D), remote_block.reshape(1, 2 * N_DOM), remote_slot, jnp.transpose(tile_mask, (1, 0, 2)))

    sum_scratch = []
    for total, lines in zip(SUM_ROWS, ((4, 16), (16, 4))):
        half = total // 2
        sum_scratch += [vmem((half, BLK), BF16), vmem((half, BLK), BF16)]
        for count in lines:
            half = half // count
            sum_scratch += [vmem((count - 1, half, BLK), BF16), vmem((half, BLK), BF16)]
        sum_scratch.append(vmem((total // 2 // lines[0], BLK), BF16))
    result, base, cross, sum_0, sum_1 = pl.pallas_call(
        layer_kernel,
        out_shape=(
            jax.ShapeDtypeStruct((rows, D), BF16),
            jax.ShapeDtypeStruct((rows, D), F32),
            jax.ShapeDtypeStruct((N_NODE - 1, ROWS, 2 * SPAN, D), BF16),
            jax.ShapeDtypeStruct((SUM_ROWS[0], BLK), BF16),
            jax.ShapeDtypeStruct((SUM_ROWS[1], BLK), BF16),
        ),
        in_specs=[IN_SMEM] * 4 + [IN_VMEM] * 16,
        out_specs=(IN_VMEM,) * 5,
        scratch_shapes=[
            vmem((ROWS, KEYS, D), BF16), vmem((ROWS, KEYS, D), BF16), vmem((ROWS, KEYS, D), BF16),
            vmem((rows, D), BF16), vmem((ROWS, HEADS * BLK, KEYS), BF16), vmem((rows, D), F32),
            vmem((rows, D), BF16), vmem((rows, D), F32),
            vmem((ROWS, D, KEYS - NEAR * BLK), BF16), vmem((ROWS, D, KEYS - NEAR * BLK), BF16),
            vmem((ROWS, D, NEAR * BLK), BF16), vmem((ROWS, D, NEAR * BLK), BF16),
            vmem((FAR + 1, 2 * SPAN, D), BF16), vmem((FAR + 1, 2 * SPAN, D), BF16), vmem((PART, BLK, D), BF16),
            vmem((2 * D, D), F32), vmem((D, D), F32), vmem((D, 4 * D), F32), vmem((D, 4 * D), F32), vmem((D, D), F32),
            vmem((SUM_ROWS[0], BLK), BF16), vmem((SUM_ROWS[1], BLK), BF16),
            vmem((1,) + staged[1:], BF16), vmem((1,) + staged[1:], BF16),
            vmem((1,) + relay[1:], BF16), vmem((1,) + relay[1:], BF16),
            vmem((1,) + land[1:], BF16), vmem((1,) + land[1:], BF16),
            vmem((PART, 2 * SPAN, D), F32), vmem((PART, 2 * SPAN, D), F32),
            vmem((2, 4, 256, 256), BF16), vmem((PART, 2 * SPAN, D), BF16),
            vmem((8, 4, 2, SPAN, D), BF16), vmem((8, 4, 2, SPAN, D), BF16), vmem((2, 4, 2, 4, 2, SPAN, D), BF16),
            vmem((2, 4, PART, SPAN, D), BF16), vmem((2, 3, 4, ROWS, SPAN, D), BF16),
            vmem((2, 3, ROWS, SPAN, D), BF16), vmem((2, 3, ROWS, SPAN, D), BF16), vmem((2, ROWS, SPAN, D), F32),
        ]
        + sum_scratch
        + [dma((1, 2, 3)), dma((1, 2, 3)), dma((1, 2, 4, 4, 2)), dma((1, 2, 4, 4, 2))]
        + [dma((2, 2, 4, 2)), dma((2, 2, 3)), dma((2, 2, 3)), dma((2, 3)), dma((2, 2, 2)), dma((2, 2, 2, 3)), dma((2, 2, 2, 15))],
        compiler_params=pltpu.CompilerParams(
            collective_id=2, has_side_effects=True, vmem_limit_bytes=VMEM_LIMIT
        ),
        name="layer",
    )(
        local_block.T, remote_slot, tile_of, wanted, features, part_0, part_a, part_b, land_a, land_b, bias, d_out,
        w_query, w_key, w_value, w_out, w_expand, w_reduce, gain_attn.reshape(1, D), gain_ffn.reshape(1, D),
    )

    factor = 1.0 / math.sqrt(rows * N_DOM * N_NODE)
    return pl.pallas_call(
        functools.partial(finish_kernel, factor),
        out_shape=(
            jax.ShapeDtypeStruct((rows, D), BF16),
            jax.ShapeDtypeStruct((rows, D), BF16),
            jax.ShapeDtypeStruct((D, D), F32),
            jax.ShapeDtypeStruct((D, D), F32),
            jax.ShapeDtypeStruct((D, D), F32),
            jax.ShapeDtypeStruct((D, D), F32),
            jax.ShapeDtypeStruct((D, 4 * D), F32),
            jax.ShapeDtypeStruct((4 * D, D), F32),
        ),
        in_specs=[IN_VMEM] * 5,
        out_specs=(IN_VMEM,) * 8,
        compiler_params=pltpu.CompilerParams(vmem_limit_bytes=VMEM_LIMIT),
        name="finish",
    )(result, base, cross, sum_0, sum_1)


def solution(mesh):
    split = P(("dom", "node"), None)
    placed = (
        (split,) + (P(),) * 8 + (P(("dom", "node"), None, None), split, split, P("dom", "node", None), split)
    )
    return jax.shard_map(
        on_device, mesh=mesh, in_specs=placed, out_specs=(split, split) + (P(),) * 6, check_vma=False
    )
```

```python
import functools
import math

import jax
import jax.numpy as jnp
from jax import lax
from jax.experimental import pallas as pl
from jax.experimental.pallas import tpu as pltpu
from jax.sharding import PartitionSpec as P

HEADS = 8
EPSILON = 1e-05
MESH = pl.DeviceIdType.MESH
F32 = jnp.float32
BF16 = jnp.bfloat16
NEG = -1e30
VMEM_LIMIT = 62 << 20

D = 256
BLK = 128
TILES = 7
NEAR = 3
ROWS = 4
PART = 16
KEYS = TILES * BLK
FAR = ROWS * (TILES - NEAR)
EARLY = NEAR * BLK
LATE = EARLY + (KEYS - EARLY) // 2
N_DOM = 32
N_NODE = 4
CHUNKS = 2
SPAN = BLK // (2 * CHUNKS)

_GROUPS = [
    [(2, 2)],
    [(2, 1), (2, 3)],
    [(1, 2), (3, 2)],
    [(1, 1), (3, 3)],
    [(1, 3), (3, 1)],
    [(2, 0), (0, 2)],
    [(1, 0), (3, 0), (0, 1), (0, 3)],
]
OFFSETS = [(a, b, c) for group in _GROUPS for c in range(2) for a, b in group] + [(0, 0, 1)]


def dom_peer(dom, offset, sign=1):
    core = lax.rem(dom, 2)
    y = lax.rem(dom // 2, 4)
    z = dom // 8
    dz, dy, dc = offset
    return (
        lax.rem(z + (dz if sign > 0 else 4 - dz), 4) * 8
        + lax.rem(y + (dy if sign > 0 else 4 - dy), 4) * 2
        + lax.rem(core + dc, 2)
    )


def nt(a, b):
    return lax.dot_general(a, b, (((1,), (1,)), ((), ())), preferred_element_type=F32)


def tn(a, b):
    return lax.dot_general(a, b, (((0,), (0,)), ((), ())), preferred_element_type=F32)


def nn(a, b):
    return jnp.dot(a, b, preferred_element_type=F32)


def place():
    dom = lax.axis_index("dom")
    return dom // 8, lax.rem(dom // 2, 4), lax.rem(dom, 2), lax.axis_index("node")


def device(z, y, core, node):
    return (z * 8 + y * 2 + core, node)


def four(value):
    return lax.rem(value, 4)


def two(value):
    return lax.rem(value, 2)


def first_step(chunk, half, step, sources, relays, sends, recvs):
    z, y, core, node = place()
    target = four((z, y)[half] + step)
    copy = pltpu.make_async_remote_copy(
        src_ref=sources[half].at[chunk, pl.ds(target * 8, 8)],
        dst_ref=relays[half].at[chunk, step - 1],
        send_sem=sends.at[chunk, half, step - 1], recv_sem=recvs.at[chunk, half, step - 1],
        device_id=(device(target, y, core, node), device(z, target, core, node))[half],
        device_id_type=MESH,
    )
    copy.start()
    return half, step, copy


def second_phase(chunk, half, group, sources, relays, lands, sends, recvs):
    z, y, core, node = place()
    copies = []
    for step in range(4):
        for flip in range(2):
            if step == 0 and flip == 0:
                continue
            target = four((y, z)[half] + step)
            side = two(core + flip)
            if group == 0:
                source = sources[half].at[chunk, (z, y)[half] * 8 + target * 2 + side]
            else:
                source = relays[half].at[chunk, group - 1, target * 2 + side]
            copy = pltpu.make_async_remote_copy(
                src_ref=source, dst_ref=lands[half].at[chunk, group, step, flip],
                send_sem=sends.at[chunk, half, group, step, flip],
                recv_sem=recvs.at[chunk, half, group, step, flip],
                device_id=(device(z, target, side, node), device(target, y, side, node))[half],
                device_id_type=MESH,
            )
            copy.start()
            copies.append(copy)
    return copies


def origin(half, group, step, flip):
    z, y, core, node = place()
    far, near = 4 - group, 4 - step
    if half == 0:
        return four(z + far) * 8 + four(y + near) * 2 + two(core + flip)
    return four(z + near) * 8 + four(y + far) * 2 + two(core + flip)


def dom_at(half, along, across, side):
    first, other = ((along, across), (across, along))[half]
    return first * 8 + other * 2 + side


def exchange_kernel(
    feat_ref, table_ref, slot_ref, mask_ref,
    part_0, part_1, part_a, part_b, land_a, land_b, wanted_ref, bias_ref, tile_ref,
    row_ref, stage_a, stage_b, relay_a, relay_b, ids_smem, held_a1, held_a2, held_a3, held_b1, held_b2, held_b3,
    near_send, near_recv, id_send, id_recv, send1, recv1, send2, recv2, line_send, line_recv, x_send, x_recv,
    own_sem, local_sem,
):
    dom = lax.axis_index("dom")
    z, y, core, node = place()
    axis = (z, y)
    stages, relays, lands = (stage_a, stage_b), (relay_a, relay_b), (land_a, land_b)
    held = ((part_a, held_a1, held_a2, held_a3), (part_b, held_b1, held_b2, held_b3))
    barrier = pltpu.get_barrier_semaphore()
    for offset in OFFSETS:
        pl.semaphore_signal(barrier, inc=1, device_id=(dom_peer(dom, offset), node), device_id_type=MESH)
    x_line = [(dom, four(node + step)) for step in range(1, N_NODE)]
    for target in x_line:
        pl.semaphore_signal(barrier, inc=1, device_id=target, device_id_type=MESH)
    row_ref[:, 0 : 2 * N_DOM] = table_ref[...]
    mine = pl.ds(node * ROWS, ROWS)
    late = (part_0, part_1)
    for half in range(2):
        late[half][mine] = feat_ref[:, half * SPAN : (half + 1) * SPAN]
        held[half][0][mine] = feat_ref[:, (2 + half) * SPAN : (3 + half) * SPAN]
    pl.semaphore_wait(barrier, len(OFFSETS) + N_NODE - 1)

    def push(src, dst, send, recv, target):
        copy = pltpu.make_async_remote_copy(
            src_ref=src, dst_ref=dst, send_sem=send, recv_sem=recv, device_id=target, device_id_type=MESH
        )
        copy.start()
        return copy

    id_copies = [
        push(row_ref, wanted_ref.at[dom], id_send.at[index], id_recv.at[index], (dom_peer(dom, offset), node))
        for index, offset in enumerate(OFFSETS)
    ]
    near_copies = [
        [
            push(
                feat_ref.at[:, pl.ds(half * SPAN, SPAN)], late[half].at[mine],
                near_send.at[half, index], near_recv.at[half, index], target,
            )
            for index, target in enumerate(x_line)
        ]
        for half in range(2)
    ]
    line_copies = []
    for step in range(1, 4):
        for half in range(2):
            target = (device(four(z + step), y, core, node), device(z, four(y + step), core, node))[half]
            copy = push(
                feat_ref.at[:, pl.ds((2 + half) * SPAN, SPAN)], held[half][step].at[mine],
                line_send.at[half, step - 1], line_recv.at[half, step - 1], target,
            )
            line_copies.append((half, step, copy))
    x_copies = {}

    def spread(half, group):
        if group == 0:
            source = feat_ref.at[:, pl.ds((2 + half) * SPAN, SPAN)]
        else:
            source = held[half][group].at[mine]
        x_copies[half, group] = [
            push(
                source, held[half][group].at[mine],
                x_send.at[half, group, index], x_recv.at[half, group, index], target,
            )
            for index, target in enumerate(x_line)
        ]

    for half in range(2):
        spread(half, 0)
    wanted_ref[dom] = row_ref[...]
    for copy in id_copies:
        copy.wait()
    to_smem = pltpu.make_async_copy(wanted_ref, ids_smem, local_sem)
    to_smem.start()
    to_smem.wait()

    def stage(half, there):
        def body(index, carry):
            peer = dom_at(half, there, index // 2, two(index))
            for slot in range(2):
                stages[half][0, there * 8 + index, slot] = late[half][ids_smem[peer, 0, 2 * dom + slot]]
            return carry

        lax.fori_loop(0, 8, body, 0)

    def pick(half, group):
        owner = dom_at(half, four(axis[half] + 4 - group), axis[1 - half], core)

        def body(index, carry):
            asker = dom_at(half, axis[half], index // 2, two(index))
            for slot in range(2):
                block = ids_smem[asker, 0, 2 * owner + slot]
                rows = held[half][group][block]
                if group == 0:
                    stages[half][1, axis[half] * 8 + index, slot] = rows
                else:
                    relays[half][1, group - 1, index, slot] = rows
            return carry

        lax.fori_loop(0, 8, body, 0)

    second = []
    kept = []

    def deliver(chunk, half, group):
        second.extend(second_phase(chunk, half, group, stages, relays, lands, send2, recv2))
        if group == 0:
            source = stages[half].at[chunk, axis[half] * 8 + axis[1 - half] * 2 + core]
        else:
            source = relays[half].at[chunk, group - 1, axis[1 - half] * 2 + core]
        copy = pltpu.make_async_copy(
            source, lands[half].at[chunk, group, 0, 0], own_sem.at[chunk, half, group]
        )
        copy.start()
        kept.append(copy)

    first = []
    for half in range(2):
        for copy in near_copies[half]:
            copy.wait()
        for step in range(1, 4):
            stage(half, four(axis[half] + step))
            first.append(first_step(0, half, step, stages, relays, send1, recv1))
    for half in range(2):
        stage(half, axis[half])
        deliver(0, half, 0)
    for half, step, copy in line_copies:
        copy.wait()
        spread(half, step)
    for half in range(2):
        for copy in x_copies[half, 0]:
            copy.wait()
        pick(half, 0)
        deliver(1, half, 0)

    width = KEYS - NEAR * BLK
    wanted_key = lax.broadcasted_iota(jnp.int32, (width, width), 1)
    in_late = wanted_key // (width // 2)
    within = lax.rem(wanted_key, width // 2)
    old_key = within // (2 * SPAN) * BLK + lax.rem(within, 2 * SPAN) + (1 - in_late) * 2 * SPAN
    reorder = (lax.broadcasted_iota(jnp.int32, (width, width), 0) == old_key).astype(F32).astype(BF16)

    def to_bias(row, carry):
        start = pl.multiple_of(row * BLK, BLK)
        diagonal = lax.broadcasted_iota(jnp.int32, (BLK, BLK), 0) == lax.broadcasted_iota(
            jnp.int32, (BLK, BLK), 1
        )
        far = []
        for tile in range(TILES):
            allowed = mask_ref[tile, pl.ds(start, BLK), :] > 0
            if tile == 0:
                allowed = jnp.logical_or(allowed, diagonal)
            bias = jnp.where(allowed, 0.0, NEG).astype(BF16)
            if tile < NEAR:
                bias_ref[pl.ds(start, BLK), tile * BLK : (tile + 1) * BLK] = bias
            else:
                far.append(bias)
        bias_ref[pl.ds(start, BLK), NEAR * BLK :] = nn(jnp.concatenate(far, 1), reorder).astype(BF16)
        return carry

    lax.fori_loop(0, ROWS, to_bias, 0)

    def tile_of(slot, carry):
        found = jnp.int32(FAR)
        for row in range(ROWS):
            for tile in range(TILES - NEAR):
                found = jnp.where(slot_ref[row, tile] == slot, row * (TILES - NEAR) + tile, found)
        tile_ref[0, slot] = found
        return carry

    lax.fori_loop(0, 2 * N_DOM, tile_of, 0)
    for half, step, copy in (first[0], first[3], first[1], first[4], first[2], first[5]):
        copy.wait()
        deliver(0, half, step)
    for group in range(1, 4):
        for half in range(2):
            for copy in x_copies[half, group]:
                copy.wait()
            pick(half, group)
            deliver(1, half, group)
    for copy in kept:
        copy.wait()
    for copy in second:
        copy.wait()


SUM_ROWS = (4096, 2048)


def rows_at(index, size):
    return pl.ds(pl.multiple_of(index * size, size), size)


def layer_kernel(
    local_ref, slot_ref, tile_ref, wanted_ref, feat_ref, part_0, part_1, part_a, part_b, far_a, far_b, bias_ref, d_out_ref,
    wq_ref, wk_ref, wv_ref, wo_ref, we_ref, wr_ref, gain_a_ref, gain_f_ref,
    out_ref, base_ref, cross_ref, sum_0, sum_1,
    fs, ks, vs, qs, ps, mixed, d_mixed, d_query, far_keys_t, far_values_t, near_keys_t, near_values_t,
    far_early, far_late, near_tiles, pair_acc, query_acc, expand_acc, reduce_acc, out_acc,
    grads_0, grads_1, stage_a, stage_b, relay_a, relay_b, land_a, land_b, acc, near_acc, chosen, cross_send,
    plane_a, plane_b, plane_land, line_send, line_land, axis_send, axis_land, axis_own,
    core_recv_0, core_sum_0, x_recv_0, x_sum_0, spot_recv_0, spot_sum_0, x_all_0,
    core_recv_1, core_sum_1, spot_recv_1, spot_sum_1, x_recv_1, x_sum_1, spot_all_1,
    send1, recv1, send2, recv2, plane_sems, line_sems, axis_sems, cross_sems, core_sems, x_sems, spot_sems,
):
    dom = lax.axis_index("dom")
    z, y, core, node = place()
    axis = (z, y)
    sources, relays, lands = (stage_a, stage_b), (relay_a, relay_b), (land_a, land_b)
    planes = (plane_a, plane_b)
    barrier = pltpu.get_barrier_semaphore()
    peers = [(dom_peer(dom, offset), node) for offset in OFFSETS]
    peers += [(dom, four(node + step)) for step in range(1, N_NODE)]
    for peer in peers:
        pl.semaphore_signal(barrier, inc=1, device_id=peer, device_id_type=MESH)

    scale = 1.0 / math.sqrt(D // HEADS)
    log2e = math.log2(math.e)
    expand_acc[...] = jnp.zeros(expand_acc.shape, F32)
    reduce_acc[...] = jnp.zeros(reduce_acc.shape, F32)
    out_acc[...] = jnp.zeros(out_acc.shape, F32)
    qs[...] = nn(feat_ref[...], wq_ref[...]).astype(BF16)
    lane_head = lax.broadcasted_iota(jnp.int32, (1, D), 1) // (D // HEADS)
    head_f32 = [(lane_head == h).astype(F32) for h in range(HEADS)]
    head_low = [mask.astype(BF16) for mask in head_f32]

    def forward_row(row, carry):
        start = pl.multiple_of(row * BLK, BLK)
        fs[row, 0:BLK] = feat_ref[pl.ds(start, BLK), :]
        for tile in range(NEAR - 1):
            block = local_ref[tile, row]
            top = (tile + 1) * BLK
            for index, part_ref in enumerate((part_0, part_1, part_a, part_b)):
                fs[row, top + index * SPAN : top + (index + 1) * SPAN] = part_ref[block]
        for tile in range(TILES - NEAR):
            slot = slot_ref[row, tile]
            asked = slot // 2
            dz = four(z + 4 - asked // 8)
            dy = four(y + 4 - four(asked // 2))
            dc = two(core + two(asked))
            for chunk in range(CHUNKS):
                top = (EARLY, LATE)[1 - chunk] + 2 * tile * SPAN
                fs[row, top : top + SPAN] = far_a[chunk, dz, dy, dc, two(slot)]
                fs[row, top + SPAN : top + 2 * SPAN] = far_b[chunk, dy, dz, dc, two(slot)]
        tile_rows = fs[row]
        keys = nn(tile_rows, wk_ref[...]).astype(BF16)
        ks[row] = keys
        values = nn(tile_rows, wv_ref[...]).astype(BF16)
        vs[row] = values
        query = qs[pl.ds(start, BLK), :]
        bias = bias_ref[pl.ds(start, BLK), :].astype(F32)
        total = jnp.zeros((BLK, D), F32)
        for pair in range(HEADS // 2):
            both = jnp.concatenate([query * head_low[2 * pair], query * head_low[2 * pair + 1]], 0)
            scores = nt(both, keys) * (scale * log2e)
            lows = []
            for half in range(2):
                mine = scores[half * BLK : (half + 1) * BLK] + bias
                top = jnp.max(mine, -1, keepdims=True)
                weight = jnp.exp2(mine - top)
                norm = 1.0 / jnp.sum(weight, -1, keepdims=True)
                lows.append((weight * norm).astype(BF16))
            probs_low = jnp.concatenate(lows, 0)
            ps[row, 2 * pair * BLK : (2 * pair + 2) * BLK, :] = probs_low
            got = nn(probs_low, values)
            total = total + got[:BLK] * head_f32[2 * pair] + got[BLK:] * head_f32[2 * pair + 1]
        mixed[pl.ds(start, BLK), :] = total
        return carry

    lax.fori_loop(0, ROWS, forward_row, 0)

    size = 256

    def feed(step, carry):
        start = pl.multiple_of(step * size, size)
        sel = pl.ds(start, size)
        mixed_low = mixed[sel, :].astype(BF16)
        gain_a = gain_a_ref[...]
        gain_f = gain_f_ref[...]
        residual = feat_ref[sel, :].astype(F32) + nn(mixed_low, wo_ref[...])
        center = residual - jnp.mean(residual, -1, keepdims=True)
        rstd_a = lax.rsqrt(jnp.mean(center * center, -1, keepdims=True) + EPSILON)
        hat_a = center * rstd_a
        first_low = (hat_a * gain_a).astype(BF16)
        pre = nn(first_low, we_ref[...])
        root = math.sqrt(2.0 / math.pi)
        square = pre * pre
        tanh = jnp.tanh(root * (pre + 0.044715 * (square * pre)))
        half = 0.5 * (1.0 + tanh)
        act_low = (pre * half).astype(BF16)
        slope = half + 0.5 * pre * (1.0 - tanh * tanh) * (root * (1.0 + 3.0 * 0.044715 * square))
        second = first_low.astype(F32) + nn(act_low, wr_ref[...])
        center = second - jnp.mean(second, -1, keepdims=True)
        rstd_f = lax.rsqrt(jnp.mean(center * center, -1, keepdims=True) + EPSILON)
        hat_f = center * rstd_f
        out_ref[sel, :] = (hat_f * gain_f).astype(BF16)
        d_hat = d_out_ref[sel, :].astype(F32) * gain_f
        d_second = rstd_f * (
            d_hat - jnp.mean(d_hat, -1, keepdims=True) - hat_f * jnp.mean(d_hat * hat_f, -1, keepdims=True)
        )
        d_second_low = d_second.astype(BF16)
        reduce_acc[...] += tn(d_second_low, act_low)
        d_pre_low = (nt(d_second_low, wr_ref[...]) * slope).astype(BF16)
        expand_acc[...] += tn(first_low, d_pre_low)
        d_first = d_second + nt(d_pre_low, we_ref[...])
        d_hat = d_first * gain_a
        d_resid = rstd_a * (
            d_hat - jnp.mean(d_hat, -1, keepdims=True) - hat_a * jnp.mean(d_hat * hat_a, -1, keepdims=True)
        )
        base_ref[sel, :] = d_resid
        d_resid_low = d_resid.astype(BF16)
        out_acc[...] += tn(mixed_low, d_resid_low)
        d_mixed[sel, :] = nt(d_resid_low, wo_ref[...]).astype(BF16)
        return carry

    lax.fori_loop(0, ROWS * BLK // size, feed, 0)

    def pack(accs, grads):
        spot = 0
        for total in accs:
            for top in range(0, total.shape[0], D):
                for left in range(0, total.shape[1], BLK):
                    grads[spot : spot + D, :] = total[top : top + D, left : left + BLK].astype(BF16)
                    spot += D

    def push(src, dst, sems, key, target):
        copy = pltpu.make_async_remote_copy(
            src_ref=src, dst_ref=dst, send_sem=sems.at[(0,) + key], recv_sem=sems.at[(1,) + key],
            device_id=target, device_id_type=MESH,
        )
        copy.start()
        return copy

    def finish(copies):
        for copy in copies:
            copy.wait()

    spot_here = z * 4 + y
    x_line = [four(node + step) for step in range(1, 4)]
    x_line = [(other, (dom, other)) for other in x_line]
    spots = [lax.rem(spot_here + step, 16) for step in range(1, 16)]
    spots = [(other, (other * 2 + core, node)) for other in spots]
    sibling = device(z, y, two(core + 1), node)

    def reduction(number, grads, total_ref, core_recv, core_sum, recvs, sums, near_all):
        lines = [(x_line, node, x_sems), (spots, spot_here, spot_sems)]
        if number == 1:
            lines.reverse()
        counts = [len(line[0]) + 1 for line in lines]
        core_rows = SUM_ROWS[number] // 2
        sizes = [core_rows // counts[0], core_rows // counts[0] // counts[1]]
        mine = rows_at(core, core_rows)

        def scatter(line, src, dst, count):
            members, own, sems = line
            return [
                push(src.at[rows_at(other, count)], dst.at[index], sems, (number, 0, index), target)
                for index, (other, target) in enumerate(members)
            ]

        def gather(line, src, dst, count):
            members, own, sems = line
            copies = [
                push(src, dst.at[rows_at(own, count)], sems, (number, 1, index), target)
                for index, (other, target) in enumerate(members)
            ]
            dst[rows_at(own, count), :] = src[...]
            return copies

        def add_up(line, src, recv, out, count):
            total = src[rows_at(line[1], count), :].astype(F32)
            for index in range(recv.shape[0]):
                total = total + recv[index].astype(F32)
            out[...] = total.astype(BF16)

        copy = push(grads.at[rows_at(two(core + 1), core_rows)], core_recv, core_sems, (number, 0), sibling)
        yield
        copy.wait()
        core_sum[...] = (grads[mine, :].astype(F32) + core_recv[...].astype(F32)).astype(BF16)
        copies = scatter(lines[0], core_sum, recvs[0], sizes[0])
        yield
        finish(copies)
        add_up(lines[0], core_sum, recvs[0], sums[0], sizes[0])
        copies = scatter(lines[1], sums[0], recvs[1], sizes[1])
        yield
        finish(copies)
        add_up(lines[1], sums[0], recvs[1], sums[1], sizes[1])
        copies = gather(lines[1], sums[1], near_all, sizes[1])
        yield
        finish(copies)
        my_part = total_ref.at[mine]
        copies = gather(lines[0], near_all, my_part, sizes[0])
        yield
        finish(copies)
        copy = push(my_part, my_part, core_sems, (number, 1), sibling)
        yield
        copy.wait()
        yield

    first_half = lax.broadcasted_iota(jnp.int32, (64, BLK), 0) < 32

    def block_diagonal(turned, pair):
        piece = turned[64 * pair : 64 * pair + 64]
        return jnp.concatenate(
            [jnp.where(first_half, piece, 0.0), jnp.where(first_half, 0.0, piece)], 1
        ).astype(BF16)

    def backward(row, begin, end):
        start = pl.multiple_of(row * BLK, BLK)
        keys = ks[row, begin:end]
        values = vs[row, begin:end]
        query = qs[pl.ds(start, BLK), :]
        grad = d_mixed[pl.ds(start, BLK), :]
        query_t = query.astype(F32).T
        grad_t = grad.astype(F32).T
        inner_full = grad.astype(F32) * mixed[pl.ds(start, BLK), :]
        query_part = jnp.zeros((BLK, D), F32)
        key_parts = []
        value_parts = []
        for pair in range(HEADS // 2):
            both = jnp.concatenate([grad * head_low[2 * pair], grad * head_low[2 * pair + 1]], 0)
            inner = jnp.concatenate(
                [
                    jnp.sum(inner_full * head_f32[2 * pair], -1, keepdims=True),
                    jnp.sum(inner_full * head_f32[2 * pair + 1], -1, keepdims=True),
                ],
                0,
            )
            probs_low = ps[row, 2 * pair * BLK : (2 * pair + 2) * BLK, begin:end]
            d_probs = nt(both, values)
            d_scores = (probs_low.astype(F32) * ((d_probs - inner) * scale)).astype(BF16)
            got = nn(d_scores, keys)
            query_part = query_part + got[:BLK] * head_f32[2 * pair] + got[BLK:] * head_f32[2 * pair + 1]
            key_parts.append(nn(block_diagonal(query_t, pair), d_scores).astype(BF16))
            value_parts.append(nn(block_diagonal(grad_t, pair), probs_low).astype(BF16))
        d_keys_t = jnp.concatenate(key_parts, 0)
        d_values_t = jnp.concatenate(value_parts, 0)
        return d_keys_t, d_values_t, nn(wk_ref[...], d_keys_t) + nn(wv_ref[...], d_values_t), query_part

    def keep_far(row, parts, begin, tiles):
        d_keys_t, d_values_t, d_rows_t = parts
        columns = slice(begin - EARLY, begin - EARLY + LATE - EARLY)
        far_keys_t[row, :, columns] = d_keys_t
        far_values_t[row, :, columns] = d_values_t
        for pair in range((TILES - NEAR) // 2):
            piece = d_rows_t[:, pair * BLK : (pair + 1) * BLK].T.astype(BF16)
            for side in range(2):
                tiles[row * (TILES - NEAR) + 2 * pair + side] = piece[side * 2 * SPAN : (side + 1) * 2 * SPAN]

    def backward_early(row, carry):
        *parts, query_part = backward(row, EARLY, LATE)
        keep_far(row, parts, EARLY, far_early)
        d_query[rows_at(row, BLK), :] = query_part
        return carry

    def backward_late(row, carry):
        *parts, query_part = backward(row, LATE, KEYS)
        keep_far(row, parts, LATE, far_late)
        d_query[rows_at(row, BLK), :] += query_part
        return carry

    def backward_near(row, carry):
        d_keys_t, d_values_t, d_rows_t, query_part = backward(row, 0, NEAR * BLK)
        near_keys_t[row] = d_keys_t
        near_values_t[row] = d_values_t
        d_query[rows_at(row, BLK), :] += query_part
        for tile in range(NEAR):
            piece = d_rows_t[:, tile * BLK : (tile + 1) * BLK].T
            near_tiles[row * NEAR + tile] = piece.astype(BF16)
        return carry

    def key_grads(row, carry):
        near_rows = fs[row, : NEAR * BLK]
        far_rows = fs[row, NEAR * BLK :]
        pair_acc[0:D, :] += nn(near_keys_t[row], near_rows) + nn(far_keys_t[row], far_rows)
        pair_acc[D : 2 * D, :] += nn(near_values_t[row], near_rows) + nn(far_values_t[row], far_rows)
        return carry

    def stage_early(half):
        def body(peer, carry):
            along, across = ((peer // 8, four(peer // 2)), (four(peer // 2), peer // 8))[half]
            for slot in range(2):
                tile = tile_ref[0, 2 * peer + slot]
                planes[half][across * 2 + two(peer), along, slot] = far_early[tile, half * SPAN : (half + 1) * SPAN]
            return carry

        lax.fori_loop(0, N_DOM, body, 0)

    def stage_late(peer, carry):
        turned = four(peer // 2) * 8 + (peer // 8) * 2 + two(peer)
        for slot in range(2):
            tile = tile_ref[0, 2 * peer + slot]
            stage_a[0, peer, slot] = far_late[tile, 0:SPAN]
            stage_b[0, turned, slot] = far_late[tile, SPAN : 2 * SPAN]
        return carry

    def send_early(half):
        copies = []
        for step in range(4):
            for flip in range(2):
                target = four(axis[1 - half] + step)
                side = two(core + flip)
                if step == 0 and flip == 0:
                    plane_land[half, 0, 0] = planes[half][target * 2 + side]
                    continue
                copies.append(
                    push(
                        planes[half].at[target * 2 + side], plane_land.at[half, step, flip],
                        plane_sems, (half, step, flip), (dom_at(half, axis[half], target, side), node),
                    )
                )
        return copies

    def sum_early(half):
        finish(early[half])
        for ahead in range(4):
            place_there = four(axis[half] + ahead)
            owner = dom_at(half, place_there, axis[1 - half], core)
            names = []
            for step in range(4):
                for flip in range(2):
                    asker = dom_at(half, axis[half], four(axis[1 - half] + 4 - step), two(core + flip))
                    names += [wanted_ref[asker, 0, 2 * owner + slot] for slot in range(2)]
            chosen[half, ahead] = selection(names)
            for top in range(0, SPAN, 16):
                arrived = plane_land[half, :, :, place_there, :, top : top + 16, :].reshape(256, D)
                total = nn(chosen[half, ahead], arrived).reshape(PART, 16, D)
                if ahead == 0:
                    total = total + near_acc[:, half * SPAN + top : half * SPAN + top + 16, :]
                line_send[half, ahead, :, top : top + 16, :] = total.astype(BF16)
        return [
            push(
                line_send.at[half, :, pl.ds(other * ROWS, ROWS)], line_land.at[half, index],
                line_sems, (half, index), target,
            )
            for index, (other, target) in enumerate(x_line)
        ]

    def turn_early(half):
        finish(lined[half])
        copies = []
        for ahead in range(4):
            total = line_send[half, ahead, pl.ds(node * ROWS, ROWS)].astype(F32)
            for index in range(3):
                total = total + line_land[half, index, ahead].astype(F32)
            if ahead == 0:
                axis_own[half] = total
            else:
                axis_send[half, ahead - 1] = total.astype(BF16)
                there = four(axis[half] + ahead)
                copies.append(
                    push(
                        axis_send.at[half, ahead - 1], axis_land.at[half, ahead - 1],
                        axis_sems, (half, ahead - 1), (dom_at(half, there, axis[1 - half], core), node),
                    )
                )
        return copies

    def end_early(half):
        finish(turned_copies[half])
        for row in range(ROWS):
            total = axis_own[half, row]
            for index in range(3):
                total = total + axis_land[half, index, row].astype(F32)
            top = row * BLK + (2 + half) * SPAN
            base_ref[top : top + SPAN, :] += total

    block_of = lax.broadcasted_iota(jnp.int32, (256, 256), 0) // 16
    same_row = lax.rem(lax.broadcasted_iota(jnp.int32, (256, 256), 0), 16) == lax.rem(
        lax.broadcasted_iota(jnp.int32, (256, 256), 1), 16
    )
    slot_of = lax.broadcasted_iota(jnp.int32, (1, 256), 1) // 16

    def selection(values):
        names = jnp.full((1, 256), -1, jnp.int32)
        for index, value in enumerate(values):
            names = jnp.where(slot_of == index, value, names)
        return jnp.logical_and(names == block_of, same_row).astype(F32).astype(BF16)

    def relay_on(arrivals):
        for half, step, copy in arrivals:
            copy.wait()
            second[half, step] = second_phase(0, half, step, sources, relays, lands, send2, recv2)
            lands[half][0, step, 0, 0] = relays[half][0, step - 1, (y, z)[half] * 2 + core]

    def combine(group):
        for half in range(2):
            finish(second[half, group])
            names = [
                wanted_ref[origin(half, group, step, flip), 0, 2 * dom + slot]
                for step in range(4)
                for flip in range(2)
                for slot in range(2)
            ]
            chosen[half, group] = selection(names)
            for top in range(0, SPAN, 16):
                rows = slice(half * SPAN + top, half * SPAN + top + 16)
                arrived = lands[half][0, group, :, :, :, top : top + 16, :].reshape(256, D)
                acc[:, rows, :] += nn(chosen[half, group], arrived).reshape(PART, 16, D)

    def cross():
        cross_send[...] = acc[...].astype(BF16)
        copies = []
        for step in range(1, N_NODE):
            other = four(node + step)
            copies.append(
                push(
                    cross_send.at[pl.ds(other * ROWS, ROWS)], cross_ref.at[step - 1],
                    cross_sems, (step - 1,), (dom, other),
                )
            )
        return copies

    pack((expand_acc, reduce_acc), grads_0)
    pl.semaphore_wait(barrier, len(peers))
    wide = reduction(
        0, grads_0, sum_0, core_recv_0, core_sum_0, (x_recv_0, spot_recv_0), (x_sum_0, spot_sum_0), x_all_0
    )
    next(wide)
    for tiles in (far_early, far_late):
        tiles[FAR] = jnp.zeros((2 * SPAN, D), BF16)
    lax.fori_loop(0, ROWS, backward_early, 0)
    next(wide)
    early = []
    for half in range(2):
        stage_early(half)
        early.append(send_early(half))
    lax.fori_loop(0, ROWS, backward_late, 0)
    lax.fori_loop(0, N_DOM, stage_late, 0)
    next(wide)
    first = [
        first_step(0, half, step, sources, relays, send1, recv1) for step in range(1, 4) for half in range(2)
    ]
    second = {}
    for half in range(2):
        second[half, 0] = second_phase(0, half, 0, sources, relays, lands, send2, recv2)
        lands[half][0, 0, 0, 0] = sources[half][0, (dom, y * 8 + z * 2 + core)[half]]

    near_tiles[ROWS * NEAR : PART] = jnp.zeros((PART - ROWS * NEAR, BLK, D), BF16)
    lax.fori_loop(0, ROWS, backward_near, 0)
    near_names = []
    for row in range(ROWS):
        near_names += [node * ROWS + row, local_ref[0, row], local_ref[1, row]]
    near_chosen = selection(near_names)
    for top in range(0, BLK, 16):
        total = nn(near_chosen, near_tiles[:, top : top + 16, :].reshape(256, D)).reshape(PART, 16, D)
        if top < 2 * SPAN:
            acc[:, top : top + 16, :] = total
        else:
            near_acc[:, top - 2 * SPAN : top - 2 * SPAN + 16, :] = total
    lined = [sum_early(half) for half in range(2)]
    next(wide)
    pair_acc[...] = jnp.zeros(pair_acc.shape, F32)
    lax.fori_loop(0, ROWS, key_grads, 0)
    d_query_low = d_query[...].astype(BF16)
    query_acc[...] = tn(feat_ref[...], d_query_low)
    pack((query_acc, pair_acc, out_acc), grads_1)
    narrow = reduction(
        1, grads_1, sum_1, core_recv_1, core_sum_1, (spot_recv_1, x_recv_1), (spot_sum_1, x_sum_1), spot_all_1
    )
    next(narrow)
    base_ref[...] += nt(d_query_low, wq_ref[...])
    next(narrow)
    relay_on(first[:3])
    next(narrow)
    next(wide)
    relay_on(first[3:])
    combine(0)
    combine(1)
    next(narrow)
    turned_copies = [turn_early(half) for half in range(2)]
    next(narrow)
    next(wide)
    combine(2)
    combine(3)
    crossing = cross()
    next(narrow)
    next(wide)
    for half in range(2):
        end_early(half)
    for row in range(ROWS):
        base_ref[row * BLK : row * BLK + 2 * SPAN, :] += acc[node * ROWS + row]
    next(narrow)
    finish(crossing)


def finish_kernel(
    factor, result_ref, base_ref, cross_ref, expand_ref, reduce_ref, rest_ref, out_ref, dx_ref, gq, gk, gv, go, ge, gr
):
    out_ref[...] = result_ref[...]
    for row in range(ROWS // 2):
        span = slice(row * BLK, row * BLK + 2 * SPAN)
        total = base_ref[span, :]
        for step in range(N_NODE - 1):
            total = total + cross_ref[step, row].astype(F32)
        dx_ref[span, :] = total.astype(BF16)
        span = slice(row * BLK + 2 * SPAN, (row + 1) * BLK)
        dx_ref[span, :] = base_ref[span, :].astype(BF16)
    for half in range(2):
        span = slice(half * BLK, (half + 1) * BLK)
        gq[:, span] = rest_ref[half].astype(F32) * factor
        gk[span, :] = (rest_ref[2 + half].astype(F32) * factor).T
        gv[span, :] = (rest_ref[4 + half].astype(F32) * factor).T
        go[:, span] = rest_ref[6 + half].astype(F32) * factor
    for part in range(4):
        span = slice(part * BLK, (part + 1) * BLK)
        ge[:, span] = expand_ref[part].astype(F32) * factor
        gr[span, :] = (reduce_ref[part].astype(F32) * factor).T


def vmem(shape, dtype):
    return pltpu.VMEM(shape, dtype)


IN_VMEM = pl.BlockSpec(memory_space=pltpu.VMEM)
IN_SMEM = pl.BlockSpec(memory_space=pltpu.SMEM)
ANYWHERE = pl.BlockSpec(memory_space=pl.ANY)


def on_device(
    features, w_query, w_key, w_value, w_out, w_expand, w_reduce, gain_attn, gain_ffn,
    tile_mask, local_block, remote_slot, remote_block, d_out,
):
    rows = features.shape[0]
    dma = pltpu.SemaphoreType.DMA
    peers = len(OFFSETS)
    land = (CHUNKS, 4, 4, 2, 2, SPAN, D)
    staged = (CHUNKS, N_DOM, 2, SPAN, D)
    relay = (CHUNKS, 3, 8, 2, SPAN, D)
    phase_sems = [dma((CHUNKS, 2, 3)), dma((CHUNKS, 2, 3)), dma((CHUNKS, 2, 4, 4, 2)), dma((CHUNKS, 2, 4, 4, 2))]
    part_0, part_1, part_a, part_b, land_a, land_b, wanted, bias, tile_of = pl.pallas_call(
        exchange_kernel,
        out_shape=(
            jax.ShapeDtypeStruct((PART, SPAN, D), BF16),
            jax.ShapeDtypeStruct((PART, SPAN, D), BF16),
            jax.ShapeDtypeStruct((PART, SPAN, D), BF16),
            jax.ShapeDtypeStruct((PART, SPAN, D), BF16),
            jax.ShapeDtypeStruct(land, BF16),
            jax.ShapeDtypeStruct(land, BF16),
            jax.ShapeDtypeStruct((N_DOM, 1, BLK), jnp.int32),
            jax.ShapeDtypeStruct((rows, KEYS), BF16),
            jax.ShapeDtypeStruct((1, 2 * N_DOM), jnp.int32),
        ),
        in_specs=[IN_VMEM, IN_VMEM, IN_SMEM, IN_VMEM],
        out_specs=(IN_VMEM,) * 4 + (ANYWHERE, ANYWHERE, IN_VMEM, IN_VMEM, IN_SMEM),
        scratch_shapes=[
            vmem((1, BLK), jnp.int32), vmem(staged, BF16), vmem(staged, BF16),
            vmem(relay, BF16), vmem(relay, BF16), pltpu.SMEM((N_DOM, 1, BLK), jnp.int32),
        ]
        + [vmem((PART, SPAN, D), BF16)] * 6
        + [dma((2, N_NODE - 1)), dma((2, N_NODE - 1)), dma((peers,)), dma((peers,))]
        + phase_sems
        + [dma((2, 3)), dma((2, 3)), dma((2, 4, 3)), dma((2, 4, 3)), dma((CHUNKS, 2, 4)), dma],
        compiler_params=pltpu.CompilerParams(
            collective_id=1, has_side_effects=True, vmem_limit_bytes=VMEM_LIMIT
        ),
        name="exchange",
    )(features.reshape(ROWS, BLK, D), remote_block.reshape(1, 2 * N_DOM), remote_slot, jnp.transpose(tile_mask, (1, 0, 2)))

    sum_scratch = []
    for total, lines in zip(SUM_ROWS, ((4, 16), (16, 4))):
        half = total // 2
        sum_scratch += [vmem((half, BLK), BF16), vmem((half, BLK), BF16)]
        for count in lines:
            half = half // count
            sum_scratch += [vmem((count - 1, half, BLK), BF16), vmem((half, BLK), BF16)]
        sum_scratch.append(vmem((total // 2 // lines[0], BLK), BF16))
    result, base, cross, sum_0, sum_1 = pl.pallas_call(
        layer_kernel,
        out_shape=(
            jax.ShapeDtypeStruct((rows, D), BF16),
            jax.ShapeDtypeStruct((rows, D), F32),
            jax.ShapeDtypeStruct((N_NODE - 1, ROWS, 2 * SPAN, D), BF16),
            jax.ShapeDtypeStruct((SUM_ROWS[0], BLK), BF16),
            jax.ShapeDtypeStruct((SUM_ROWS[1], BLK), BF16),
        ),
        in_specs=[IN_SMEM] * 4 + [IN_VMEM] * 17,
        out_specs=(IN_VMEM,) * 5,
        scratch_shapes=[
            vmem((ROWS, KEYS, D), BF16), vmem((ROWS, KEYS, D), BF16), vmem((ROWS, KEYS, D), BF16),
            vmem((rows, D), BF16), vmem((ROWS, HEADS * BLK, KEYS), BF16), vmem((rows, D), F32),
            vmem((rows, D), BF16), vmem((rows, D), F32),
            vmem((ROWS, D, KEYS - NEAR * BLK), BF16), vmem((ROWS, D, KEYS - NEAR * BLK), BF16),
            vmem((ROWS, D, NEAR * BLK), BF16), vmem((ROWS, D, NEAR * BLK), BF16),
            vmem((FAR + 1, 2 * SPAN, D), BF16), vmem((FAR + 1, 2 * SPAN, D), BF16), vmem((PART, BLK, D), BF16),
            vmem((2 * D, D), F32), vmem((D, D), F32), vmem((D, 4 * D), F32), vmem((D, 4 * D), F32), vmem((D, D), F32),
            vmem((SUM_ROWS[0], BLK), BF16), vmem((SUM_ROWS[1], BLK), BF16),
            vmem((1,) + staged[1:], BF16), vmem((1,) + staged[1:], BF16),
            vmem((1,) + relay[1:], BF16), vmem((1,) + relay[1:], BF16),
            vmem((1,) + land[1:], BF16), vmem((1,) + land[1:], BF16),
            vmem((PART, 2 * SPAN, D), F32), vmem((PART, 2 * SPAN, D), F32),
            vmem((2, 4, 256, 256), BF16), vmem((PART, 2 * SPAN, D), BF16),
            vmem((8, 4, 2, SPAN, D), BF16), vmem((8, 4, 2, SPAN, D), BF16), vmem((2, 4, 2, 4, 2, SPAN, D), BF16),
            vmem((2, 4, PART, SPAN, D), BF16), vmem((2, 3, 4, ROWS, SPAN, D), BF16),
            vmem((2, 3, ROWS, SPAN, D), BF16), vmem((2, 3, ROWS, SPAN, D), BF16), vmem((2, ROWS, SPAN, D), F32),
        ]
        + sum_scratch
        + [dma((1, 2, 3)), dma((1, 2, 3)), dma((1, 2, 4, 4, 2)), dma((1, 2, 4, 4, 2))]
        + [dma((2, 2, 4, 2)), dma((2, 2, 3)), dma((2, 2, 3)), dma((2, 3)), dma((2, 2, 2)), dma((2, 2, 2, 3)), dma((2, 2, 2, 15))],
        compiler_params=pltpu.CompilerParams(
            collective_id=2, has_side_effects=True, vmem_limit_bytes=VMEM_LIMIT
        ),
        name="layer",
    )(
        local_block.T, remote_slot, tile_of, wanted, features, part_0, part_1, part_a, part_b, land_a, land_b, bias, d_out,
        w_query, w_key, w_value, w_out, w_expand, w_reduce, gain_attn.reshape(1, D), gain_ffn.reshape(1, D),
    )

    factor = 1.0 / math.sqrt(rows * N_DOM * N_NODE)
    pieces = sum_0.reshape(16, D, BLK)
    return pl.pallas_call(
        functools.partial(finish_kernel, factor),
        out_shape=(
            jax.ShapeDtypeStruct((rows, D), BF16),
            jax.ShapeDtypeStruct((rows, D), BF16),
            jax.ShapeDtypeStruct((D, D), F32),
            jax.ShapeDtypeStruct((D, D), F32),
            jax.ShapeDtypeStruct((D, D), F32),
            jax.ShapeDtypeStruct((D, D), F32),
            jax.ShapeDtypeStruct((D, 4 * D), F32),
            jax.ShapeDtypeStruct((4 * D, D), F32),
        ),
        grid=(2,),
        in_specs=[
            pl.BlockSpec((rows // 2, D), lambda i: (i, 0)),
            pl.BlockSpec((rows // 2, D), lambda i: (i, 0)),
            pl.BlockSpec((N_NODE - 1, ROWS // 2, 2 * SPAN, D), lambda i: (0, i, 0, 0)),
            pl.BlockSpec((4, D, BLK), lambda i: (i, 0, 0)),
            pl.BlockSpec((4, D, BLK), lambda i: (2 + i, 0, 0)),
            pl.BlockSpec((8, BLK, BLK), lambda i: (0, i, 0)),
        ],
        out_specs=(
            pl.BlockSpec((rows // 2, D), lambda i: (i, 0)),
            pl.BlockSpec((rows // 2, D), lambda i: (i, 0)),
            pl.BlockSpec((BLK, D), lambda i: (i, 0)),
            pl.BlockSpec((D, BLK), lambda i: (0, i)),
            pl.BlockSpec((D, BLK), lambda i: (0, i)),
            pl.BlockSpec((BLK, D), lambda i: (i, 0)),
            pl.BlockSpec((D, 2 * D), lambda i: (0, i)),
            pl.BlockSpec((2 * D, D), lambda i: (i, 0)),
        ),
        compiler_params=pltpu.CompilerParams(vmem_limit_bytes=VMEM_LIMIT),
        name="finish",
    )(result, base, cross, pieces, pieces, sum_1.reshape(8, D, BLK))


def solution(mesh):
    split = P(("dom", "node"), None)
    placed = (
        (split,) + (P(),) * 8 + (P(("dom", "node"), None, None), split, split, P("dom", "node", None), split)
    )
    return jax.shard_map(
        on_device, mesh=mesh, in_specs=placed, out_specs=(split, split) + (P(),) * 6, check_vma=False
    )
```

```python
import functools
import math

import jax
import jax.numpy as jnp
from jax import lax
from jax.experimental import pallas as pl
from jax.experimental.pallas import tpu as pltpu
from jax.sharding import PartitionSpec as P

HEADS = 8
EPSILON = 1e-05
MESH = pl.DeviceIdType.MESH
F32 = jnp.float32
BF16 = jnp.bfloat16
NEG = -1e30
VMEM_LIMIT = 62 << 20

D = 256
BLK = 128
TILES = 7
NEAR = 3
ROWS = 4
PART = 16
KEYS = TILES * BLK
FAR = ROWS * (TILES - NEAR)
EARLY = NEAR * BLK
LATE = EARLY + (KEYS - EARLY) // 2
N_DOM = 32
N_NODE = 4
CHUNKS = 2
SPAN = BLK // (2 * CHUNKS)

_GROUPS = [
    [(2, 2)],
    [(2, 1), (2, 3)],
    [(1, 2), (3, 2)],
    [(1, 1), (3, 3)],
    [(1, 3), (3, 1)],
    [(2, 0), (0, 2)],
    [(1, 0), (3, 0), (0, 1), (0, 3)],
]
OFFSETS = [(a, b, c) for group in _GROUPS for c in range(2) for a, b in group] + [(0, 0, 1)]


def dom_peer(dom, offset, sign=1):
    core = lax.rem(dom, 2)
    y = lax.rem(dom // 2, 4)
    z = dom // 8
    dz, dy, dc = offset
    return (
        lax.rem(z + (dz if sign > 0 else 4 - dz), 4) * 8
        + lax.rem(y + (dy if sign > 0 else 4 - dy), 4) * 2
        + lax.rem(core + dc, 2)
    )


def nt(a, b):
    return lax.dot_general(a, b, (((1,), (1,)), ((), ())), preferred_element_type=F32)


def tn(a, b):
    return lax.dot_general(a, b, (((0,), (0,)), ((), ())), preferred_element_type=F32)


def nn(a, b):
    return jnp.dot(a, b, preferred_element_type=F32)


def place():
    dom = lax.axis_index("dom")
    return dom // 8, lax.rem(dom // 2, 4), lax.rem(dom, 2), lax.axis_index("node")


def device(z, y, core, node):
    return (z * 8 + y * 2 + core, node)


def four(value):
    return lax.rem(value, 4)


def two(value):
    return lax.rem(value, 2)


def first_step(chunk, half, step, sources, relays, sends, recvs):
    z, y, core, node = place()
    target = four((z, y)[half] + step)
    copy = pltpu.make_async_remote_copy(
        src_ref=sources[half].at[chunk, pl.ds(target * 8, 8)],
        dst_ref=relays[half].at[chunk, step - 1],
        send_sem=sends.at[chunk, half, step - 1], recv_sem=recvs.at[chunk, half, step - 1],
        device_id=(device(target, y, core, node), device(z, target, core, node))[half],
        device_id_type=MESH,
    )
    copy.start()
    return half, step, copy


def second_phase(chunk, half, group, sources, relays, lands, sends, recvs):
    z, y, core, node = place()
    copies = []
    for step in range(4):
        for flip in range(2):
            if step == 0 and flip == 0:
                continue
            target = four((y, z)[half] + step)
            side = two(core + flip)
            if group == 0:
                source = sources[half].at[chunk, (z, y)[half] * 8 + target * 2 + side]
            else:
                source = relays[half].at[chunk, group - 1, target * 2 + side]
            copy = pltpu.make_async_remote_copy(
                src_ref=source, dst_ref=lands[half].at[chunk, group, step, flip],
                send_sem=sends.at[chunk, half, group, step, flip],
                recv_sem=recvs.at[chunk, half, group, step, flip],
                device_id=(device(z, target, side, node), device(target, y, side, node))[half],
                device_id_type=MESH,
            )
            copy.start()
            copies.append(copy)
    return copies


def origin(half, group, step, flip):
    z, y, core, node = place()
    far, near = 4 - group, 4 - step
    if half == 0:
        return four(z + far) * 8 + four(y + near) * 2 + two(core + flip)
    return four(z + near) * 8 + four(y + far) * 2 + two(core + flip)


def dom_at(half, along, across, side):
    first, other = ((along, across), (across, along))[half]
    return first * 8 + other * 2 + side


def exchange_kernel(
    feat_ref, table_ref, slot_ref, mask_ref,
    part_0, part_1, part_a, part_b, land_a, land_b, wanted_ref, bias_ref, tile_ref,
    row_ref, stage_a, stage_b, relay_a, relay_b, ids_smem, held_a1, held_a2, held_a3, held_b1, held_b2, held_b3,
    near_send, near_recv, id_send, id_recv, send1, recv1, send2, recv2, line_send, line_recv, x_send, x_recv,
    own_sem, local_sem,
):
    dom = lax.axis_index("dom")
    z, y, core, node = place()
    axis = (z, y)
    stages, relays, lands = (stage_a, stage_b), (relay_a, relay_b), (land_a, land_b)
    held = ((part_a, held_a1, held_a2, held_a3), (part_b, held_b1, held_b2, held_b3))
    barrier = pltpu.get_barrier_semaphore()
    for offset in OFFSETS:
        pl.semaphore_signal(barrier, inc=1, device_id=(dom_peer(dom, offset), node), device_id_type=MESH)
    x_line = [(dom, four(node + step)) for step in range(1, N_NODE)]
    for target in x_line:
        pl.semaphore_signal(barrier, inc=1, device_id=target, device_id_type=MESH)
    row_ref[:, 0 : 2 * N_DOM] = table_ref[...]
    mine = pl.ds(node * ROWS, ROWS)
    late = (part_0, part_1)
    for half in range(2):
        late[half][mine] = feat_ref[:, half * SPAN : (half + 1) * SPAN]
        held[half][0][mine] = feat_ref[:, (2 + half) * SPAN : (3 + half) * SPAN]
    pl.semaphore_wait(barrier, len(OFFSETS) + N_NODE - 1)

    def push(src, dst, send, recv, target):
        copy = pltpu.make_async_remote_copy(
            src_ref=src, dst_ref=dst, send_sem=send, recv_sem=recv, device_id=target, device_id_type=MESH
        )
        copy.start()
        return copy

    id_copies = [
        push(row_ref, wanted_ref.at[dom], id_send.at[index], id_recv.at[index], (dom_peer(dom, offset), node))
        for index, offset in enumerate(OFFSETS)
    ]
    near_copies = [
        [
            push(
                feat_ref.at[:, pl.ds(half * SPAN, SPAN)], late[half].at[mine],
                near_send.at[half, index], near_recv.at[half, index], target,
            )
            for index, target in enumerate(x_line)
        ]
        for half in range(2)
    ]
    line_copies = []
    for step in range(1, 4):
        for half in range(2):
            target = (device(four(z + step), y, core, node), device(z, four(y + step), core, node))[half]
            copy = push(
                feat_ref.at[:, pl.ds((2 + half) * SPAN, SPAN)], held[half][step].at[mine],
                line_send.at[half, step - 1], line_recv.at[half, step - 1], target,
            )
            line_copies.append((half, step, copy))
    x_copies = {}

    def spread(half, group):
        if group == 0:
            source = feat_ref.at[:, pl.ds((2 + half) * SPAN, SPAN)]
        else:
            source = held[half][group].at[mine]
        x_copies[half, group] = [
            push(
                source, held[half][group].at[mine],
                x_send.at[half, group, index], x_recv.at[half, group, index], target,
            )
            for index, target in enumerate(x_line)
        ]

    for half in range(2):
        spread(half, 0)
    wanted_ref[dom] = row_ref[...]
    for copy in id_copies:
        copy.wait()
    to_smem = pltpu.make_async_copy(wanted_ref, ids_smem, local_sem)
    to_smem.start()
    to_smem.wait()

    def stage(half, there):
        def body(index, carry):
            peer = dom_at(half, there, index // 2, two(index))
            for slot in range(2):
                stages[half][0, there * 8 + index, slot] = late[half][ids_smem[peer, 0, 2 * dom + slot]]
            return carry

        lax.fori_loop(0, 8, body, 0)

    def pick(half, group):
        owner = dom_at(half, four(axis[half] + 4 - group), axis[1 - half], core)

        def body(index, carry):
            asker = dom_at(half, axis[half], index // 2, two(index))
            for slot in range(2):
                block = ids_smem[asker, 0, 2 * owner + slot]
                rows = held[half][group][block]
                if group == 0:
                    stages[half][1, axis[half] * 8 + index, slot] = rows
                else:
                    relays[half][1, group - 1, index, slot] = rows
            return carry

        lax.fori_loop(0, 8, body, 0)

    second = []
    kept = []

    def deliver(chunk, half, group):
        second.extend(second_phase(chunk, half, group, stages, relays, lands, send2, recv2))
        if group == 0:
            source = stages[half].at[chunk, axis[half] * 8 + axis[1 - half] * 2 + core]
        else:
            source = relays[half].at[chunk, group - 1, axis[1 - half] * 2 + core]
        copy = pltpu.make_async_copy(
            source, lands[half].at[chunk, group, 0, 0], own_sem.at[chunk, half, group]
        )
        copy.start()
        kept.append(copy)

    first = []
    for half in range(2):
        for copy in near_copies[half]:
            copy.wait()
        for step in range(1, 4):
            stage(half, four(axis[half] + step))
            first.append(first_step(0, half, step, stages, relays, send1, recv1))
    for half in range(2):
        stage(half, axis[half])
        deliver(0, half, 0)
    for half, step, copy in line_copies:
        copy.wait()
        spread(half, step)
    for half in range(2):
        for copy in x_copies[half, 0]:
            copy.wait()
        pick(half, 0)
        deliver(1, half, 0)

    width = KEYS - NEAR * BLK
    wanted_key = lax.broadcasted_iota(jnp.int32, (width, width), 1)
    in_late = wanted_key // (width // 2)
    within = lax.rem(wanted_key, width // 2)
    old_key = within // (2 * SPAN) * BLK + lax.rem(within, 2 * SPAN) + (1 - in_late) * 2 * SPAN
    reorder = (lax.broadcasted_iota(jnp.int32, (width, width), 0) == old_key).astype(F32).astype(BF16)

    def to_bias(row, carry):
        start = pl.multiple_of(row * BLK, BLK)
        diagonal = lax.broadcasted_iota(jnp.int32, (BLK, BLK), 0) == lax.broadcasted_iota(
            jnp.int32, (BLK, BLK), 1
        )
        far = []
        for tile in range(TILES):
            allowed = mask_ref[tile, pl.ds(start, BLK), :] > 0
            if tile == 0:
                allowed = jnp.logical_or(allowed, diagonal)
            bias = jnp.where(allowed, 0.0, NEG).astype(BF16)
            if tile < NEAR:
                bias_ref[pl.ds(start, BLK), tile * BLK : (tile + 1) * BLK] = bias
            else:
                far.append(bias)
        bias_ref[pl.ds(start, BLK), NEAR * BLK :] = nn(jnp.concatenate(far, 1), reorder).astype(BF16)
        return carry

    lax.fori_loop(0, ROWS, to_bias, 0)

    def tile_of(slot, carry):
        found = jnp.int32(FAR)
        for row in range(ROWS):
            for tile in range(TILES - NEAR):
                found = jnp.where(slot_ref[row, tile] == slot, row * (TILES - NEAR) + tile, found)
        tile_ref[0, slot] = found
        return carry

    lax.fori_loop(0, 2 * N_DOM, tile_of, 0)
    for half, step, copy in (first[0], first[3], first[1], first[4], first[2], first[5]):
        copy.wait()
        deliver(0, half, step)
    for group in range(1, 4):
        for half in range(2):
            for copy in x_copies[half, group]:
                copy.wait()
            pick(half, group)
            deliver(1, half, group)
    for copy in kept:
        copy.wait()
    for copy in second:
        copy.wait()


SUM_ROWS = (4096, 2048)


def rows_at(index, size):
    return pl.ds(pl.multiple_of(index * size, size), size)


def layer_kernel(
    local_ref, slot_ref, tile_ref, wanted_ref, feat_ref, part_0, part_1, part_a, part_b, far_a, far_b, bias_ref, d_out_ref,
    wq_ref, wk_ref, wv_ref, wo_ref, we_ref, wr_ref, gain_a_ref, gain_f_ref,
    out_ref, base_ref, cross_ref, sum_0, sum_1,
    fs, ks, vs, qs, ps, mixed, d_mixed, d_query, far_keys_t, far_values_t, near_keys_t, near_values_t,
    far_early, far_late, near_tiles, pair_acc, query_acc, expand_acc, reduce_acc, out_acc,
    grads_0, grads_1, stage_a, stage_b, relay_a, relay_b, land_a, land_b, acc, near_acc, chosen, cross_send,
    plane_a, plane_b, plane_land, line_send, line_land, axis_send, axis_land, axis_own,
    core_recv_0, core_sum_0, x_recv_0, x_sum_0, spot_recv_0, spot_sum_0, x_all_0,
    core_recv_1, core_sum_1, spot_recv_1, spot_sum_1, x_recv_1, x_sum_1, spot_all_1,
    send1, recv1, send2, recv2, plane_sems, line_sems, axis_sems, cross_sems, core_sems, x_sems, spot_sems,
):
    dom = lax.axis_index("dom")
    z, y, core, node = place()
    axis = (z, y)
    sources, relays, lands = (stage_a, stage_b), (relay_a, relay_b), (land_a, land_b)
    planes = (plane_a, plane_b)
    barrier = pltpu.get_barrier_semaphore()
    peers = [(dom_peer(dom, offset), node) for offset in OFFSETS]
    peers += [(dom, four(node + step)) for step in range(1, N_NODE)]
    for peer in peers:
        pl.semaphore_signal(barrier, inc=1, device_id=peer, device_id_type=MESH)

    scale = 1.0 / math.sqrt(D // HEADS)
    log2e = math.log2(math.e)
    expand_acc[...] = jnp.zeros(expand_acc.shape, F32)
    reduce_acc[...] = jnp.zeros(reduce_acc.shape, F32)
    out_acc[...] = jnp.zeros(out_acc.shape, F32)
    qs[...] = nn(feat_ref[...], wq_ref[...]).astype(BF16)
    lane_head = lax.broadcasted_iota(jnp.int32, (1, D), 1) // (D // HEADS)
    head_f32 = [(lane_head == h).astype(F32) for h in range(HEADS)]
    head_low = [mask.astype(BF16) for mask in head_f32]

    def forward_row(row, carry):
        start = pl.multiple_of(row * BLK, BLK)
        fs[row, 0:BLK] = feat_ref[pl.ds(start, BLK), :]
        for tile in range(NEAR - 1):
            block = local_ref[tile, row]
            top = (tile + 1) * BLK
            for index, part_ref in enumerate((part_0, part_1, part_a, part_b)):
                fs[row, top + index * SPAN : top + (index + 1) * SPAN] = part_ref[block]
        for tile in range(TILES - NEAR):
            slot = slot_ref[row, tile]
            asked = slot // 2
            dz = four(z + 4 - asked // 8)
            dy = four(y + 4 - four(asked // 2))
            dc = two(core + two(asked))
            for chunk in range(CHUNKS):
                top = (EARLY, LATE)[1 - chunk] + 2 * tile * SPAN
                fs[row, top : top + SPAN] = far_a[chunk, dz, dy, dc, two(slot)]
                fs[row, top + SPAN : top + 2 * SPAN] = far_b[chunk, dy, dz, dc, two(slot)]
        tile_rows = fs[row]
        keys = nn(tile_rows, wk_ref[...]).astype(BF16)
        ks[row] = keys
        values = nn(tile_rows, wv_ref[...]).astype(BF16)
        vs[row] = values
        query = qs[pl.ds(start, BLK), :]
        bias = bias_ref[pl.ds(start, BLK), :].astype(F32)
        total = jnp.zeros((BLK, D), F32)
        for pair in range(HEADS // 2):
            both = jnp.concatenate([query * head_low[2 * pair], query * head_low[2 * pair + 1]], 0)
            scores = nt(both, keys) * (scale * log2e)
            lows = []
            for half in range(2):
                mine = scores[half * BLK : (half + 1) * BLK] + bias
                top = jnp.max(mine, -1, keepdims=True)
                weight = jnp.exp2(mine - top)
                norm = 1.0 / jnp.sum(weight, -1, keepdims=True)
                lows.append((weight * norm).astype(BF16))
            probs_low = jnp.concatenate(lows, 0)
            ps[row, 2 * pair * BLK : (2 * pair + 2) * BLK, :] = probs_low
            got = nn(probs_low, values)
            total = total + got[:BLK] * head_f32[2 * pair] + got[BLK:] * head_f32[2 * pair + 1]
        mixed[pl.ds(start, BLK), :] = total
        return carry

    lax.fori_loop(0, ROWS, forward_row, 0)

    size = 256

    def feed(step, carry):
        start = pl.multiple_of(step * size, size)
        sel = pl.ds(start, size)
        mixed_low = mixed[sel, :].astype(BF16)
        gain_a = gain_a_ref[...]
        gain_f = gain_f_ref[...]
        residual = feat_ref[sel, :].astype(F32) + nn(mixed_low, wo_ref[...])
        center = residual - jnp.mean(residual, -1, keepdims=True)
        rstd_a = lax.rsqrt(jnp.mean(center * center, -1, keepdims=True) + EPSILON)
        hat_a = center * rstd_a
        first_low = (hat_a * gain_a).astype(BF16)
        pre = nn(first_low, we_ref[...])
        root = math.sqrt(2.0 / math.pi)
        square = pre * pre
        tanh = jnp.tanh(root * (pre + 0.044715 * (square * pre)))
        half = 0.5 * (1.0 + tanh)
        act_low = (pre * half).astype(BF16)
        slope = half + 0.5 * pre * (1.0 - tanh * tanh) * (root * (1.0 + 3.0 * 0.044715 * square))
        second = first_low.astype(F32) + nn(act_low, wr_ref[...])
        center = second - jnp.mean(second, -1, keepdims=True)
        rstd_f = lax.rsqrt(jnp.mean(center * center, -1, keepdims=True) + EPSILON)
        hat_f = center * rstd_f
        out_ref[sel, :] = (hat_f * gain_f).astype(BF16)
        d_hat = d_out_ref[sel, :].astype(F32) * gain_f
        d_second = rstd_f * (
            d_hat - jnp.mean(d_hat, -1, keepdims=True) - hat_f * jnp.mean(d_hat * hat_f, -1, keepdims=True)
        )
        d_second_low = d_second.astype(BF16)
        reduce_acc[...] += tn(d_second_low, act_low)
        d_pre_low = (nt(d_second_low, wr_ref[...]) * slope).astype(BF16)
        expand_acc[...] += tn(first_low, d_pre_low)
        d_first = d_second + nt(d_pre_low, we_ref[...])
        d_hat = d_first * gain_a
        d_resid = rstd_a * (
            d_hat - jnp.mean(d_hat, -1, keepdims=True) - hat_a * jnp.mean(d_hat * hat_a, -1, keepdims=True)
        )
        base_ref[sel, :] = d_resid
        d_resid_low = d_resid.astype(BF16)
        out_acc[...] += tn(mixed_low, d_resid_low)
        d_mixed[sel, :] = nt(d_resid_low, wo_ref[...]).astype(BF16)
        return carry

    lax.fori_loop(0, ROWS * BLK // size, feed, 0)

    def pack(accs, grads):
        spot = 0
        for total in accs:
            for top in range(0, total.shape[0], D):
                for left in range(0, total.shape[1], BLK):
                    grads[spot : spot + D, :] = total[top : top + D, left : left + BLK].astype(BF16)
                    spot += D

    def push(src, dst, sems, key, target):
        copy = pltpu.make_async_remote_copy(
            src_ref=src, dst_ref=dst, send_sem=sems.at[(0,) + key], recv_sem=sems.at[(1,) + key],
            device_id=target, device_id_type=MESH,
        )
        copy.start()
        return copy

    def finish(copies):
        for copy in copies:
            copy.wait()

    spot_here = z * 4 + y
    x_line = [four(node + step) for step in range(1, 4)]
    x_line = [(other, (dom, other)) for other in x_line]
    spots = [lax.rem(spot_here + step, 16) for step in range(1, 16)]
    spots = [(other, (other * 2 + core, node)) for other in spots]
    sibling = device(z, y, two(core + 1), node)

    def reduction(number, grads, total_ref, core_recv, core_sum, recvs, sums, near_all):
        lines = [(x_line, node, x_sems), (spots, spot_here, spot_sems)]
        if number == 1:
            lines.reverse()
        counts = [len(line[0]) + 1 for line in lines]
        core_rows = SUM_ROWS[number] // 2
        sizes = [core_rows // counts[0], core_rows // counts[0] // counts[1]]
        mine = rows_at(core, core_rows)

        def scatter(line, src, dst, count):
            members, own, sems = line
            return [
                push(src.at[rows_at(other, count)], dst.at[index], sems, (number, 0, index), target)
                for index, (other, target) in enumerate(members)
            ]

        def gather(line, src, dst, count):
            members, own, sems = line
            copies = [
                push(src, dst.at[rows_at(own, count)], sems, (number, 1, index), target)
                for index, (other, target) in enumerate(members)
            ]
            dst[rows_at(own, count), :] = src[...]
            return copies

        def add_up(line, src, recv, out, count):
            total = src[rows_at(line[1], count), :].astype(F32)
            for index in range(recv.shape[0]):
                total = total + recv[index].astype(F32)
            out[...] = total.astype(BF16)

        copy = push(grads.at[rows_at(two(core + 1), core_rows)], core_recv, core_sems, (number, 0), sibling)
        yield
        copy.wait()
        core_sum[...] = (grads[mine, :].astype(F32) + core_recv[...].astype(F32)).astype(BF16)
        copies = scatter(lines[0], core_sum, recvs[0], sizes[0])
        yield
        finish(copies)
        add_up(lines[0], core_sum, recvs[0], sums[0], sizes[0])
        copies = scatter(lines[1], sums[0], recvs[1], sizes[1])
        yield
        finish(copies)
        add_up(lines[1], sums[0], recvs[1], sums[1], sizes[1])
        copies = gather(lines[1], sums[1], near_all, sizes[1])
        yield
        finish(copies)
        my_part = total_ref.at[mine]
        copies = gather(lines[0], near_all, my_part, sizes[0])
        yield
        finish(copies)
        copy = push(my_part, my_part, core_sems, (number, 1), sibling)
        yield
        copy.wait()
        yield

    first_half = lax.broadcasted_iota(jnp.int32, (64, BLK), 0) < 32

    def block_diagonal(turned, pair):
        piece = turned[64 * pair : 64 * pair + 64]
        return jnp.concatenate(
            [jnp.where(first_half, piece, 0.0), jnp.where(first_half, 0.0, piece)], 1
        ).astype(BF16)

    def backward(row, begin, end):
        start = pl.multiple_of(row * BLK, BLK)
        keys = ks[row, begin:end]
        values = vs[row, begin:end]
        query = qs[pl.ds(start, BLK), :]
        grad = d_mixed[pl.ds(start, BLK), :]
        query_t = query.astype(F32).T
        grad_t = grad.astype(F32).T
        inner_full = grad.astype(F32) * mixed[pl.ds(start, BLK), :]
        query_part = jnp.zeros((BLK, D), F32)
        key_parts = []
        value_parts = []
        for pair in range(HEADS // 2):
            both = jnp.concatenate([grad * head_low[2 * pair], grad * head_low[2 * pair + 1]], 0)
            inner = jnp.concatenate(
                [
                    jnp.sum(inner_full * head_f32[2 * pair], -1, keepdims=True),
                    jnp.sum(inner_full * head_f32[2 * pair + 1], -1, keepdims=True),
                ],
                0,
            )
            probs_low = ps[row, 2 * pair * BLK : (2 * pair + 2) * BLK, begin:end]
            d_probs = nt(both, values)
            d_scores = (probs_low.astype(F32) * ((d_probs - inner) * scale)).astype(BF16)
            got = nn(d_scores, keys)
            query_part = query_part + got[:BLK] * head_f32[2 * pair] + got[BLK:] * head_f32[2 * pair + 1]
            key_parts.append(nn(block_diagonal(query_t, pair), d_scores).astype(BF16))
            value_parts.append(nn(block_diagonal(grad_t, pair), probs_low).astype(BF16))
        d_keys_t = jnp.concatenate(key_parts, 0)
        d_values_t = jnp.concatenate(value_parts, 0)
        return d_keys_t, d_values_t, nn(wk_ref[...], d_keys_t) + nn(wv_ref[...], d_values_t), query_part

    def keep_far(row, parts, begin, tiles):
        d_keys_t, d_values_t, d_rows_t = parts
        columns = slice(begin - EARLY, begin - EARLY + LATE - EARLY)
        far_keys_t[row, :, columns] = d_keys_t
        far_values_t[row, :, columns] = d_values_t
        for pair in range((TILES - NEAR) // 2):
            piece = d_rows_t[:, pair * BLK : (pair + 1) * BLK].T.astype(BF16)
            for side in range(2):
                tiles[row * (TILES - NEAR) + 2 * pair + side] = piece[side * 2 * SPAN : (side + 1) * 2 * SPAN]

    def backward_early(row, carry):
        *parts, query_part = backward(row, EARLY, LATE)
        keep_far(row, parts, EARLY, far_early)
        d_query[rows_at(row, BLK), :] = query_part
        return carry

    def backward_late(row, carry):
        *parts, query_part = backward(row, LATE, KEYS)
        keep_far(row, parts, LATE, far_late)
        d_query[rows_at(row, BLK), :] += query_part
        return carry

    def backward_near(row, carry):
        d_keys_t, d_values_t, d_rows_t, query_part = backward(row, 0, NEAR * BLK)
        near_keys_t[row] = d_keys_t
        near_values_t[row] = d_values_t
        d_query[rows_at(row, BLK), :] += query_part
        for tile in range(NEAR):
            piece = d_rows_t[:, tile * BLK : (tile + 1) * BLK].T
            near_tiles[row * NEAR + tile] = piece.astype(BF16)
        return carry

    def key_grads(row, carry):
        near_rows = fs[row, : NEAR * BLK]
        far_rows = fs[row, NEAR * BLK :]
        pair_acc[0:D, :] += nn(near_keys_t[row], near_rows) + nn(far_keys_t[row], far_rows)
        pair_acc[D : 2 * D, :] += nn(near_values_t[row], near_rows) + nn(far_values_t[row], far_rows)
        return carry

    def stage_early(half):
        def body(peer, carry):
            along, across = ((peer // 8, four(peer // 2)), (four(peer // 2), peer // 8))[half]
            for slot in range(2):
                tile = tile_ref[0, 2 * peer + slot]
                planes[half][across * 2 + two(peer), along, slot] = far_early[tile, half * SPAN : (half + 1) * SPAN]
            return carry

        lax.fori_loop(0, N_DOM, body, 0)

    def stage_late(peer, carry):
        turned = four(peer // 2) * 8 + (peer // 8) * 2 + two(peer)
        for slot in range(2):
            tile = tile_ref[0, 2 * peer + slot]
            stage_a[0, peer, slot] = far_late[tile, 0:SPAN]
            stage_b[0, turned, slot] = far_late[tile, SPAN : 2 * SPAN]
        return carry

    def send_early(half):
        copies = []
        for step in range(4):
            for flip in range(2):
                target = four(axis[1 - half] + step)
                side = two(core + flip)
                if step == 0 and flip == 0:
                    plane_land[half, 0, 0] = planes[half][target * 2 + side]
                    continue
                copies.append(
                    push(
                        planes[half].at[target * 2 + side], plane_land.at[half, step, flip],
                        plane_sems, (half, step, flip), (dom_at(half, axis[half], target, side), node),
                    )
                )
        return copies

    def sum_early(half):
        finish(early[half])
        for ahead in range(4):
            place_there = four(axis[half] + ahead)
            owner = dom_at(half, place_there, axis[1 - half], core)
            names = []
            for step in range(4):
                for flip in range(2):
                    asker = dom_at(half, axis[half], four(axis[1 - half] + 4 - step), two(core + flip))
                    names += [wanted_ref[asker, 0, 2 * owner + slot] for slot in range(2)]
            chosen[half, ahead] = selection(names)
            for top in range(0, SPAN, 16):
                arrived = plane_land[half, :, :, place_there, :, top : top + 16, :].reshape(256, D)
                total = nn(chosen[half, ahead], arrived).reshape(PART, 16, D)
                if ahead == 0:
                    total = total + near_acc[:, half * SPAN + top : half * SPAN + top + 16, :]
                line_send[half, ahead, :, top : top + 16, :] = total.astype(BF16)
        return [
            push(
                line_send.at[half, :, pl.ds(other * ROWS, ROWS)], line_land.at[half, index],
                line_sems, (half, index), target,
            )
            for index, (other, target) in enumerate(x_line)
        ]

    def turn_early(half):
        finish(lined[half])
        copies = []
        for ahead in range(4):
            total = line_send[half, ahead, pl.ds(node * ROWS, ROWS)].astype(F32)
            for index in range(3):
                total = total + line_land[half, index, ahead].astype(F32)
            if ahead == 0:
                axis_own[half] = total
            else:
                axis_send[half, ahead - 1] = total.astype(BF16)
                there = four(axis[half] + ahead)
                copies.append(
                    push(
                        axis_send.at[half, ahead - 1], axis_land.at[half, ahead - 1],
                        axis_sems, (half, ahead - 1), (dom_at(half, there, axis[1 - half], core), node),
                    )
                )
        return copies

    def end_early(half):
        finish(turned_copies[half])
        for row in range(ROWS):
            total = axis_own[half, row]
            for index in range(3):
                total = total + axis_land[half, index, row].astype(F32)
            top = row * BLK + (2 + half) * SPAN
            base_ref[top : top + SPAN, :] += total

    block_of = lax.broadcasted_iota(jnp.int32, (256, 256), 0) // 16
    same_row = lax.rem(lax.broadcasted_iota(jnp.int32, (256, 256), 0), 16) == lax.rem(
        lax.broadcasted_iota(jnp.int32, (256, 256), 1), 16
    )
    slot_of = lax.broadcasted_iota(jnp.int32, (1, 256), 1) // 16

    def selection(values):
        names = jnp.full((1, 256), -1, jnp.int32)
        for index, value in enumerate(values):
            names = jnp.where(slot_of == index, value, names)
        return jnp.logical_and(names == block_of, same_row).astype(F32).astype(BF16)

    def relay_on(arrivals):
        for half, step, copy in arrivals:
            copy.wait()
            second[half, step] = second_phase(0, half, step, sources, relays, lands, send2, recv2)
            lands[half][0, step, 0, 0] = relays[half][0, step - 1, (y, z)[half] * 2 + core]

    def combine(group):
        for half in range(2):
            finish(second[half, group])
            names = [
                wanted_ref[origin(half, group, step, flip), 0, 2 * dom + slot]
                for step in range(4)
                for flip in range(2)
                for slot in range(2)
            ]
            chosen[half, group] = selection(names)
            for top in range(0, SPAN, 16):
                rows = slice(half * SPAN + top, half * SPAN + top + 16)
                arrived = lands[half][0, group, :, :, :, top : top + 16, :].reshape(256, D)
                acc[:, rows, :] += nn(chosen[half, group], arrived).reshape(PART, 16, D)

    def cross():
        cross_send[...] = acc[...].astype(BF16)
        copies = []
        for step in range(1, N_NODE):
            other = four(node + step)
            copies.append(
                push(
                    cross_send.at[pl.ds(other * ROWS, ROWS)], cross_ref.at[step - 1],
                    cross_sems, (step - 1,), (dom, other),
                )
            )
        return copies

    pack((expand_acc, reduce_acc), grads_0)
    pl.semaphore_wait(barrier, len(peers))
    wide = reduction(
        0, grads_0, sum_0, core_recv_0, core_sum_0, (x_recv_0, spot_recv_0), (x_sum_0, spot_sum_0), x_all_0
    )
    next(wide)
    for tiles in (far_early, far_late):
        tiles[FAR] = jnp.zeros((2 * SPAN, D), BF16)
    lax.fori_loop(0, ROWS, backward_early, 0)
    next(wide)
    early = []
    for half in range(2):
        stage_early(half)
        early.append(send_early(half))
    lax.fori_loop(0, ROWS, backward_late, 0)
    lax.fori_loop(0, N_DOM, stage_late, 0)
    next(wide)
    first = [
        first_step(0, half, step, sources, relays, send1, recv1) for step in range(1, 4) for half in range(2)
    ]
    second = {}
    for half in range(2):
        second[half, 0] = second_phase(0, half, 0, sources, relays, lands, send2, recv2)
        lands[half][0, 0, 0, 0] = sources[half][0, (dom, y * 8 + z * 2 + core)[half]]

    near_tiles[ROWS * NEAR : PART] = jnp.zeros((PART - ROWS * NEAR, BLK, D), BF16)
    lax.fori_loop(0, ROWS, backward_near, 0)
    near_names = []
    for row in range(ROWS):
        near_names += [node * ROWS + row, local_ref[0, row], local_ref[1, row]]
    near_chosen = selection(near_names)
    for top in range(0, BLK, 16):
        total = nn(near_chosen, near_tiles[:, top : top + 16, :].reshape(256, D)).reshape(PART, 16, D)
        if top < 2 * SPAN:
            acc[:, top : top + 16, :] = total
        else:
            near_acc[:, top - 2 * SPAN : top - 2 * SPAN + 16, :] = total
    lined = [sum_early(half) for half in range(2)]
    next(wide)
    pair_acc[...] = jnp.zeros(pair_acc.shape, F32)
    lax.fori_loop(0, ROWS, key_grads, 0)
    d_query_low = d_query[...].astype(BF16)
    query_acc[...] = tn(feat_ref[...], d_query_low)
    pack((query_acc, pair_acc, out_acc), grads_1)
    narrow = reduction(
        1, grads_1, sum_1, core_recv_1, core_sum_1, (spot_recv_1, x_recv_1), (spot_sum_1, x_sum_1), spot_all_1
    )
    next(narrow)
    base_ref[...] += nt(d_query_low, wq_ref[...])
    next(narrow)
    relay_on(first[:3])
    next(narrow)
    next(wide)
    relay_on(first[3:])
    combine(0)
    combine(1)
    next(narrow)
    combine(2)
    combine(3)
    crossing = cross()
    turned_copies = [turn_early(half) for half in range(2)]
    next(narrow)
    next(wide)
    next(narrow)
    next(wide)
    for half in range(2):
        end_early(half)
    for row in range(ROWS):
        base_ref[row * BLK : row * BLK + 2 * SPAN, :] += acc[node * ROWS + row]
    next(narrow)
    finish(crossing)


def finish_kernel(
    factor, result_ref, base_ref, cross_ref, expand_ref, reduce_ref, rest_ref, out_ref, dx_ref, gq, gk, gv, go, ge, gr
):
    out_ref[...] = result_ref[...]
    for row in range(ROWS // 2):
        span = slice(row * BLK, row * BLK + 2 * SPAN)
        total = base_ref[span, :]
        for step in range(N_NODE - 1):
            total = total + cross_ref[step, row].astype(F32)
        dx_ref[span, :] = total.astype(BF16)
        span = slice(row * BLK + 2 * SPAN, (row + 1) * BLK)
        dx_ref[span, :] = base_ref[span, :].astype(BF16)
    for half in range(2):
        span = slice(half * BLK, (half + 1) * BLK)
        gq[:, span] = rest_ref[half].astype(F32) * factor
        gk[span, :] = (rest_ref[2 + half].astype(F32) * factor).T
        gv[span, :] = (rest_ref[4 + half].astype(F32) * factor).T
        go[:, span] = rest_ref[6 + half].astype(F32) * factor
    for part in range(4):
        span = slice(part * BLK, (part + 1) * BLK)
        ge[:, span] = expand_ref[part].astype(F32) * factor
        gr[span, :] = (reduce_ref[part].astype(F32) * factor).T


def vmem(shape, dtype):
    return pltpu.VMEM(shape, dtype)


IN_VMEM = pl.BlockSpec(memory_space=pltpu.VMEM)
IN_SMEM = pl.BlockSpec(memory_space=pltpu.SMEM)
ANYWHERE = pl.BlockSpec(memory_space=pl.ANY)


def on_device(
    features, w_query, w_key, w_value, w_out, w_expand, w_reduce, gain_attn, gain_ffn,
    tile_mask, local_block, remote_slot, remote_block, d_out,
):
    rows = features.shape[0]
    dma = pltpu.SemaphoreType.DMA
    peers = len(OFFSETS)
    land = (CHUNKS, 4, 4, 2, 2, SPAN, D)
    staged = (CHUNKS, N_DOM, 2, SPAN, D)
    relay = (CHUNKS, 3, 8, 2, SPAN, D)
    phase_sems = [dma((CHUNKS, 2, 3)), dma((CHUNKS, 2, 3)), dma((CHUNKS, 2, 4, 4, 2)), dma((CHUNKS, 2, 4, 4, 2))]
    part_0, part_1, part_a, part_b, land_a, land_b, wanted, bias, tile_of = pl.pallas_call(
        exchange_kernel,
        out_shape=(
            jax.ShapeDtypeStruct((PART, SPAN, D), BF16),
            jax.ShapeDtypeStruct((PART, SPAN, D), BF16),
            jax.ShapeDtypeStruct((PART, SPAN, D), BF16),
            jax.ShapeDtypeStruct((PART, SPAN, D), BF16),
            jax.ShapeDtypeStruct(land, BF16),
            jax.ShapeDtypeStruct(land, BF16),
            jax.ShapeDtypeStruct((N_DOM, 1, BLK), jnp.int32),
            jax.ShapeDtypeStruct((rows, KEYS), BF16),
            jax.ShapeDtypeStruct((1, 2 * N_DOM), jnp.int32),
        ),
        in_specs=[IN_VMEM, IN_VMEM, IN_SMEM, IN_VMEM],
        out_specs=(IN_VMEM,) * 4 + (ANYWHERE, ANYWHERE, IN_VMEM, IN_VMEM, IN_SMEM),
        scratch_shapes=[
            vmem((1, BLK), jnp.int32), vmem(staged, BF16), vmem(staged, BF16),
            vmem(relay, BF16), vmem(relay, BF16), pltpu.SMEM((N_DOM, 1, BLK), jnp.int32),
        ]
        + [vmem((PART, SPAN, D), BF16)] * 6
        + [dma((2, N_NODE - 1)), dma((2, N_NODE - 1)), dma((peers,)), dma((peers,))]
        + phase_sems
        + [dma((2, 3)), dma((2, 3)), dma((2, 4, 3)), dma((2, 4, 3)), dma((CHUNKS, 2, 4)), dma],
        compiler_params=pltpu.CompilerParams(
            collective_id=1, has_side_effects=True, vmem_limit_bytes=VMEM_LIMIT
        ),
        name="exchange",
    )(features.reshape(ROWS, BLK, D), remote_block.reshape(1, 2 * N_DOM), remote_slot, jnp.transpose(tile_mask, (1, 0, 2)))

    sum_scratch = []
    for total, lines in zip(SUM_ROWS, ((4, 16), (16, 4))):
        half = total // 2
        sum_scratch += [vmem((half, BLK), BF16), vmem((half, BLK), BF16)]
        for count in lines:
            half = half // count
            sum_scratch += [vmem((count - 1, half, BLK), BF16), vmem((half, BLK), BF16)]
        sum_scratch.append(vmem((total // 2 // lines[0], BLK), BF16))
    result, base, cross, sum_0, sum_1 = pl.pallas_call(
        layer_kernel,
        out_shape=(
            jax.ShapeDtypeStruct((rows, D), BF16),
            jax.ShapeDtypeStruct((rows, D), F32),
            jax.ShapeDtypeStruct((N_NODE - 1, ROWS, 2 * SPAN, D), BF16),
            jax.ShapeDtypeStruct((SUM_ROWS[0], BLK), BF16),
            jax.ShapeDtypeStruct((SUM_ROWS[1], BLK), BF16),
        ),
        in_specs=[IN_SMEM] * 4 + [IN_VMEM] * 17,
        out_specs=(IN_VMEM,) * 5,
        scratch_shapes=[
            vmem((ROWS, KEYS, D), BF16), vmem((ROWS, KEYS, D), BF16), vmem((ROWS, KEYS, D), BF16),
            vmem((rows, D), BF16), vmem((ROWS, HEADS * BLK, KEYS), BF16), vmem((rows, D), F32),
            vmem((rows, D), BF16), vmem((rows, D), F32),
            vmem((ROWS, D, KEYS - NEAR * BLK), BF16), vmem((ROWS, D, KEYS - NEAR * BLK), BF16),
            vmem((ROWS, D, NEAR * BLK), BF16), vmem((ROWS, D, NEAR * BLK), BF16),
            vmem((FAR + 1, 2 * SPAN, D), BF16), vmem((FAR + 1, 2 * SPAN, D), BF16), vmem((PART, BLK, D), BF16),
            vmem((2 * D, D), F32), vmem((D, D), F32), vmem((D, 4 * D), F32), vmem((D, 4 * D), F32), vmem((D, D), F32),
            vmem((SUM_ROWS[0], BLK), BF16), vmem((SUM_ROWS[1], BLK), BF16),
            vmem((1,) + staged[1:], BF16), vmem((1,) + staged[1:], BF16),
            vmem((1,) + relay[1:], BF16), vmem((1,) + relay[1:], BF16),
            vmem((1,) + land[1:], BF16), vmem((1,) + land[1:], BF16),
            vmem((PART, 2 * SPAN, D), F32), vmem((PART, 2 * SPAN, D), F32),
            vmem((2, 4, 256, 256), BF16), vmem((PART, 2 * SPAN, D), BF16),
            vmem((8, 4, 2, SPAN, D), BF16), vmem((8, 4, 2, SPAN, D), BF16), vmem((2, 4, 2, 4, 2, SPAN, D), BF16),
            vmem((2, 4, PART, SPAN, D), BF16), vmem((2, 3, 4, ROWS, SPAN, D), BF16),
            vmem((2, 3, ROWS, SPAN, D), BF16), vmem((2, 3, ROWS, SPAN, D), BF16), vmem((2, ROWS, SPAN, D), F32),
        ]
        + sum_scratch
        + [dma((1, 2, 3)), dma((1, 2, 3)), dma((1, 2, 4, 4, 2)), dma((1, 2, 4, 4, 2))]
        + [dma((2, 2, 4, 2)), dma((2, 2, 3)), dma((2, 2, 3)), dma((2, 3)), dma((2, 2, 2)), dma((2, 2, 2, 3)), dma((2, 2, 2, 15))],
        compiler_params=pltpu.CompilerParams(
            collective_id=2, has_side_effects=True, vmem_limit_bytes=VMEM_LIMIT
        ),
        name="layer",
    )(
        local_block.T, remote_slot, tile_of, wanted, features, part_0, part_1, part_a, part_b, land_a, land_b, bias, d_out,
        w_query, w_key, w_value, w_out, w_expand, w_reduce, gain_attn.reshape(1, D), gain_ffn.reshape(1, D),
    )

    factor = 1.0 / math.sqrt(rows * N_DOM * N_NODE)
    pieces = sum_0.reshape(16, D, BLK)
    return pl.pallas_call(
        functools.partial(finish_kernel, factor),
        out_shape=(
            jax.ShapeDtypeStruct((rows, D), BF16),
            jax.ShapeDtypeStruct((rows, D), BF16),
            jax.ShapeDtypeStruct((D, D), F32),
            jax.ShapeDtypeStruct((D, D), F32),
            jax.ShapeDtypeStruct((D, D), F32),
            jax.ShapeDtypeStruct((D, D), F32),
            jax.ShapeDtypeStruct((D, 4 * D), F32),
            jax.ShapeDtypeStruct((4 * D, D), F32),
        ),
        grid=(2,),
        in_specs=[
            pl.BlockSpec((rows // 2, D), lambda i: (i, 0)),
            pl.BlockSpec((rows // 2, D), lambda i: (i, 0)),
            pl.BlockSpec((N_NODE - 1, ROWS // 2, 2 * SPAN, D), lambda i: (0, i, 0, 0)),
            pl.BlockSpec((4, D, BLK), lambda i: (i, 0, 0)),
            pl.BlockSpec((4, D, BLK), lambda i: (2 + i, 0, 0)),
            pl.BlockSpec((8, BLK, BLK), lambda i: (0, i, 0)),
        ],
        out_specs=(
            pl.BlockSpec((rows // 2, D), lambda i: (i, 0)),
            pl.BlockSpec((rows // 2, D), lambda i: (i, 0)),
            pl.BlockSpec((BLK, D), lambda i: (i, 0)),
            pl.BlockSpec((D, BLK), lambda i: (0, i)),
            pl.BlockSpec((D, BLK), lambda i: (0, i)),
            pl.BlockSpec((BLK, D), lambda i: (i, 0)),
            pl.BlockSpec((D, 2 * D), lambda i: (0, i)),
            pl.BlockSpec((2 * D, D), lambda i: (i, 0)),
        ),
        compiler_params=pltpu.CompilerParams(vmem_limit_bytes=VMEM_LIMIT),
        name="finish",
    )(result, base, cross, pieces, pieces, sum_1.reshape(8, D, BLK))


def solution(mesh):
    split = P(("dom", "node"), None)
    placed = (
        (split,) + (P(),) * 8 + (P(("dom", "node"), None, None), split, split, P("dom", "node", None), split)
    )
    return jax.shard_map(
        on_device, mesh=mesh, in_specs=placed, out_specs=(split, split) + (P(),) * 6, check_vma=False
    )
```
